128 devices in a mesh: seq: 128 (over z, x, y, core).
Axes of the slice: x: 4, y: 4, z: 4, core: 2. Of those that a mesh axis runs over, the one named last changes fastest.
Arguments:
- block_in: bfloat16 [2, 16384, 512], P(None, 'seq'), may hold values from -6 to 6
- out_grad: bfloat16 [2, 16384, 512], P(None, 'seq'), may hold values from -6 to 6
- lengths: int32 [2, 16], replicated, may hold values from 0 to 8192, as said below
- ln_gain: float32 [512], replicated, may hold values from 0.25 to 1.75
- ln_bias: float32 [512], replicated, may hold values from -3 to 3
- b_proj: bfloat16 [512, 512], replicated, may hold values from -0.25 to 0.25
- c_proj: bfloat16 [512, 512], replicated, may hold values from -0.25 to 0.25
- glu_weight: bfloat16 [512, 1024], replicated, may hold values from -0.25 to 0.25
- skip_gain: float32 [512], replicated, may hold values from -4 to 4
- log_rate: float32 [256], replicated
- angle: float32 [256], replicated, may hold values from -3.140625 to 3.140625
Outputs:
- block_out: bfloat16 [2, 16384, 512], P(None, 'seq')
- in_grad: bfloat16 [2, 16384, 512], P(None, 'seq')
- gain_grad: float32 [512], P('seq')
- bias_grad: float32 [512], P('seq')
- b_grad: float32 [512, 512], P('seq')
- c_grad: float32 [512, 512], P('seq')
- glu_grad: float32 [512, 1024], P('seq')
- skip_grad: float32 [512], P('seq')
- rate_grad: float32 [256], P('seq')
- angle_grad: float32 [256], P('seq')
The draws below stay inside these ranges and needn't reach their ends.
Inputs may be any that keep to these rules, and one draw needn't show every extreme that they name: Each row lists one micro-batch's image sequence lengths in token order, each 1024 or 8192, followed by zeros, summing to 16384.
All inputs are finite; a program needn't handle non-finite values.
Results may differ from the reference program's by a relative error of at most 0.035.
Values may be sent and summed in bfloat16 or wider, within the bound.
No kernel may reach another device: no remote copies, remote signals or barrier semaphores. Data moves between devices by JAX's collectives and lax.ppermute only.
A program may use at most 128 MiB of HBM per device.

```python
import math
import jax
import jax.numpy as jnp
from jax import lax

D = 512
STATE = 256
MICRO = 2
SEQ_MIN = 1024
TOK_MB = 16384
LONG = 8192


def draw_lengths(key, part):
    key = jax.random.fold_in(key, 7)
    units = TOK_MB // SEQ_MIN
    long_units = LONG // SEQ_MIN
    region = units - long_units
    choices_count = region - long_units + 2
    which_key, offset_key = jax.random.split(key)
    which = jax.random.randint(which_key, (), 0, 2)
    batch_ids = jnp.arange(MICRO, dtype=jnp.int32)[:, None]
    leading = batch_ids % 2 == which
    first_long = jnp.where(leading, 0, region)
    region_base = jnp.where(leading, long_units, 0)
    offset = jax.random.randint(offset_key, (MICRO, 1), 0, choices_count)
    has_second = offset < choices_count - 1
    second_long = jnp.where(has_second, region_base + offset, -4 * units)
    slots = jnp.arange(units, dtype=jnp.int32)[None, :]
    inside_first = jnp.logical_and(slots > first_long, slots < first_long + long_units)
    inside_second = jnp.logical_and(slots > second_long, slots < second_long + long_units)
    marks = jnp.logical_not(jnp.logical_or(inside_first, inside_second)).astype(jnp.int32)
    owner = jnp.cumsum(marks, axis=1) - 1
    counts = jnp.sum((owner[:, :, None] == slots[:, None, :]).astype(jnp.int32), axis=1)
    return (counts * SEQ_MIN).astype(jnp.int32)


def draw_log_rate(key, part):
    key = jax.random.fold_in(key, 11)
    lower = math.log(1.0 / LONG)
    upper = math.log(1.0 / 30.0)
    return jax.random.uniform(key, (STATE,), jnp.float32, lower, upper)


def shard_levels(key, dims, shards, least, top_value):
    level = 1.0
    for axis_at, parts in shards:
        draws = jax.random.uniform(jax.random.fold_in(jax.random.fold_in(key, 6), axis_at), (parts,), jnp.float32, least / len(shards), top_value / len(shards))
        level = level * jnp.repeat(jnp.exp(draws), dims[axis_at] // parts).reshape((-1,) + (1,) * (len(dims) - 1 - axis_at))
    return level


def scatter_about(rng, extent, spread, bound, pieces=(), kind=jnp.bfloat16):
    array = jax.random.normal(rng, extent, jnp.float32) * spread
    if len(pieces) > 0:
        array = shard_levels(rng, extent, pieces, -0.22, 0.18) * array
    return jnp.clip(array, min=-bound, max=bound).astype(kind)


def setup_inputs(seed: int = 0) -> dict:
    splits = jax.random.split(jax.random.key(seed), 12)
    block_in = scatter_about(splits[0], (MICRO, TOK_MB, D), 1.0, 6.0, ((1, 128),))
    out_grad = scatter_about(splits[1], (MICRO, TOK_MB, D), 1.0, 6.0, ((1, 128),))
    lengths = draw_lengths(jax.random.fold_in(splits[11], 71), 0)
    ln_gain = jnp.clip(1.0 + 0.15 * jax.random.normal(splits[3], (D,), jnp.float32), 0.25, 1.75)
    ln_bias = scatter_about(splits[4], (D,), 0.5, 3.0, (), jnp.float32)
    b_proj = scatter_about(splits[5], (D, 2 * STATE), D ** -0.5, 0.25)
    c_proj = scatter_about(splits[6], (2 * STATE, D), (2 * STATE) ** -0.5, 0.25)
    glu_weight = scatter_about(splits[7], (D, 2 * D), D ** -0.5, 0.25)
    skip_gain = scatter_about(splits[8], (D,), 1.0, 4.0, (), jnp.float32)
    log_rate = draw_log_rate(jax.random.fold_in(splits[11], 71), 0)
    angle = jnp.clip(jax.random.uniform(splits[10], (STATE,), jnp.float32, -3.140625, 3.140625), -3.140625, 3.140625)
    return {"block_in": block_in, "out_grad": out_grad, "lengths": lengths, "ln_gain": ln_gain, "ln_bias": ln_bias, "b_proj": b_proj, "c_proj": c_proj, "glu_weight": glu_weight, "skip_gain": skip_gain, "log_rate": log_rate, "angle": angle}


@jax.custom_vjp
def low(v):
    return lax.optimization_barrier(v.astype(jnp.bfloat16)).astype(jnp.float32)

@jax.custom_vjp
def low_back(v):
    return v

def low_keep(v):
    return (low(v), None)

def low_pass(kept, grad):
    return (grad,)

def back_keep(v):
    return (v, None)

def back_low(kept, grad):
    return (low(grad),)
low.defvjp(low_keep, low_pass)
low_back.defvjp(back_keep, back_low)

def normalize(rows, gain, bias):
    mean = lax.optimization_barrier(jnp.mean(rows, axis=-1, keepdims=True))
    centered = rows - mean
    variance = lax.optimization_barrier(jnp.mean(centered * centered, axis=-1, keepdims=True))
    return centered * lax.rsqrt(variance + 1e-05) * gain + bias

def complex_step(earlier, later):
    return (later[0] * earlier[0] - later[1] * earlier[1], later[0] * earlier[1] + later[1] * earlier[0], later[0] * earlier[2] - later[1] * earlier[3] + later[2], later[0] * earlier[3] + later[1] * earlier[2] + later[3])

def decay_params(log_rate, angle):
    radius = jnp.exp(-jnp.exp(log_rate))
    scale = jnp.sqrt(-jnp.expm1(-2.0 * jnp.exp(log_rate)))
    return (radius * jnp.cos(angle), radius * jnp.sin(angle), scale)

def glu_gate(gated):
    half = gated.shape[-1] // 2
    return gated[..., :half] * jax.nn.sigmoid(gated[..., half:])

def start_flags(positions, lens):
    offsets = jnp.cumsum(lens) - lens
    return jnp.any(positions[:, None] == offsets[None, :], axis=1)

def forward(rows, starts, gain, bias, b_weight, c_weight, glu_w, skip, log_rate, angle):
    highest = lax.Precision.HIGHEST
    normed = low(normalize(rows, gain, bias))
    proj = low_back(low(jnp.dot(normed, b_weight, precision=highest)))
    lam_re, lam_im, scale = decay_params(log_rate, angle)
    channels = proj.shape[1] // 2
    pairs = proj.reshape(-1, channels, 2)
    keep = jnp.logical_not(starts)[:, None]
    decay_re = jnp.where(keep, lam_re[None, :], 0.0)
    decay_im = jnp.where(keep, lam_im[None, :], 0.0)
    prefix = lax.associative_scan(complex_step, (decay_re, decay_im, scale * pairs[:, :, 0], scale * pairs[:, :, 1]), axis=0)
    hidden = jnp.stack([prefix[2], prefix[3]], axis=2).reshape(-1, 2 * channels)
    hidden = low_back(low(hidden))
    mixed = low_back(jnp.dot(hidden, c_weight, precision=highest) + skip * normed)
    active = low(jax.nn.gelu(mixed))
    gated = low_back(jnp.dot(active, glu_w, precision=highest))
    return rows + glu_gate(gated)

def reference(block_in, out_grad, lengths, ln_gain, ln_bias, b_proj, c_proj, glu_weight, skip_gain, log_rate, angle):
    micro_count, length, width = block_in.shape
    positions = jnp.arange(length, dtype=jnp.int32)
    weights = (ln_gain, ln_bias, b_proj.astype(jnp.float32), c_proj.astype(jnp.float32), glu_weight.astype(jnp.float32), skip_gain, log_rate, angle)
    outputs = []
    input_grads = []
    totals = None
    for index in range(micro_count):
        starts = start_flags(positions, lengths[index])
        rows = block_in[index].astype(jnp.float32)

        def wrapped(rows_in, gain, bias, b_weight, c_weight, glu_w, skip, rates, angles):
            return forward(rows_in, starts, gain, bias, b_weight, c_weight, glu_w, skip, rates, angles)
        result, back = jax.vjp(wrapped, rows, *weights)
        grads = back(out_grad[index].astype(jnp.float32))
        outputs.append(result.astype(jnp.bfloat16))
        input_grads.append(grads[0].astype(jnp.bfloat16))
        if totals is None:
            totals = list(grads[1:])
        else:
            totals = [total + piece for total, piece in zip(totals, grads[1:])]
    return (jnp.stack(outputs), jnp.stack(input_grads), totals[0], totals[1], totals[2], totals[3], totals[4], totals[5], totals[6], totals[7])
```

```python
import functools

import jax
import jax.numpy as jnp
import numpy as np
from jax import lax
from jax.experimental import pallas as pl
from jax.experimental.pallas import tpu as pltpu
from jax.sharding import PartitionSpec as P

F32 = jnp.float32
BF16 = jnp.bfloat16
VMEM_LIMIT = 56 * 1024 * 1024
TOK = 128
GROUPS = TOK // 8
MICRO = 2
HALVES = 2
N = 128


def deal():
    out = np.zeros((256, 256), np.float32)
    for n in range(128):
        out[2 * n, n] = 1.0
        out[2 * n + 1, 128 + n] = 1.0
    return out


def dot(a, b):
    return jnp.dot(a, b, preferred_element_type=F32)


def dot_tn(a, b):
    return lax.dot_general(a, b, (((0,), (0,)), ((), ())), preferred_element_type=F32)


def dot_nt(a, b):
    return lax.dot_general(a, b, (((1,), (1,)), ((), ())), preferred_element_type=F32)


def cmul(a, b):
    return (a[0] * b[0] - a[1] * b[1], a[0] * b[1] + a[1] * b[0])


def conj(a):
    return (a[0], -a[1])


def rows_iota(shape=(8, 128)):
    return lax.broadcasted_iota(jnp.int32, shape, len(shape) - 2)


def params(log_rate, angle):
    u = jnp.exp(log_rate)
    r = jnp.exp(-u)
    lam = (r * jnp.cos(angle), r * jnp.sin(angle))
    w = 2.0 * u
    small = jnp.minimum(w, 0.5)
    poly = 1.0 - small * (1.0 / 11.0)
    for k in range(10, 1, -1):
        poly = 1.0 - small * (1.0 / k) * poly
    gap = jnp.where(w < 0.5, small * poly, 1.0 - jnp.exp(-w))
    scale = jnp.sqrt(gap)
    return u, r, lam, scale


def powers(lam, count):
    out = [lam]
    for _ in range(count):
        out.append(cmul(out[-1], out[-1]))
    return out


def lam_tiles(log_rate_ref, angle_ref):
    out = []
    for half in range(HALVES):
        lr = jnp.broadcast_to(log_rate_ref[half : half + 1, :], (8, 128))
        an = jnp.broadcast_to(angle_ref[half : half + 1, :], (8, 128))
        out.append(params(lr, an))
    return out


def scan_tables(pows, reverse):
    row = rows_iota()
    pos = (7 - row) if reverse else row
    levels = []
    for s, p in ((1, pows[0]), (2, pows[1]), (4, pows[2])):
        keep = pos >= s
        levels.append((s, (jnp.where(keep, p[0], 0.0), jnp.where(keep, p[1], 0.0))))
    e = pos + 1
    table = (jnp.ones((8, 128), F32), jnp.zeros((8, 128), F32))
    for bit in range(4):
        on = (lax.shift_right_logical(e, bit) & 1) == 1
        table = cmul(table, (jnp.where(on, pows[bit][0], 1.0), jnp.where(on, pows[bit][1], 0.0)))
    return levels, table


def group_scan(x, levels, reverse):
    xr, xi = x
    for s, (mr, mi) in levels:
        shift = 8 - s if reverse else s
        rr = pltpu.roll(xr, shift, 1)
        ri = pltpu.roll(xi, shift, 1)
        xr, xi = xr + (mr * rr - mi * ri), xi + (mr * ri + mi * rr)
    return xr, xi


def tile_rows(parts):
    rows = []
    for comp in range(2):
        for micro in range(MICRO):
            for half in range(HALVES):
                rows.append(parts[(micro, half)][comp])
    return jnp.concatenate(rows, axis=0)


def tile_lam(p):
    row = rows_iota()
    odd = (row & 1) == 1
    re = jnp.where(odd, p[1][0], p[0][0])
    im = jnp.where(odd, p[1][1], p[0][1])
    return re, jnp.where(row < 4, -im, im)


def tile_mul(c, coef):
    return c * coef[0] + pltpu.roll(c, 4, 0) * coef[1]


def gather_carry(ends_ref, me, step, dmax, coef, coef8):
    chains = []
    for chain in range(8):
        acc = jnp.zeros((8, 128), F32)
        for i in range(7, -1, -1):
            d = chain * 8 + i
            at = jnp.clip(me + step * (1 + d), 0, N - 1)
            e = ends_ref[at].astype(F32)
            e = jnp.where(d <= dmax, e, 0.0)
            acc = e if i == 7 else tile_mul(acc, coef) + e
        chains.append(acc)
    total = chains[7]
    for chain in range(6, -1, -1):
        total = tile_mul(total, coef8) + chains[chain]
    return total


def segment(lengths_ref, micro, base):
    first = jnp.int32(0)
    last = jnp.int32(N * TOK)
    at = jnp.int32(0)
    for slot in range(16):
        first = jnp.where(at <= base, jnp.maximum(first, at), first)
        last = jnp.where(at > base, jnp.minimum(last, at), last)
        at = at + lengths_ref[micro, slot]
    return first, last


def distance_tiles(lengths_ref, me):
    base = me * TOK
    row = rows_iota()
    second = (row & 2) == 2
    ahead, behind = [], []
    for micro in range(MICRO):
        first, last = segment(lengths_ref, micro, base)
        ahead.append((base - first) // TOK - 1)
        behind.append((last - base) // TOK - 2)
    pick = lambda two: jnp.where(second, two[1], two[0])
    return pick(ahead), pick(behind)


def groups_of(value, micro_groups=MICRO * GROUPS):
    return value.reshape(micro_groups, 8, 128)


def split_channels(value):
    out = []
    for half in range(HALVES):
        c = 256 * half
        out.append((groups_of(value[:, c : c + 128]), groups_of(value[:, c + 128 : c + 256])))
    return out


def join_channels(halves):
    cols = []
    for re, im in halves:
        cols.append(re.reshape(MICRO * TOK, 128))
        cols.append(im.reshape(MICRO * TOK, 128))
    return jnp.concatenate(cols, axis=1)


def permute(value_bf, matrix):
    return jnp.concatenate([dot(value_bf[:, :256], matrix), dot(value_bf[:, 256:], matrix)], axis=1)


def layer_norm(x):
    mean = jnp.mean(x, axis=1, keepdims=True)
    centered = x - mean
    var = jnp.mean(centered * centered, axis=1, keepdims=True)
    rstd = lax.rsqrt(var + 1e-05)
    return centered * rstd, rstd


def chain_from(x, micro, step8, init, reverse):
    before = {}
    v = init
    order = range(GROUPS - 1, -1, -1) if reverse else range(GROUPS)
    for g in order:
        before[g] = v
        xr, xi = x[0][micro * GROUPS + g], x[1][micro * GROUPS + g]
        if v is None:
            v = (xr, xi)
        else:
            m = cmul(v, step8)
            v = (xr + m[0], xi + m[1])
    return before, v


def edge_bcast(pair, edge):
    return tuple(jnp.broadcast_to(p[edge : edge + 1, :], (8, 128)) for p in pair)


def kernel_first(x_ref, gain_ref, bias_ref, b_ref, deal_ref, log_rate_ref, angle_ref, normed_ref, pairs_ref, local_ref, ends_ref):
    x = x_ref[...].astype(F32)
    xhat, _ = layer_norm(x)
    normed = (xhat * gain_ref[...] + bias_ref[...]).astype(BF16)
    normed_ref[...] = normed
    proj = dot(normed, b_ref[...]).astype(BF16)
    pairs = permute(proj, deal_ref[...])
    pairs_ref[...] = pairs.astype(BF16)
    halves = split_channels(pairs)
    lams = lam_tiles(log_rate_ref, angle_ref)
    parts, scanned = {}, []
    for half in range(HALVES):
        _, _, lam, scale = lams[half]
        pows = powers(lam, 3)
        levels, _ = scan_tables(pows, False)
        re, im = halves[half]
        x8 = group_scan((re * scale, im * scale), levels, False)
        scanned.append(x8)
        for micro in range(MICRO):
            _, v = chain_from(x8, micro, pows[3], None, False)
            parts[(micro, half)] = (v[0][7:8, :], v[1][7:8, :])
    local_ref[...] = join_channels(scanned)
    ends_ref[...] = jnp.broadcast_to(tile_rows(parts).astype(BF16)[None], (N, 8, 128))


def tile_row(tile, comp, micro, half):
    at = comp * 4 + micro * 2 + half
    return jnp.broadcast_to(tile[at : at + 1, :], (8, 128))


def carry_pows(lams):
    long_pows = [powers(lams[half][2], 10) for half in range(HALVES)]
    return long_pows


def kernel_middle(
    lengths_ref, ends_ref, local_ref, normed_ref, x_ref, go_ref, c_ref, glu_ref, skip_ref, deal_ref, deal_back_ref, log_rate_ref, angle_ref,
    out_ref, act_ref, dgated_ref, hidden_ref, dy_ref, back_ref, prior_ref, firsts_ref,
):
    me = lax.axis_index("seq")
    ahead, _ = distance_tiles(lengths_ref, me)
    lams = lam_tiles(log_rate_ref, angle_ref)
    pows = carry_pows(lams)
    coef = tile_lam([p[7] for p in pows])
    coef8 = tile_lam([p[10] for p in pows])
    carry = gather_carry(ends_ref, me, -1, ahead, coef, coef8)
    local = split_channels(local_ref[...])
    row = rows_iota((MICRO * GROUPS, 8, 128))
    states, priors = [], []
    for half in range(HALVES):
        _, table = scan_tables(pows[half], False)
        x8 = local[half]
        before_r, before_i = [], []
        for micro in range(MICRO):
            init = (tile_row(carry, 0, micro, half), tile_row(carry, 1, micro, half))
            before, _ = chain_from(x8, micro, pows[half][3], init, False)
            for g in range(GROUPS):
                edge = edge_bcast(before[g], 7)
                before_r.append(edge[0])
                before_i.append(edge[1])
        br, bi = jnp.stack(before_r), jnp.stack(before_i)
        hr = x8[0] + (table[0] * br - table[1] * bi)
        hi = x8[1] + (table[0] * bi + table[1] * br)
        states.append((hr, hi))
        priors.append((jnp.where(row == 0, br, pltpu.roll(hr, 1, 1)), jnp.where(row == 0, bi, pltpu.roll(hi, 1, 1))))
    prior_ref[...] = join_channels(priors)
    hidden = permute(join_channels(states).astype(BF16), deal_back_ref[...]).astype(BF16)
    hidden_ref[...] = hidden
    y = dot(hidden, c_ref[...]) + skip_ref[...] * normed_ref[...].astype(F32)
    k0, k1 = 0.7978845608028654, 0.044715
    yy = y * y
    t = jnp.tanh(k0 * (y + k1 * (yy * y)))
    act = (0.5 * y * (1.0 + t)).astype(BF16)
    act_ref[...] = act
    slope = 0.5 * (1.0 + t) + 0.5 * y * (1.0 - t * t) * (k0 * (1.0 + 3.0 * k1 * yy))
    gated = dot(act, glu_ref[...])
    value, gate = gated[:, :512], gated[:, 512:]
    sig = jax.nn.sigmoid(gate)
    go = go_ref[...].astype(F32)
    out_ref[...] = (x_ref[...].astype(F32) + value * sig).astype(BF16)
    gs = go * sig
    dgated = jnp.concatenate([gs, gs * value * (1.0 - sig)], axis=1).astype(BF16)
    dgated_ref[...] = dgated
    dy = (dot_nt(dgated, glu_ref[...]) * slope).astype(BF16)
    dy_ref[...] = dy
    dhidden = dot_nt(dy, c_ref[...]).astype(BF16)
    q = split_channels(permute(dhidden, deal_ref[...]))
    parts, scanned = {}, []
    for half in range(HALVES):
        cp = [conj(p) for p in pows[half][:4]]
        levels, _ = scan_tables(cp, True)
        x8 = group_scan(q[half], levels, True)
        scanned.append(x8)
        for micro in range(MICRO):
            _, v = chain_from(x8, micro, cp[3], None, True)
            parts[(micro, half)] = (v[0][0:1, :], v[1][0:1, :])
    back_ref[...] = join_channels(scanned)
    firsts_ref[...] = jnp.broadcast_to(tile_rows(parts).astype(BF16)[None], (N, 8, 128))


def chunk_rows(left, right):
    w = left.shape[1]
    a = left.reshape(64, 8, w)
    b = right.reshape(64, 8, w)
    low = rows_iota((64, 8, w)) < 4
    even = jnp.where(low, a, pltpu.roll(b, 4, 1))
    odd = jnp.where(low, pltpu.roll(a, 4, 1), b)
    return jnp.stack([even, odd], axis=1).reshape(128, 8, w)


def kernel_weights(act_ref, dgated_ref, hidden_ref, dy_ref, out_ref):
    glu = dot_tn(act_ref[...], dgated_ref[...])
    c = dot_tn(hidden_ref[...], dy_ref[...])
    out_ref[...] = chunk_rows(glu[:, :768], jnp.concatenate([glu[:, 768:], c], axis=1)).astype(BF16)


def small_chunks(vectors, channels):
    dest = lax.broadcasted_iota(jnp.int32, (N, 512), 0)
    feature = lax.broadcasted_iota(jnp.int32, (N, 512), 1)
    lane = lax.broadcasted_iota(jnp.int32, (512, 128), 1)
    row = lax.broadcasted_iota(jnp.int32, (512, 128), 0)
    by_four = ((feature // 4) == dest, row % 4)
    by_two = (((feature % 256) // 2) == dest, row % 2 + 2 * (row // 256))
    total = jnp.zeros((N, 128), F32)
    for v, vec in enumerate(vectors + [channels]):
        mine, inner = by_two if v == len(vectors) else by_four
        high = vec.astype(BF16).astype(F32)
        rest = vec - high
        for part, base in ((high, 4 * v), (rest, 64 + 4 * v)):
            spread = jnp.where(mine, part, 0.0).astype(BF16)
            place = jnp.where(lane == base + inner, 1.0, 0.0).astype(BF16)
            total = total + dot(spread, place)
    return total


def kernel_last(
    lengths_ref, firsts_ref, back_ref, prior_ref, pairs_ref, normed_ref, x_ref, go_ref, dy_ref, b_ref, gain_ref, skip_ref, deal_back_ref,
    log_rate_ref, angle_ref, in_grad_ref, out_ref,
):
    me = lax.axis_index("seq")
    _, behind = distance_tiles(lengths_ref, me)
    lams = lam_tiles(log_rate_ref, angle_ref)
    pows = [[conj(p) for p in per_half] for per_half in carry_pows(lams)]
    coef = tile_lam([p[7] for p in pows])
    coef8 = tile_lam([p[10] for p in pows])
    carry = gather_carry(firsts_ref, me, 1, behind, coef, coef8)
    local = split_channels(back_ref[...])
    prior = split_channels(prior_ref[...])
    pairs = split_channels(pairs_ref[...].astype(F32))
    projs, rates, angles = [], [], []
    for half in range(HALVES):
        u, r, lam, scale = lams[half]
        _, table = scan_tables(pows[half], True)
        x8 = local[half]
        after_r, after_i = [], []
        for micro in range(MICRO):
            init = (tile_row(carry, 0, micro, half), tile_row(carry, 1, micro, half))
            after, _ = chain_from(x8, micro, pows[half][3], init, True)
            for g in range(GROUPS):
                edge = edge_bcast(after[g], 0)
                after_r.append(edge[0])
                after_i.append(edge[1])
        ar, ai = jnp.stack(after_r), jnp.stack(after_i)
        gr = x8[0] + (table[0] * ar - table[1] * ai)
        gi = x8[1] + (table[0] * ai + table[1] * ar)
        pr, pi = prior[half]
        total = lambda v: jnp.sum(jnp.sum(v, axis=0), axis=0, keepdims=True)
        d_re = total(gr * pr + gi * pi)
        d_im = total(gi * pr - gr * pi)
        d_scale = total(gr * pairs[half][0] + gi * pairs[half][1])
        one = lambda t: t[0:1, :]
        lr, li = one(lam[0]), one(lam[1])
        rates.append(one(u) * (one(r) * one(r) * d_scale / one(scale) - (lr * d_re + li * d_im)))
        angles.append(lr * d_im - li * d_re)
        projs.append((gr * scale, gi * scale))
    dproj = permute(join_channels(projs).astype(BF16), deal_back_ref[...]).astype(BF16)
    normed = normed_ref[...]
    b_grad = dot_tn(normed, dproj)
    dy = dy_ref[...].astype(F32)
    dnormed = dot_nt(dproj, b_ref[...]) + skip_ref[...] * dy
    go = go_ref[...].astype(F32)
    xhat, rstd = layer_norm(x_ref[...].astype(F32))
    col = lambda v: jnp.sum(v, axis=0, keepdims=True)
    gain_grad = col(dnormed * xhat)
    bias_grad = col(dnormed)
    skip_grad = col(dy * normed.astype(F32))
    smalls = small_chunks([gain_grad, bias_grad, skip_grad], jnp.concatenate(rates + angles, axis=1))
    chunks = chunk_rows(b_grad[:, :256], b_grad[:, 256:])
    out_ref[:, :, 0:256] = chunks.astype(BF16)
    out_ref[:, :, 256:384] = jnp.broadcast_to(smalls[:, None, :], (N, 8, 128)).astype(BF16)
    dx = dnormed * gain_ref[...]
    m1 = jnp.mean(dx, axis=1, keepdims=True)
    m2 = jnp.mean(dx * xhat, axis=1, keepdims=True)
    in_grad_ref[...] = (go + rstd * (dx - m1 - xhat * m2)).astype(BF16)


def kernel_sum(wide_ref, narrow_ref, b_ref, c_ref, glu_ref, small_ref):
    wide = jnp.sum(wide_ref[...].astype(F32), axis=0)
    glu_ref[:, 0:768] = wide[0:4, :]
    glu_ref[:, 768:1024] = wide[4:8, 0:256]
    c_ref[...] = wide[4:8, 256:768]
    narrow = jnp.sum(narrow_ref[...].astype(F32), axis=0)
    b_ref[:, 0:256] = narrow[0:4, 0:256]
    b_ref[:, 256:512] = narrow[4:8, 0:256]
    small = narrow[:, 256:384]
    small_ref[...] = small + pltpu.roll(small, 64, 1)


def call(kernel, outs, args, smem=(), flops=0, nbytes=0):
    space = lambda i: pltpu.SMEM if i in smem else pltpu.VMEM
    return pl.pallas_call(
        kernel,
        out_shape=[jax.ShapeDtypeStruct(s, d) for s, d in outs],
        in_specs=[pl.BlockSpec(memory_space=space(i)) for i in range(len(args))],
        out_specs=[pl.BlockSpec(memory_space=pltpu.VMEM) for _ in outs],
        compiler_params=pltpu.CompilerParams(vmem_limit_bytes=VMEM_LIMIT),
        cost_estimate=pl.CostEstimate(flops=flops, bytes_accessed=nbytes, transcendentals=0),
    )(*args)


def body(block_in, out_grad, lengths, ln_gain, ln_bias, b_proj, c_proj, glu_weight, skip_gain, log_rate, angle):
    rows = MICRO * TOK
    x = block_in.reshape(rows, 512)
    go = out_grad.reshape(rows, 512)
    gain, bias, skip = (v.reshape(1, 512) for v in (ln_gain, ln_bias, skip_gain))
    rate2, angle2 = log_rate.reshape(2, 128), angle.reshape(2, 128)
    spread = deal()
    deal_m = jnp.asarray(spread, BF16)
    back_m = jnp.asarray(spread.T.copy(), BF16)
    full = (rows, 512)
    exchange = functools.partial(lax.all_to_all, axis_name="seq", split_axis=0, concat_axis=0, tiled=True)
    normed, pairs, local, ends = call(
        kernel_first, [(full, BF16), (full, BF16), (full, F32), ((N, 8, 128), BF16)], [x, gain, bias, b_proj, deal_m, rate2, angle2],
        flops=300_000_000, nbytes=3_000_000,
    )
    ends = exchange(ends)
    out, act, dgated, hidden, dy, back, prior, firsts = call(
        kernel_middle,
        [(full, BF16), (full, BF16), ((rows, 1024), BF16), (full, BF16), (full, BF16), (full, F32), (full, F32), ((N, 8, 128), BF16)],
        [lengths, ends, local, normed, x, go, c_proj, glu_weight, skip, deal_m, back_m, rate2, angle2],
        smem=(0,), flops=1_200_000_000, nbytes=6_000_000,
    )
    firsts = exchange(firsts)
    (wide,) = call(
        kernel_weights, [((N, 8, 768), BF16)], [act, dgated, hidden, dy], flops=400_000_000, nbytes=3_000_000
    )
    wide = exchange(wide)
    in_grad, narrow = call(
        kernel_last, [(full, BF16), ((N, 8, 384), BF16)],
        [lengths, firsts, back, prior, pairs, normed, x, go, dy, b_proj, gain, skip, back_m, rate2, angle2],
        smem=(0,), flops=600_000_000, nbytes=5_000_000,
    )
    narrow = exchange(narrow)
    b_grad, c_grad, glu_grad, small = call(
        kernel_sum, [((4, 512), F32), ((4, 512), F32), ((4, 1024), F32), ((8, 128), F32)], [wide, narrow], flops=2_000_000, nbytes=2_500_000
    )
    return (
        out.reshape(block_in.shape),
        in_grad.reshape(block_in.shape),
        small[0, 0:4],
        small[0, 4:8],
        b_grad,
        c_grad,
        glu_grad,
        small[0, 8:12],
        small[0, 12:14],
        small[0, 14:16],
    )


def solution(mesh):
    tokens = P(None, "seq", None)
    in_specs = (tokens, tokens) + (P(),) * 9
    out_specs = (tokens, tokens, P("seq"), P("seq"), P("seq", None), P("seq", None), P("seq", None), P("seq"), P("seq"), P("seq"))
    return jax.shard_map(body, mesh=mesh, in_specs=in_specs, out_specs=out_specs, check_vma=False)
```

```python
import functools

import jax
import jax.numpy as jnp
import numpy as np
from jax import lax
from jax.experimental import pallas as pl
from jax.experimental.pallas import tpu as pltpu
from jax.sharding import PartitionSpec as P

F32 = jnp.float32
BF16 = jnp.bfloat16
VMEM_LIMIT = 56 * 1024 * 1024
TOK = 128
GROUPS = TOK // 8
MICRO = 2
HALVES = 2
N = 128
CHIPS = 64


def deal():
    out = np.zeros((256, 256), np.float32)
    for n in range(128):
        out[2 * n, n] = 1.0
        out[2 * n + 1, 128 + n] = 1.0
    return out


def dot(a, b):
    return jnp.dot(a, b, preferred_element_type=F32)


def dot_tn(a, b):
    return lax.dot_general(a, b, (((0,), (0,)), ((), ())), preferred_element_type=F32)


def dot_nt(a, b):
    return lax.dot_general(a, b, (((1,), (1,)), ((), ())), preferred_element_type=F32)


def cmul(a, b):
    return (a[0] * b[0] - a[1] * b[1], a[0] * b[1] + a[1] * b[0])


def conj(a):
    return (a[0], -a[1])


def rows_iota(shape=(8, 128)):
    return lax.broadcasted_iota(jnp.int32, shape, len(shape) - 2)


def params(log_rate, angle):
    u = jnp.exp(log_rate)
    r = jnp.exp(-u)
    lam = (r * jnp.cos(angle), r * jnp.sin(angle))
    w = 2.0 * u
    small = jnp.minimum(w, 0.5)
    poly = 1.0 - small * (1.0 / 11.0)
    for k in range(10, 1, -1):
        poly = 1.0 - small * (1.0 / k) * poly
    gap = jnp.where(w < 0.5, small * poly, 1.0 - jnp.exp(-w))
    scale = jnp.sqrt(gap)
    return u, r, lam, scale


def powers(lam, count):
    out = [lam]
    for _ in range(count):
        out.append(cmul(out[-1], out[-1]))
    return out


def lam_tiles(log_rate_ref, angle_ref):
    out = []
    for half in range(HALVES):
        lr = jnp.broadcast_to(log_rate_ref[half : half + 1, :], (8, 128))
        an = jnp.broadcast_to(angle_ref[half : half + 1, :], (8, 128))
        out.append(params(lr, an))
    return out


def scan_tables(pows, reverse):
    row = rows_iota()
    pos = (7 - row) if reverse else row
    levels = []
    for s, p in ((1, pows[0]), (2, pows[1]), (4, pows[2])):
        keep = pos >= s
        levels.append((s, (jnp.where(keep, p[0], 0.0), jnp.where(keep, p[1], 0.0))))
    e = pos + 1
    table = (jnp.ones((8, 128), F32), jnp.zeros((8, 128), F32))
    for bit in range(4):
        on = (lax.shift_right_logical(e, bit) & 1) == 1
        table = cmul(table, (jnp.where(on, pows[bit][0], 1.0), jnp.where(on, pows[bit][1], 0.0)))
    return levels, table


def group_scan(x, levels, reverse):
    xr, xi = x
    for s, (mr, mi) in levels:
        shift = 8 - s if reverse else s
        rr = pltpu.roll(xr, shift, 1)
        ri = pltpu.roll(xi, shift, 1)
        xr, xi = xr + (mr * rr - mi * ri), xi + (mr * ri + mi * rr)
    return xr, xi


def tile_rows(parts):
    rows = []
    for comp in range(2):
        for micro in range(MICRO):
            for half in range(HALVES):
                rows.append(parts[(micro, half)][comp])
    return jnp.concatenate(rows, axis=0)


def tile_lam(p):
    row = rows_iota()
    odd = (row & 1) == 1
    re = jnp.where(odd, p[1][0], p[0][0])
    im = jnp.where(odd, p[1][1], p[0][1])
    return re, jnp.where(row < 4, -im, im)


def tile_mul(c, coef):
    return c * coef[0] + pltpu.roll(c, 4, 0) * coef[1]


def gather_carry(ends_ref, me, step, dmax, coef, coef8):
    chains = []
    for chain in range(8):
        acc = jnp.zeros((8, 128), F32)
        for i in range(7, -1, -1):
            d = chain * 8 + i
            at = jnp.clip(me + step * (1 + d), 0, N - 1)
            e = ends_ref[at].astype(F32)
            e = jnp.where(d <= dmax, e, 0.0)
            acc = e if i == 7 else tile_mul(acc, coef) + e
        chains.append(acc)
    total = chains[7]
    for chain in range(6, -1, -1):
        total = tile_mul(total, coef8) + chains[chain]
    return total


def segment(lengths_ref, micro, base):
    first = jnp.int32(0)
    last = jnp.int32(N * TOK)
    at = jnp.int32(0)
    for slot in range(16):
        first = jnp.where(at <= base, jnp.maximum(first, at), first)
        last = jnp.where(at > base, jnp.minimum(last, at), last)
        at = at + lengths_ref[micro, slot]
    return first, last


def distance_tiles(lengths_ref, me):
    base = me * TOK
    row = rows_iota()
    second = (row & 2) == 2
    ahead, behind = [], []
    for micro in range(MICRO):
        first, last = segment(lengths_ref, micro, base)
        ahead.append((base - first) // TOK - 1)
        behind.append((last - base) // TOK - 2)
    pick = lambda two: jnp.where(second, two[1], two[0])
    return pick(ahead), pick(behind)


def groups_of(value, micro_groups=MICRO * GROUPS):
    return value.reshape(micro_groups, 8, 128)


def split_channels(value):
    out = []
    for half in range(HALVES):
        c = 256 * half
        out.append((groups_of(value[:, c : c + 128]), groups_of(value[:, c + 128 : c + 256])))
    return out


def join_channels(halves):
    cols = []
    for re, im in halves:
        cols.append(re.reshape(MICRO * TOK, 128))
        cols.append(im.reshape(MICRO * TOK, 128))
    return jnp.concatenate(cols, axis=1)


def permute(value_bf, matrix):
    return jnp.concatenate([dot(value_bf[:, :256], matrix), dot(value_bf[:, 256:], matrix)], axis=1)


def layer_norm(x):
    mean = jnp.mean(x, axis=1, keepdims=True)
    centered = x - mean
    var = jnp.mean(centered * centered, axis=1, keepdims=True)
    rstd = lax.rsqrt(var + 1e-05)
    return centered * rstd, rstd


def chain_from(x, micro, step8, init, reverse):
    before = {}
    v = init
    order = range(GROUPS - 1, -1, -1) if reverse else range(GROUPS)
    for g in order:
        before[g] = v
        xr, xi = x[0][micro * GROUPS + g], x[1][micro * GROUPS + g]
        if v is None:
            v = (xr, xi)
        else:
            m = cmul(v, step8)
            v = (xr + m[0], xi + m[1])
    return before, v


def edge_bcast(pair, edge):
    return tuple(jnp.broadcast_to(p[edge : edge + 1, :], (8, 128)) for p in pair)


def kernel_first(x_ref, gain_ref, bias_ref, b_ref, deal_ref, log_rate_ref, angle_ref, normed_ref, pairs_ref, local_ref, ends_ref):
    x = x_ref[...].astype(F32)
    xhat, _ = layer_norm(x)
    normed = (xhat * gain_ref[...] + bias_ref[...]).astype(BF16)
    normed_ref[...] = normed
    proj = dot(normed, b_ref[...]).astype(BF16)
    pairs = permute(proj, deal_ref[...])
    pairs_ref[...] = pairs.astype(BF16)
    halves = split_channels(pairs)
    lams = lam_tiles(log_rate_ref, angle_ref)
    parts, scanned = {}, []
    for half in range(HALVES):
        _, _, lam, scale = lams[half]
        pows = powers(lam, 3)
        levels, _ = scan_tables(pows, False)
        re, im = halves[half]
        x8 = group_scan((re * scale, im * scale), levels, False)
        scanned.append(x8)
        for micro in range(MICRO):
            _, v = chain_from(x8, micro, pows[3], None, False)
            parts[(micro, half)] = (v[0][7:8, :], v[1][7:8, :])
    local_ref[...] = join_channels(scanned)
    ends_ref[...] = jnp.broadcast_to(tile_rows(parts).astype(BF16)[None], (N, 8, 128))


def tile_row(tile, comp, micro, half):
    at = comp * 4 + micro * 2 + half
    return jnp.broadcast_to(tile[at : at + 1, :], (8, 128))


def carry_pows(lams):
    long_pows = [powers(lams[half][2], 10) for half in range(HALVES)]
    return long_pows


def kernel_middle(
    lengths_ref, ends_ref, local_ref, normed_ref, x_ref, go_ref, c_ref, glu_ref, skip_ref, deal_ref, deal_back_ref, log_rate_ref, angle_ref,
    out_ref, act_ref, dgated_ref, hidden_ref, dy_ref, back_ref, prior_ref, firsts_ref,
):
    me = lax.axis_index("seq")
    ahead, _ = distance_tiles(lengths_ref, me)
    lams = lam_tiles(log_rate_ref, angle_ref)
    pows = carry_pows(lams)
    coef = tile_lam([p[7] for p in pows])
    coef8 = tile_lam([p[10] for p in pows])
    carry = gather_carry(ends_ref, me, -1, ahead, coef, coef8)
    local = split_channels(local_ref[...])
    row = rows_iota((MICRO * GROUPS, 8, 128))
    states, priors = [], []
    for half in range(HALVES):
        _, table = scan_tables(pows[half], False)
        x8 = local[half]
        before_r, before_i = [], []
        for micro in range(MICRO):
            init = (tile_row(carry, 0, micro, half), tile_row(carry, 1, micro, half))
            before, _ = chain_from(x8, micro, pows[half][3], init, False)
            for g in range(GROUPS):
                edge = edge_bcast(before[g], 7)
                before_r.append(edge[0])
                before_i.append(edge[1])
        br, bi = jnp.stack(before_r), jnp.stack(before_i)
        hr = x8[0] + (table[0] * br - table[1] * bi)
        hi = x8[1] + (table[0] * bi + table[1] * br)
        states.append((hr, hi))
        priors.append((jnp.where(row == 0, br, pltpu.roll(hr, 1, 1)), jnp.where(row == 0, bi, pltpu.roll(hi, 1, 1))))
    prior_ref[...] = join_channels(priors)
    hidden = permute(join_channels(states).astype(BF16), deal_back_ref[...]).astype(BF16)
    hidden_ref[...] = hidden
    y = dot(hidden, c_ref[...]) + skip_ref[...] * normed_ref[...].astype(F32)
    k0, k1 = 0.7978845608028654, 0.044715
    yy = y * y
    t = jnp.tanh(k0 * (y + k1 * (yy * y)))
    act = (0.5 * y * (1.0 + t)).astype(BF16)
    act_ref[...] = act
    slope = 0.5 * (1.0 + t) + 0.5 * y * (1.0 - t * t) * (k0 * (1.0 + 3.0 * k1 * yy))
    gated = dot(act, glu_ref[...])
    value, gate = gated[:, :512], gated[:, 512:]
    sig = jax.nn.sigmoid(gate)
    go = go_ref[...].astype(F32)
    out_ref[...] = (x_ref[...].astype(F32) + value * sig).astype(BF16)
    gs = go * sig
    dgated = jnp.concatenate([gs, gs * value * (1.0 - sig)], axis=1).astype(BF16)
    dgated_ref[...] = dgated
    dy = (dot_nt(dgated, glu_ref[...]) * slope).astype(BF16)
    dy_ref[...] = dy
    dhidden = dot_nt(dy, c_ref[...]).astype(BF16)
    q = split_channels(permute(dhidden, deal_ref[...]))
    parts, scanned = {}, []
    for half in range(HALVES):
        cp = [conj(p) for p in pows[half][:4]]
        levels, _ = scan_tables(cp, True)
        x8 = group_scan(q[half], levels, True)
        scanned.append(x8)
        for micro in range(MICRO):
            _, v = chain_from(x8, micro, cp[3], None, True)
            parts[(micro, half)] = (v[0][0:1, :], v[1][0:1, :])
    back_ref[...] = join_channels(scanned)
    firsts_ref[...] = jnp.broadcast_to(tile_rows(parts).astype(BF16)[None], (N, 8, 128))


def chunk_rows(left, right):
    w = left.shape[1]
    a = left.reshape(CHIPS, 8, w)
    b = right.reshape(CHIPS, 8, w)
    low = rows_iota((CHIPS, 8, w)) < 4
    return jnp.where(low, a, pltpu.roll(b, 4, 1)), jnp.where(low, pltpu.roll(a, 4, 1), b)


def kernel_weights(act_ref, dgated_ref, hidden_ref, dy_ref, keep_ref, send_ref):
    core = lax.axis_index("seq") % 2
    glu = dot_tn(act_ref[...], dgated_ref[...])
    c = dot_tn(hidden_ref[...], dy_ref[...])
    even, odd = chunk_rows(glu[:, :768], jnp.concatenate([glu[:, 768:], c], axis=1))
    keep_ref[...] = jnp.where(core == 0, even, odd).astype(BF16)
    send_ref[...] = jnp.where(core == 0, odd, even).astype(BF16)


def kernel_pack(keep_ref, got_ref, out_ref):
    out_ref[:, :, 0:768] = (keep_ref[...].astype(F32) + got_ref[...].astype(F32)).astype(BF16)


def kernel_pack_rest(keep_ref, got_ref, buffer_ref, out_ref, rest, sem):
    del buffer_ref
    rest[:, :, 0:256] = (keep_ref[:, :, 0:256].astype(F32) + got_ref[:, :, 0:256].astype(F32)).astype(BF16)
    low = rows_iota((CHIPS, 8, 128)) < 4
    rest[:, :, 256:384] = jnp.where(low, keep_ref[:, :, 256:384].astype(F32), got_ref[:, :, 256:384].astype(F32)).astype(BF16)
    copy = pltpu.make_async_copy(rest, out_ref.at[:, :, 768:1152], sem)
    copy.start()
    copy.wait()


def small_chunks(vectors, channels, core):
    dest = 2 * lax.broadcasted_iota(jnp.int32, (CHIPS, 512), 0) + core
    feature = lax.broadcasted_iota(jnp.int32, (CHIPS, 512), 1)
    lane = lax.broadcasted_iota(jnp.int32, (512, 128), 1)
    row = lax.broadcasted_iota(jnp.int32, (512, 128), 0)
    by_four = ((feature // 4) == dest, row % 4)
    by_two = (((feature % 256) // 2) == dest, row % 2 + 2 * (row // 256))
    total = jnp.zeros((CHIPS, 128), F32)
    for v, vec in enumerate(vectors + [channels]):
        mine, inner = by_two if v == len(vectors) else by_four
        high = vec.astype(BF16).astype(F32)
        rest = vec - high
        for part, base in ((high, 4 * v), (rest, 64 + 4 * v)):
            spread = jnp.where(mine, part, 0.0).astype(BF16)
            place = jnp.where(lane == base + inner, 1.0, 0.0).astype(BF16)
            total = total + dot(spread, place)
    return total


def kernel_last(
    lengths_ref, firsts_ref, back_ref, prior_ref, pairs_ref, normed_ref, x_ref, go_ref, dy_ref, b_ref, gain_ref, skip_ref, deal_back_ref,
    log_rate_ref, angle_ref, buffer_ref, in_grad_ref, keep_ref, send_ref,
):
    del buffer_ref
    me = lax.axis_index("seq")
    core = me % 2
    _, behind = distance_tiles(lengths_ref, me)
    lams = lam_tiles(log_rate_ref, angle_ref)
    pows = [[conj(p) for p in per_half] for per_half in carry_pows(lams)]
    coef = tile_lam([p[7] for p in pows])
    coef8 = tile_lam([p[10] for p in pows])
    carry = gather_carry(firsts_ref, me, 1, behind, coef, coef8)
    local = split_channels(back_ref[...])
    prior = split_channels(prior_ref[...])
    pairs = split_channels(pairs_ref[...].astype(F32))
    projs, rates, angles = [], [], []
    for half in range(HALVES):
        u, r, lam, scale = lams[half]
        _, table = scan_tables(pows[half], True)
        x8 = local[half]
        after_r, after_i = [], []
        for micro in range(MICRO):
            init = (tile_row(carry, 0, micro, half), tile_row(carry, 1, micro, half))
            after, _ = chain_from(x8, micro, pows[half][3], init, True)
            for g in range(GROUPS):
                edge = edge_bcast(after[g], 0)
                after_r.append(edge[0])
                after_i.append(edge[1])
        ar, ai = jnp.stack(after_r), jnp.stack(after_i)
        gr = x8[0] + (table[0] * ar - table[1] * ai)
        gi = x8[1] + (table[0] * ai + table[1] * ar)
        pr, pi = prior[half]
        total = lambda v: jnp.sum(jnp.sum(v, axis=0), axis=0, keepdims=True)
        d_re = total(gr * pr + gi * pi)
        d_im = total(gi * pr - gr * pi)
        d_scale = total(gr * pairs[half][0] + gi * pairs[half][1])
        one = lambda t: t[0:1, :]
        lr, li = one(lam[0]), one(lam[1])
        rates.append(one(u) * (one(r) * one(r) * d_scale / one(scale) - (lr * d_re + li * d_im)))
        angles.append(lr * d_im - li * d_re)
        projs.append((gr * scale, gi * scale))
    dproj = permute(join_channels(projs).astype(BF16), deal_back_ref[...]).astype(BF16)
    normed = normed_ref[...]
    b_grad = dot_tn(normed, dproj)
    dy = dy_ref[...].astype(F32)
    dnormed = dot_nt(dproj, b_ref[...]) + skip_ref[...] * dy
    go = go_ref[...].astype(F32)
    xhat, rstd = layer_norm(x_ref[...].astype(F32))
    col = lambda v: jnp.sum(v, axis=0, keepdims=True)
    gain_grad = col(dnormed * xhat)
    bias_grad = col(dnormed)
    skip_grad = col(dy * normed.astype(F32))
    channels = jnp.concatenate(rates + angles, axis=1)
    even, odd = chunk_rows(b_grad[:, :256], b_grad[:, 256:])
    keep_ref[:, :, 0:256] = jnp.where(core == 0, even, odd).astype(BF16)
    send_ref[:, :, 0:256] = jnp.where(core == 0, odd, even).astype(BF16)
    for ref, mine in ((keep_ref, core), (send_ref, 1 - core)):
        smalls = small_chunks([gain_grad, bias_grad, skip_grad], channels, mine)
        ref[:, :, 256:384] = jnp.broadcast_to(smalls[:, None, :], (CHIPS, 8, 128)).astype(BF16)
    dx = dnormed * gain_ref[...]
    m1 = jnp.mean(dx, axis=1, keepdims=True)
    m2 = jnp.mean(dx * xhat, axis=1, keepdims=True)
    in_grad_ref[...] = (go + rstd * (dx - m1 - xhat * m2)).astype(BF16)


def kernel_sum(parts_ref, b_ref, c_ref, glu_ref, gain_ref, bias_ref, skip_ref, rate_ref, angle_ref):
    total = jnp.sum(parts_ref[...].astype(F32), axis=0)
    glu_ref[:, 0:768] = total[0:4, 0:768]
    glu_ref[:, 768:1024] = total[4:8, 0:256]
    c_ref[...] = total[4:8, 256:768]
    b_ref[:, 0:256] = total[0:4, 768:1024]
    b_ref[:, 256:512] = total[4:8, 768:1024]
    small = total[:, 1024:1152]
    small = small + pltpu.roll(small, 4, 0)
    small = small + pltpu.roll(small, 64, 1)
    for ref, at in ((gain_ref, 0), (bias_ref, 4), (skip_ref, 8), (rate_ref, 12), (angle_ref, 14)):
        ref[...] = (pltpu.roll(small, 128 - at, 1) if at else small)[0:1, 0 : ref.shape[1]]


def call(kernel, outs, args, smem=(), anywhere=(), out_any=(), scratch=(), alias=None, flops=0, nbytes=0):
    def space(i):
        if i in smem:
            return pltpu.SMEM
        return pl.ANY if i in anywhere else pltpu.VMEM

    return pl.pallas_call(
        kernel,
        out_shape=[jax.ShapeDtypeStruct(s, d) for s, d in outs],
        in_specs=[pl.BlockSpec(memory_space=space(i)) for i in range(len(args))],
        out_specs=[pl.BlockSpec(memory_space=pl.ANY if i in out_any else pltpu.VMEM) for i in range(len(outs))],
        scratch_shapes=list(scratch),
        input_output_aliases=alias or {},
        compiler_params=pltpu.CompilerParams(vmem_limit_bytes=VMEM_LIMIT),
        cost_estimate=pl.CostEstimate(flops=flops, bytes_accessed=nbytes, transcendentals=0),
    )(*args)


def body(block_in, out_grad, lengths, ln_gain, ln_bias, b_proj, c_proj, glu_weight, skip_gain, log_rate, angle):
    rows = MICRO * TOK
    x = block_in.reshape(rows, 512)
    go = out_grad.reshape(rows, 512)
    gain, bias, skip = (v.reshape(1, 512) for v in (ln_gain, ln_bias, skip_gain))
    rate2, angle2 = log_rate.reshape(2, 128), angle.reshape(2, 128)
    spread = deal()
    deal_m = jnp.asarray(spread, BF16)
    back_m = jnp.asarray(spread.T.copy(), BF16)
    full = (rows, 512)
    exchange = functools.partial(lax.all_to_all, axis_name="seq", split_axis=0, concat_axis=0, tiled=True)
    normed, pairs, local, ends = call(
        kernel_first, [(full, BF16), (full, BF16), (full, F32), ((N, 8, 128), BF16)], [x, gain, bias, b_proj, deal_m, rate2, angle2],
        flops=300_000_000, nbytes=3_000_000,
    )
    ends = exchange(ends)
    out, act, dgated, hidden, dy, back, prior, firsts = call(
        kernel_middle,
        [(full, BF16), (full, BF16), ((rows, 1024), BF16), (full, BF16), (full, BF16), (full, F32), (full, F32), ((N, 8, 128), BF16)],
        [lengths, ends, local, normed, x, go, c_proj, glu_weight, skip, deal_m, back_m, rate2, angle2],
        smem=(0,), flops=1_200_000_000, nbytes=6_000_000,
    )
    firsts = exchange(firsts)
    swap = functools.partial(lax.ppermute, axis_name="seq", perm=[(i, i ^ 1) for i in range(N)])
    same_core = [[2 * t + core for t in range(CHIPS)] for core in range(2)]
    wide_shape, rest_shape = (CHIPS, 8, 768), (CHIPS, 8, 384)
    keep, send = call(
        kernel_weights, [(wide_shape, BF16), (wide_shape, BF16)], [act, dgated, hidden, dy], flops=400_000_000, nbytes=3_000_000
    )
    (packed,) = call(kernel_pack, [((CHIPS, 8, 1152), BF16)], [keep, swap(send)], flops=1_000_000, nbytes=2_400_000)
    in_grad, keep, send = call(
        kernel_last, [(full, BF16), (rest_shape, BF16), (rest_shape, BF16)],
        [lengths, firsts, back, prior, pairs, normed, x, go, dy, b_proj, gain, skip, back_m, rate2, angle2, packed],
        smem=(0,), anywhere=(15,), flops=600_000_000, nbytes=5_000_000,
    )
    (packed,) = call(
        kernel_pack_rest, [((CHIPS, 8, 1152), BF16)], [keep, swap(send), packed], anywhere=(2,), out_any=(0,), alias={2: 0},
        scratch=[pltpu.VMEM(rest_shape, BF16), pltpu.SemaphoreType.DMA], flops=1_000_000, nbytes=1_200_000,
    )
    parts = lax.all_to_all(packed, "seq", split_axis=0, concat_axis=0, tiled=True, axis_index_groups=same_core)
    b_grad, c_grad, glu_grad, gain_grad, bias_grad, skip_grad, rate_grad, angle_grad = call(
        kernel_sum,
        [((4, 512), F32), ((4, 512), F32), ((4, 1024), F32)] + [((1, w), F32) for w in (4, 4, 4, 2, 2)],
        [parts], flops=1_000_000, nbytes=1_300_000,
    )
    return (
        out.reshape(block_in.shape),
        in_grad.reshape(block_in.shape),
        gain_grad.reshape(4),
        bias_grad.reshape(4),
        b_grad,
        c_grad,
        glu_grad,
        skip_grad.reshape(4),
        rate_grad.reshape(2),
        angle_grad.reshape(2),
    )


def solution(mesh):
    tokens = P(None, "seq", None)
    in_specs = (tokens, tokens) + (P(),) * 9
    out_specs = (tokens, tokens, P("seq"), P("seq"), P("seq", None), P("seq", None), P("seq", None), P("seq"), P("seq"), P("seq"))
    return jax.shard_map(body, mesh=mesh, in_specs=in_specs, out_specs=out_specs, check_vma=False)
```

```python
import functools

import jax
import jax.numpy as jnp
import numpy as np
from jax import lax
from jax.experimental import pallas as pl
from jax.experimental.pallas import tpu as pltpu
from jax.sharding import PartitionSpec as P

F32 = jnp.float32
BF16 = jnp.bfloat16
VMEM_LIMIT = 40 * 1024 * 1024
TOK = 128
GROUPS = TOK // 8
MICRO = 2
HALVES = 2
N = 128
CHIPS = 64


def deal():
    out = np.zeros((256, 256), np.float32)
    for n in range(128):
        out[2 * n, n] = 1.0
        out[2 * n + 1, 128 + n] = 1.0
    return out


def dot(a, b):
    return jnp.dot(a, b, preferred_element_type=F32)


def dot_tn(a, b):
    return lax.dot_general(a, b, (((0,), (0,)), ((), ())), preferred_element_type=F32)


def dot_nt(a, b):
    return lax.dot_general(a, b, (((1,), (1,)), ((), ())), preferred_element_type=F32)


def cmul(a, b):
    return (a[0] * b[0] - a[1] * b[1], a[0] * b[1] + a[1] * b[0])


def conj(a):
    return (a[0], -a[1])


def rows_iota(shape=(8, 128)):
    return lax.broadcasted_iota(jnp.int32, shape, len(shape) - 2)


def params(log_rate, angle):
    u = jnp.exp(log_rate)
    r = jnp.exp(-u)
    lam = (r * jnp.cos(angle), r * jnp.sin(angle))
    w = 2.0 * u
    small = jnp.minimum(w, 0.5)
    poly = 1.0 - small * (1.0 / 11.0)
    for k in range(10, 1, -1):
        poly = 1.0 - small * (1.0 / k) * poly
    gap = jnp.where(w < 0.5, small * poly, 1.0 - jnp.exp(-w))
    scale = jnp.sqrt(gap)
    return u, r, lam, scale


def powers(lam, count):
    out = [lam]
    for _ in range(count):
        out.append(cmul(out[-1], out[-1]))
    return out


def lam_tiles(log_rate_ref, angle_ref):
    out = []
    for half in range(HALVES):
        lr = jnp.broadcast_to(log_rate_ref[half : half + 1, :], (8, 128))
        an = jnp.broadcast_to(angle_ref[half : half + 1, :], (8, 128))
        out.append(params(lr, an))
    return out


def scan_tables(pows, reverse):
    row = rows_iota()
    pos = (7 - row) if reverse else row
    levels = []
    for s, p in ((1, pows[0]), (2, pows[1]), (4, pows[2])):
        keep = pos >= s
        levels.append((s, (jnp.where(keep, p[0], 0.0), jnp.where(keep, p[1], 0.0))))
    e = pos + 1
    table = (jnp.ones((8, 128), F32), jnp.zeros((8, 128), F32))
    for bit in range(4):
        on = (lax.shift_right_logical(e, bit) & 1) == 1
        table = cmul(table, (jnp.where(on, pows[bit][0], 1.0), jnp.where(on, pows[bit][1], 0.0)))
    return levels, table


def group_scan(x, levels, reverse):
    xr, xi = x
    for s, (mr, mi) in levels:
        shift = 8 - s if reverse else s
        rr = pltpu.roll(xr, shift, 1)
        ri = pltpu.roll(xi, shift, 1)
        xr, xi = xr + (mr * rr - mi * ri), xi + (mr * ri + mi * rr)
    return xr, xi


def tile_rows(parts):
    rows = []
    for comp in range(2):
        for micro in range(MICRO):
            for half in range(HALVES):
                rows.append(parts[(micro, half)][comp])
    return jnp.concatenate(rows, axis=0)


def tile_lam(p):
    row = rows_iota()
    odd = (row & 1) == 1
    re = jnp.where(odd, p[1][0], p[0][0])
    im = jnp.where(odd, p[1][1], p[0][1])
    return re, jnp.where(row < 4, -im, im)


def tile_mul(c, coef):
    return c * coef[0] + pltpu.roll(c, 4, 0) * coef[1]


def gather_carry(ends_ref, me, step, dmax, coef, coef8):
    chains = []
    for chain in range(8):
        acc = jnp.zeros((8, 128), F32)
        for i in range(7, -1, -1):
            d = chain * 8 + i
            at = jnp.clip(me + step * (1 + d), 0, N - 1)
            e = ends_ref[at, 0].astype(F32)
            e = jnp.where(d <= dmax, e, 0.0)
            acc = e if i == 7 else tile_mul(acc, coef) + e
        chains.append(acc)
    total = chains[7]
    for chain in range(6, -1, -1):
        total = tile_mul(total, coef8) + chains[chain]
    return total


def segment(lengths_ref, micro, base):
    first = jnp.int32(0)
    last = jnp.int32(N * TOK)
    at = jnp.int32(0)
    for slot in range(16):
        first = jnp.where(at <= base, jnp.maximum(first, at), first)
        last = jnp.where(at > base, jnp.minimum(last, at), last)
        at = at + lengths_ref[micro, slot]
    return first, last


def distance_tiles(lengths_ref, me):
    base = me * TOK
    row = rows_iota()
    second = (row & 2) == 2
    ahead, behind = [], []
    for micro in range(MICRO):
        first, last = segment(lengths_ref, micro, base)
        ahead.append((base - first) // TOK - 1)
        behind.append((last - base) // TOK - 2)
    pick = lambda two: jnp.where(second, two[1], two[0])
    return pick(ahead), pick(behind)


def groups_of(value, micro_groups=MICRO * GROUPS):
    return value.reshape(micro_groups, 8, 128)


def split_channels(value):
    out = []
    for half in range(HALVES):
        c = 256 * half
        out.append((groups_of(value[:, c : c + 128]), groups_of(value[:, c + 128 : c + 256])))
    return out


def join_channels(halves):
    cols = []
    for re, im in halves:
        cols.append(re.reshape(MICRO * TOK, 128))
        cols.append(im.reshape(MICRO * TOK, 128))
    return jnp.concatenate(cols, axis=1)


def permute(value_bf, matrix):
    return jnp.concatenate([dot(value_bf[:, :256], matrix), dot(value_bf[:, 256:], matrix)], axis=1)


def layer_norm(x):
    mean = jnp.mean(x, axis=1, keepdims=True)
    centered = x - mean
    var = jnp.mean(centered * centered, axis=1, keepdims=True)
    rstd = lax.rsqrt(var + 1e-05)
    return centered * rstd, rstd


def chain_from(x, micro, step8, init, reverse):
    before = {}
    v = init
    order = range(GROUPS - 1, -1, -1) if reverse else range(GROUPS)
    for g in order:
        before[g] = v
        xr, xi = x[0][micro * GROUPS + g], x[1][micro * GROUPS + g]
        if v is None:
            v = (xr, xi)
        else:
            m = cmul(v, step8)
            v = (xr + m[0], xi + m[1])
    return before, v


def edge_bcast(pair, edge):
    return tuple(jnp.broadcast_to(p[edge : edge + 1, :], (8, 128)) for p in pair)


class Ports:
    def __init__(self, ins, outs, refs):
        n_in, n_out = len(ins), len(outs)
        scratch = list(refs[n_in + n_out :])
        self.refs, self.pending, self.leaving = {}, {}, []
        self.out_copies = {}
        held_in = [(name, ref) for (name, _, mode), ref in zip(ins, refs) if mode == "hbm"]
        held_out = [(name, ref) for (name, _, _, mode), ref in zip(outs, refs[n_in:]) if mode == "hbm"]
        for (name, _, _mode), ref in zip(ins, refs):
            self.refs[name] = ref
        for (name, _, _, _mode), ref in zip(outs, refs[n_in:]):
            self.refs[name] = ref
        sems = scratch[-1] if held_in or held_out else None
        for i, (name, ref) in enumerate(held_in):
            copy = pltpu.make_async_copy(ref, scratch[i], sems.at[i])
            copy.start()
            self.pending[name] = copy
            self.refs[name] = scratch[i]
        for j, (name, ref) in enumerate(held_out):
            i = len(held_in) + j
            self.refs[name] = scratch[i]
            self.out_copies[name] = pltpu.make_async_copy(scratch[i], ref, sems.at[i])

    def ref(self, name):
        if name in self.pending:
            self.pending.pop(name).wait()
        return self.refs[name]

    def get(self, name):
        return self.ref(name)[...]

    def put(self, name, value):
        self.refs[name][...] = value
        self.send(name)

    def send(self, name):
        if name in self.out_copies:
            self.out_copies[name].start()
            self.leaving.append(name)

    def finish(self):
        for name in list(self.pending):
            self.ref(name)
        for name in self.leaving:
            self.out_copies[name].wait()


def call(kernel, ins, outs, extra=(), flops=0, nbytes=0):
    def run(*refs):
        n_extra = len(extra)
        ports = Ports(ins, outs, refs[: len(refs) - n_extra] if n_extra else refs)
        kernel(ports, *(refs[len(refs) - n_extra :] if n_extra else ()))
        ports.finish()

    spaces = {"hbm": pl.ANY, "vmem": pltpu.VMEM, "auto": pltpu.VMEM, "smem": pltpu.SMEM}
    args = []
    for _, array, mode in ins:
        if mode == "hbm":
            array = pltpu.with_memory_space_constraint(array, pltpu.HBM)
        elif mode == "vmem":
            array = pltpu.with_memory_space_constraint(array, pltpu.VMEM)
        args.append(array)
    shapes = []
    for _, shape, kind, mode in outs:
        shapes.append(pltpu.VMEM(shape, kind) if mode == "vmem" else jax.ShapeDtypeStruct(shape, kind))
    held = [(a.shape, a.dtype) for _, a, mode in ins if mode == "hbm"] + [(s, d) for _, s, d, mode in outs if mode == "hbm"]
    scratch = [pltpu.VMEM(s, d) for s, d in held]
    if held:
        scratch.append(pltpu.SemaphoreType.DMA((len(held),)))
    return pl.pallas_call(
        run,
        out_shape=shapes,
        in_specs=[pl.BlockSpec(memory_space=spaces[mode]) for _, _, mode in ins],
        out_specs=[pl.BlockSpec(memory_space=spaces[mode]) for _, _, _, mode in outs],
        scratch_shapes=scratch + list(extra),
        compiler_params=pltpu.CompilerParams(vmem_limit_bytes=VMEM_LIMIT),
        cost_estimate=pl.CostEstimate(flops=flops, bytes_accessed=nbytes, transcendentals=0),
    )(*args)


def chunk_rows(left, right):
    w = left.shape[1]
    a = left.reshape(CHIPS, 8, w)
    b = right.reshape(CHIPS, 8, w)
    low = rows_iota((CHIPS, 8, w)) < 4
    return jnp.where(low, a, pltpu.roll(b, 4, 1)), jnp.where(low, pltpu.roll(a, 4, 1), b)


def kernel_first(io):
    x = io.get("x").astype(F32)
    xhat, _ = layer_norm(x)
    normed = (xhat * io.get("gain") + io.get("bias")).astype(BF16)
    io.put("normed", normed)
    proj = dot(normed, io.get("b")).astype(BF16)
    pairs = permute(proj, io.get("deal"))
    io.put("pairs", pairs.astype(BF16))
    halves = split_channels(pairs)
    lams = lam_tiles(io.ref("log_rate"), io.ref("angle"))
    parts, scanned = {}, []
    for half in range(HALVES):
        _, _, lam, scale = lams[half]
        pows = powers(lam, 3)
        levels, _ = scan_tables(pows, False)
        re, im = halves[half]
        x8 = group_scan((re * scale, im * scale), levels, False)
        scanned.append(x8)
        for micro in range(MICRO):
            _, v = chain_from(x8, micro, pows[3], None, False)
            parts[(micro, half)] = (v[0][7:8, :], v[1][7:8, :])
    io.put("local", join_channels(scanned))
    ends = io.ref("ends")
    ends[:, 0] = jnp.broadcast_to(tile_rows(parts).astype(BF16)[None], (N, 8, 128))
    even, odd = chunk_rows(xhat[:TOK].T, xhat[TOK:].T)
    ends[:, 1] = jnp.stack([even, odd], axis=1).reshape(N, 8, 128).astype(BF16)


def tile_row(tile, comp, micro, half):
    at = comp * 4 + micro * 2 + half
    return jnp.broadcast_to(tile[at : at + 1, :], (8, 128))


def total(v):
    return jnp.sum(jnp.sum(v, axis=0), axis=0, keepdims=True)


def column_sum(v):
    return jnp.sum(v, axis=0, keepdims=True)


def place_smalls(fours, twos, core):
    dest = 2 * lax.broadcasted_iota(jnp.int32, (CHIPS, 512), 0) + core
    feature = lax.broadcasted_iota(jnp.int32, (CHIPS, 512), 1)
    lane = lax.broadcasted_iota(jnp.int32, (512, 128), 1)
    row = lax.broadcasted_iota(jnp.int32, (512, 128), 0)
    by_four = ((feature // 4) == dest, row % 4)
    by_two = (((feature % 256) // 2) == dest, row % 2 + 2 * (row // 256))
    out = jnp.zeros((CHIPS, 128), F32)
    for v, vec in enumerate(fours + twos):
        mine, inner = by_four if v < len(fours) else by_two
        high = vec.astype(BF16).astype(F32)
        rest = vec - high
        for part, base in ((high, 4 * v), (rest, 64 + 4 * v)):
            spread = jnp.where(mine, part, 0.0).astype(BF16)
            place = jnp.where(lane == base + inner, 1.0, 0.0).astype(BF16)
            out = out + dot(spread, place)
    return out


def kernel_middle(io):
    me = lax.axis_index("seq")
    core = me % 2
    ahead, _ = distance_tiles(io.ref("lengths"), me)
    lams = lam_tiles(io.ref("log_rate"), io.ref("angle"))
    pows = [powers(lams[half][2], 10) for half in range(HALVES)]
    coef = tile_lam([p[7] for p in pows])
    coef8 = tile_lam([p[10] for p in pows])
    carry = gather_carry(io.ref("ends"), me, -1, ahead, coef, coef8)
    local = split_channels(io.get("local"))
    row = rows_iota((MICRO * GROUPS, 8, 128))
    states, priors, heads = [], [], {}
    for half in range(HALVES):
        _, table = scan_tables(pows[half], False)
        x8 = local[half]
        before_r, before_i = [], []
        for micro in range(MICRO):
            init = (tile_row(carry, 0, micro, half), tile_row(carry, 1, micro, half))
            before, _ = chain_from(x8, micro, pows[half][3], init, False)
            for g in range(GROUPS):
                edge = edge_bcast(before[g], 7)
                before_r.append(edge[0])
                before_i.append(edge[1])
        br, bi = jnp.stack(before_r), jnp.stack(before_i)
        hr = x8[0] + (table[0] * br - table[1] * bi)
        hi = x8[1] + (table[0] * bi + table[1] * br)
        states.append((hr, hi))
        prior = (jnp.where(row == 0, br, pltpu.roll(hr, 1, 1)), jnp.where(row == 0, bi, pltpu.roll(hi, 1, 1)))
        priors.append(prior)
        _, back_table = scan_tables([conj(p) for p in pows[half][:4]], True)
        for micro in range(MICRO):
            _, v = chain_from(prior, micro, pows[half][3], None, False)
            m = cmul(v, conj(back_table))
            heads[(micro, half)] = (column_sum(m[0]), column_sum(m[1]))
    hidden = permute(join_channels(states).astype(BF16), io.get("deal_back")).astype(BF16)
    normed = io.get("normed")
    y = dot(hidden, io.get("c")) + io.get("skip") * normed.astype(F32)
    k0, k1 = 0.7978845608028654, 0.044715
    yy = y * y
    t = jnp.tanh(k0 * (y + k1 * (yy * y)))
    act = (0.5 * y * (1.0 + t)).astype(BF16)
    slope = 0.5 * (1.0 + t) + 0.5 * y * (1.0 - t * t) * (k0 * (1.0 + 3.0 * k1 * yy))
    gated = dot(act, io.get("glu"))
    value, gate = gated[:, :512], gated[:, 512:]
    sig = jax.nn.sigmoid(gate)
    go = io.get("go").astype(F32)
    x = io.get("x").astype(F32)
    io.put("out", (x + value * sig).astype(BF16))
    gs = go * sig
    dgated = jnp.concatenate([gs, gs * value * (1.0 - sig)], axis=1).astype(BF16)
    dy = (dot_nt(dgated, io.get("glu")) * slope).astype(BF16)
    dhidden = dot_nt(dy, io.get("c")).astype(BF16)
    q = split_channels(permute(dhidden, io.get("deal")))
    pairs = split_channels(io.get("pairs").astype(F32))
    parts, projs, rates, angles = {}, [], [], []
    for half in range(HALVES):
        u, r, lam, scale = lams[half]
        cp = [conj(p) for p in pows[half][:4]]
        levels, table = scan_tables(cp, True)
        x8 = group_scan(q[half], levels, True)
        after_r, after_i = [], []
        for micro in range(MICRO):
            zero = (jnp.zeros((8, 128), F32), jnp.zeros((8, 128), F32))
            after, v = chain_from(x8, micro, cp[3], zero, True)
            parts[(micro, half)] = (v[0][0:1, :], v[1][0:1, :])
            for g in range(GROUPS):
                edge = edge_bcast(after[g], 0)
                after_r.append(edge[0])
                after_i.append(edge[1])
        ar, ai = jnp.stack(after_r), jnp.stack(after_i)
        gr = x8[0] + (table[0] * ar - table[1] * ai)
        gi = x8[1] + (table[0] * ai + table[1] * ar)
        pr, pi = priors[half]
        d_re = total(gr * pr + gi * pi)
        d_im = total(gi * pr - gr * pi)
        d_scale = total(gr * pairs[half][0] + gi * pairs[half][1])
        rate, turn = chain_rule([t[0:1, :] for t in (u, r, lam[0], lam[1], scale)], d_re, d_im, d_scale)
        rates.append(rate)
        angles.append(turn)
        projs.append((gr * scale, gi * scale))
    dproj = permute(join_channels(projs).astype(BF16), io.get("deal_back")).astype(BF16)
    dyf = dy.astype(F32)
    dnormed = dot_nt(dproj, io.get("b")) + io.get("skip") * dyf
    io.put("dnormed", dnormed)
    xhat, _ = layer_norm(x)
    fours = [column_sum(dnormed * xhat), column_sum(dnormed), column_sum(dyf * normed.astype(F32))]
    twos = [jnp.concatenate(rates + angles, axis=1)]
    for micro in range(MICRO):
        twos.append(jnp.concatenate([heads[(micro, half)][comp] for comp in range(2) for half in range(HALVES)], axis=1))
    first = tile_rows(parts).astype(BF16)
    keep, send = io.ref("keep"), io.ref("send")
    for ref in (keep, send):
        ref[:, :, 1024:1152] = jnp.broadcast_to(first[None], (CHIPS, 8, 128))
    for ref, mine in ((keep, core), (send, 1 - core)):
        ref[:, :, 1152:1280] = jnp.broadcast_to(place_smalls(fours, twos, mine)[:, None, :], (CHIPS, 8, 128)).astype(BF16)
    glu_grad = dot_tn(act, dgated)
    c_grad = dot_tn(hidden, dy)
    b_grad = dot_tn(normed, dproj)
    even, odd = chunk_rows(glu_grad, jnp.concatenate([c_grad, b_grad], axis=1))
    keep[:, :, 0:1024] = jnp.where(core == 0, even, odd).astype(BF16)
    send[:, :, 0:1024] = jnp.where(core == 0, odd, even).astype(BF16)


def chain_rule(rows, d_re, d_im, d_scale):
    u, r, lr, li, scale = rows
    return u * (r * r * d_scale / scale - (lr * d_re + li * d_im)), lr * d_im - li * d_re


def kernel_pack(io):
    keep, got, out = io.ref("keep"), io.ref("got"), io.ref("packed")
    out[:, :, 0:1024] = (keep[:, :, 0:1024].astype(F32) + got[:, :, 0:1024].astype(F32)).astype(BF16)
    out[:, :, 1024:1152] = keep[:, :, 1024:1152]
    out[:, :, 1152:1280] = got[:, :, 1024:1152]
    low = rows_iota((CHIPS, 8, 128)) < 4
    out[:, :, 1280:1408] = jnp.where(low, keep[:, :, 1152:1280].astype(F32), got[:, :, 1152:1280].astype(F32)).astype(BF16)


def start_bits(lengths_ref, micro):
    bits = jnp.int32(0)
    at = jnp.int32(0)
    for slot in range(16):
        unit = at // (8 * TOK)
        bits = jnp.where(at < N * TOK, bits | lax.shift_left(jnp.int32(1), jnp.minimum(unit, 15)), bits)
        at = at + lengths_ref[micro, slot]
    return bits


def all_carries(first, lengths_ref, coefs):
    row = rows_iota()
    second = (row & 2) == 2
    bits = [start_bits(lengths_ref, micro) for micro in range(MICRO)]
    groups = first.reshape(16, 8, 8, 128)
    step = lambda c, coef: c * coef[0] + pltpu.roll(c, 4, 1) * coef[1]
    inner = [None] * 8
    inner[7] = jnp.zeros((16, 8, 128), F32)
    for p in range(6, -1, -1):
        inner[p] = groups[:, p + 1] + step(inner[p + 1], coefs[0])
    whole = groups[:, 0] + step(inner[0], coefs[0])
    entering = [None] * 16
    entering[15] = jnp.zeros((8, 128), F32)
    for g in range(14, -1, -1):
        value = whole[g + 1] + tile_mul(entering[g + 1], coefs[3])
        off = [(lax.shift_right_logical(b, g + 1) & 1) for b in bits]
        entering[g] = jnp.where(jnp.where(second, off[1], off[0]) == 1, 0.0, value)
    enter = jnp.stack(entering)
    out = []
    factor = enter
    for p in range(7, -1, -1):
        out.append(inner[p] + factor)
        factor = step(factor, coefs[0])
    return jnp.stack(out[::-1], axis=1).reshape(N, 8, 128)


def kernel_last(io, carries):
    me = lax.axis_index("seq")
    core, chip = me % 2, me // 2
    lams = lam_tiles(io.ref("log_rate"), io.ref("angle"))
    pows = [[conj(p) for p in powers(lams[half][2], 10)] for half in range(HALVES)]
    coefs = [tile_lam([p[7 + i] for p in pows]) for i in range(4)]
    parts = io.ref("parts")
    own = parts[:, :, 1024:1152].astype(F32)
    other = parts[:, :, 1152:1280].astype(F32)
    first = jnp.stack([jnp.where(core == 0, own, other), jnp.where(core == 0, other, own)], axis=1).reshape(N, 8, 128)
    enter = all_carries(first, io.ref("lengths"), coefs)
    carries[...] = enter
    mine = carries[me]
    reach = []
    for half in range(HALVES):
        _, table = scan_tables(pows[half], True)
        tiles = [table]
        for _ in range(GROUPS - 1):
            tiles.append(cmul(tiles[-1], pows[half][3]))
        reach.append((jnp.concatenate([t[0] for t in tiles[::-1]], axis=0), jnp.concatenate([t[1] for t in tiles[::-1]], axis=0)))
    scale_row = jnp.concatenate([lams[half][3][0:1, :] for half in (0, 0, 1, 1)], axis=1)
    rows = []
    for micro in range(MICRO):
        cols = []
        for half in range(HALVES):
            nr = tile_row(mine, 0, micro, half)[0:1, :]
            ni = tile_row(mine, 1, micro, half)[0:1, :]
            lr, li = reach[half]
            cols += [lr * nr - li * ni, lr * ni + li * nr]
        rows.append(jnp.concatenate(cols, axis=1))
    dproj = jnp.concatenate(rows, axis=0) * scale_row
    dproj = permute(dproj.astype(BF16), io.get("deal_back")).astype(BF16)
    dnormed = dot_nt(dproj, io.get("b")) + io.get("dnormed")
    xhat, rstd = layer_norm(io.get("x").astype(F32))
    dx = dnormed * io.get("gain")
    m1 = jnp.mean(dx, axis=1, keepdims=True)
    m2 = jnp.mean(dx * xhat, axis=1, keepdims=True)
    io.put("in_grad", (io.get("go").astype(F32) + rstd * (dx - m1 - xhat * m2)).astype(BF16))
    ends = io.ref("ends")
    reach_cols = jnp.concatenate([reach[0][0], reach[0][1], reach[1][0], reach[1][1]], axis=1)
    moved = dot(ends[:, 1].reshape(N * 8, 128), reach_cols.astype(BF16))
    low = rows_iota((N, 8, 128)) < 4
    spread = lambda comp, half: jnp.where(low, enter[:, comp * 4 + half : comp * 4 + half + 1, :], enter[:, comp * 4 + 2 + half : comp * 4 + 3 + half, :])
    cols = []
    for half in range(HALVES):
        c = 256 * half
        mr = moved[:, c : c + 128].reshape(N, 8, 128)
        mi = moved[:, c + 128 : c + 256].reshape(N, 8, 128)
        nr, ni = spread(0, half), spread(1, half)
        cols += [jnp.sum(mr * nr - mi * ni, axis=0), jnp.sum(mr * ni + mi * nr, axis=0)]
    rows8 = jnp.concatenate(cols, axis=1)
    rows8 = rows8 + pltpu.roll(rows8, 4, 0)
    enter_sum = jnp.sum(enter, axis=0)
    cols = []
    for half in range(HALVES):
        pick = lambda comp: enter_sum[comp * 4 + half : comp * 4 + half + 1, :] + enter_sum[comp * 4 + 2 + half : comp * 4 + 3 + half, :]
        nr, ni = pick(0), pick(1)
        lr, li = column_sum(reach[half][0]), column_sum(reach[half][1])
        cols += [lr * nr - li * ni, lr * ni + li * nr]
    sums_row = jnp.concatenate(cols, axis=1)
    low512 = rows_iota((8, 512)) < 4
    both = jnp.where(low512, rows8, sums_row) * scale_row
    back = io.get("deal_back").astype(F32)
    exact = functools.partial(jnp.dot, preferred_element_type=F32, precision=lax.Precision.HIGHEST)
    both = jnp.concatenate([exact(both[:, :256], back), exact(both[:, 256:], back)], axis=1)
    moved_x, moved_one = both, jnp.broadcast_to(both[4:5, :], (8, 512))
    feature = lax.broadcasted_iota(jnp.int32, (8, 512), 1)
    here = feature == 4 * me + rows_iota((8, 512)) % 4
    at_row = lambda name: jnp.sum(jnp.where(here, io.get(name), 0.0), axis=1, keepdims=True)
    gain_f, bias_f = at_row("gain"), at_row("bias")
    b_rows = io.ref("b_tiles")[chip].astype(F32)
    b_rows = jnp.where(core == 0, b_rows, pltpu.roll(b_rows, 4, 0))
    gain_carry = jnp.sum(b_rows * moved_x, axis=1, keepdims=True)
    bias_carry = jnp.sum(b_rows * moved_one, axis=1, keepdims=True)
    summed = jnp.sum(parts[:, :, 0:1024].astype(F32), axis=0)
    io.put("glu_grad", summed[0:4, :])
    io.put("c_grad", summed[4:8, 0:512])
    io.put("b_grad", summed[4:8, 512:1024] + (gain_f * moved_x + bias_f * moved_one)[0:4, :])
    small = parts[:, :, 1280:1408].astype(F32)
    small = small + pltpu.roll(small, 64, 2)
    hsel, lane0 = me // 64, (2 * me) % 128
    pick = jnp.where(
        lax.broadcasted_iota(jnp.int32, (128, 128), 0) == lane0 + lax.broadcasted_iota(jnp.int32, (128, 128), 1) % 2, 1.0, 0.0
    )
    picked = exact(enter.reshape(N * 8, 128), pick).reshape(N, 8, 128)
    lane = lax.broadcasted_iota(jnp.int32, (8, 128), 1)
    which = ((lane // 2) % 2) * 4 + ((lane // 4) % 2) * 2 + hsel
    picked = jnp.sum(jnp.where(which == rows_iota(), picked, 0.0), axis=1, keepdims=True).reshape(CHIPS, 2, 1, 128)
    own = jnp.where(core == 0, picked[:, 0], picked[:, 1])
    other = jnp.where(core == 0, picked[:, 1], picked[:, 0])
    picked = jnp.where(rows_iota((CHIPS, 8, 128)) < 4, own, other)
    fold = lambda v: v[0:1, :] + v[4:5, :]
    sums = fold(jnp.sum(small, axis=0))
    same = fold(jnp.sum(picked * small, axis=0))
    cross_re = fold(jnp.sum(pltpu.roll(picked, 126, 2) * small, axis=0))
    cross_im = fold(jnp.sum(pltpu.roll(picked, 2, 2) * small, axis=0))
    shift = lambda v, by: pltpu.roll(v, 128 - by, 1)
    d_re = shift(same, 16) + shift(same, 18) + shift(same, 20) + shift(same, 22)
    d_im = shift(cross_re, 16) + shift(cross_re, 20) - shift(cross_im, 18) - shift(cross_im, 22)
    e = ends[:, 0].astype(F32)
    straight = jnp.sum(enter * e, axis=0)
    crossed = jnp.sum(enter * pltpu.roll(e, 4, 1), axis=0)
    folded = lambda t, at, half: t[at + half : at + half + 1, :] + t[at + 2 + half : at + 3 + half, :]
    stacked = []
    for half in range(HALVES):
        u, r, lam, scale = lams[half]
        z_re = folded(straight, 0, half) + folded(straight, 4, half)
        z_im = folded(crossed, 4, half) - folded(crossed, 0, half)
        d_scale = (lam[0][0:1] * z_re + lam[1][0:1] * z_im) / scale[0:1]
        one = jnp.zeros((1, 128), F32)
        stacked.append(jnp.concatenate([u[0:1], r[0:1], lam[0][0:1], lam[1][0:1], scale[0:1], d_scale, one, one], axis=0))
    local = exact(jnp.where(hsel == 0, stacked[0], stacked[1]), pick)
    rate, turn = chain_rule([local[i : i + 1, :] for i in range(5)], d_re, d_im, local[5:6, :])
    diagonal = lax.broadcasted_iota(jnp.int32, (8, 128), 1) == rows_iota()
    to_lanes = lambda v: column_sum(jnp.where(diagonal, v, 0.0))
    io.put("gain_grad", (sums + to_lanes(gain_carry))[:, 0:4])
    io.put("bias_grad", (shift(sums, 4) + to_lanes(bias_carry))[:, 0:4])
    io.put("skip_grad", shift(sums, 8)[:, 0:4])
    io.put("rate_grad", (shift(sums, 12) + rate)[:, 0:2])
    io.put("angle_grad", (shift(sums, 14) + turn)[:, 0:2])


def body(block_in, out_grad, lengths, ln_gain, ln_bias, b_proj, c_proj, glu_weight, skip_gain, log_rate, angle):
    rows = MICRO * TOK
    x = block_in.reshape(rows, 512)
    go = out_grad.reshape(rows, 512)
    gain, bias, skip = (v.reshape(1, 512) for v in (ln_gain, ln_bias, skip_gain))
    rate2, angle2 = log_rate.reshape(2, 128), angle.reshape(2, 128)
    spread = deal()
    deal_m = jnp.asarray(spread, BF16)
    back_m = jnp.asarray(spread.T.copy(), BF16)
    full = (rows, 512)
    params = [("log_rate", rate2, "hbm"), ("angle", angle2, "hbm")]
    normed, pairs, local, ends = call(
        kernel_first,
        [("x", x, "hbm"), ("gain", gain, "hbm"), ("bias", bias, "hbm"), ("b", b_proj, "hbm"), ("deal", deal_m, "hbm")] + params,
        [("normed", full, BF16, "vmem"), ("pairs", full, BF16, "vmem"), ("local", full, F32, "vmem"), ("ends", (N, 2, 8, 128), BF16, "vmem")],
        flops=300_000_000, nbytes=3_000_000,
    )
    ends = lax.all_to_all(ends, "seq", split_axis=0, concat_axis=0, tiled=True)
    held = (CHIPS, 8, 1280)
    out, dnormed, keep, send = call(
        kernel_middle,
        [("lengths", lengths, "smem"), ("ends", ends, "vmem"), ("local", local, "vmem"), ("normed", normed, "vmem"), ("pairs", pairs, "vmem")]
        + params
        + [("deal_back", back_m, "hbm"), ("c", c_proj, "hbm"), ("skip", skip, "hbm"), ("glu", glu_weight, "hbm"), ("go", go, "hbm")]
        + [("x", x, "hbm"), ("deal", deal_m, "hbm"), ("b", b_proj, "hbm")],
        [("out", full, BF16, "hbm"), ("dnormed", full, F32, "vmem"), ("keep", held, BF16, "vmem"), ("send", held, BF16, "vmem")],
        flops=1_600_000_000, nbytes=6_000_000,
    )
    got = lax.ppermute(send, "seq", [(i, i ^ 1) for i in range(N)])
    (packed,) = call(
        kernel_pack, [("keep", keep, "vmem"), ("got", got, "vmem")], [("packed", (CHIPS, 8, 1408), BF16, "vmem")], flops=1_000_000, nbytes=2_400_000
    )
    same_core = [[2 * t + core for t in range(CHIPS)] for core in range(2)]
    parts = lax.all_to_all(packed, "seq", split_axis=0, concat_axis=0, tiled=True, axis_index_groups=same_core)
    in_grad, b_grad, c_grad, glu_grad, gain_grad, bias_grad, skip_grad, rate_grad, angle_grad = call(
        kernel_last,
        [("lengths", lengths, "smem"), ("ends", ends, "vmem"), ("parts", parts, "vmem"), ("dnormed", dnormed, "vmem")]
        + params
        + [("deal_back", back_m, "hbm"), ("b", b_proj, "hbm"), ("x", x, "hbm"), ("gain", gain, "hbm"), ("go", go, "hbm"), ("bias", bias, "hbm")]
        + [("b_tiles", b_proj.reshape(CHIPS, 8, 512), "hbm")],
        [("in_grad", full, BF16, "hbm"), ("b_grad", (4, 512), F32, "auto"), ("c_grad", (4, 512), F32, "auto"), ("glu_grad", (4, 1024), F32, "auto")]
        + [(name, (1, w), F32, "auto") for name, w in (("gain_grad", 4), ("bias_grad", 4), ("skip_grad", 4), ("rate_grad", 2), ("angle_grad", 2))],
        extra=[pltpu.VMEM((N, 8, 128), F32)], flops=600_000_000, nbytes=5_000_000,
    )
    return (
        out.reshape(block_in.shape),
        in_grad.reshape(block_in.shape),
        gain_grad.reshape(4),
        bias_grad.reshape(4),
        b_grad,
        c_grad,
        glu_grad,
        skip_grad.reshape(4),
        rate_grad.reshape(2),
        angle_grad.reshape(2),
    )


def solution(mesh):
    tokens = P(None, "seq", None)
    in_specs = (tokens, tokens) + (P(),) * 9
    out_specs = (tokens, tokens, P("seq"), P("seq"), P("seq", None), P("seq", None), P("seq", None), P("seq"), P("seq"), P("seq"))
    return jax.shard_map(body, mesh=mesh, in_specs=in_specs, out_specs=out_specs, check_vma=False)
```

```python
import functools

import jax
import jax.numpy as jnp
import numpy as np
from jax import lax
from jax.experimental import pallas as pl
from jax.experimental.pallas import tpu as pltpu
from jax.sharding import PartitionSpec as P

F32 = jnp.float32
BF16 = jnp.bfloat16
VMEM_LIMIT = 40 * 1024 * 1024
TOK = 128
GROUPS = TOK // 8
MICRO = 2
HALVES = 2
N = 128
CHIPS = 64


def deal():
    out = np.zeros((256, 256), np.float32)
    for n in range(128):
        out[2 * n, n] = 1.0
        out[2 * n + 1, 128 + n] = 1.0
    return out


def dot(a, b):
    return jnp.dot(a, b, preferred_element_type=F32)


def dot_tn(a, b):
    return lax.dot_general(a, b, (((0,), (0,)), ((), ())), preferred_element_type=F32)


def dot_nt(a, b):
    return lax.dot_general(a, b, (((1,), (1,)), ((), ())), preferred_element_type=F32)


def cmul(a, b):
    return (a[0] * b[0] - a[1] * b[1], a[0] * b[1] + a[1] * b[0])


def conj(a):
    return (a[0], -a[1])


def rows_iota(shape=(8, 128)):
    return lax.broadcasted_iota(jnp.int32, shape, len(shape) - 2)


def params(log_rate, angle):
    u = jnp.exp(log_rate)
    r = jnp.exp(-u)
    lam = (r * jnp.cos(angle), r * jnp.sin(angle))
    w = 2.0 * u
    small = jnp.minimum(w, 0.5)
    poly = 1.0 - small * (1.0 / 11.0)
    for k in range(10, 1, -1):
        poly = 1.0 - small * (1.0 / k) * poly
    gap = jnp.where(w < 0.5, small * poly, 1.0 - jnp.exp(-w))
    scale = jnp.sqrt(gap)
    return u, r, lam, scale


def powers(lam, count):
    out = [lam]
    for _ in range(count):
        out.append(cmul(out[-1], out[-1]))
    return out


def spread_rows(pair, half):
    return tuple(jnp.broadcast_to(v[half : half + 1, :], (8, 128)) for v in pair)


def scan_tables(pows, reverse):
    row = rows_iota()
    pos = (7 - row) if reverse else row
    levels = []
    for s, p in ((1, pows[0]), (2, pows[1]), (4, pows[2])):
        keep = pos >= s
        levels.append((s, (jnp.where(keep, p[0], 0.0), jnp.where(keep, p[1], 0.0))))
    e = pos + 1
    table = (jnp.ones((8, 128), F32), jnp.zeros((8, 128), F32))
    for bit in range(4):
        on = (lax.shift_right_logical(e, bit) & 1) == 1
        table = cmul(table, (jnp.where(on, pows[bit][0], 1.0), jnp.where(on, pows[bit][1], 0.0)))
    return levels, table


def group_scan(x, levels, reverse):
    xr, xi = x
    for s, (mr, mi) in levels:
        shift = 8 - s if reverse else s
        rr = pltpu.roll(xr, shift, 1)
        ri = pltpu.roll(xi, shift, 1)
        xr, xi = xr + (mr * rr - mi * ri), xi + (mr * ri + mi * rr)
    return xr, xi


def tile_rows(parts):
    rows = []
    for comp in range(2):
        for micro in range(MICRO):
            for half in range(HALVES):
                rows.append(parts[(micro, half)][comp])
    return jnp.concatenate(rows, axis=0)


def tile_lam(p):
    row = rows_iota()
    odd = (row & 1) == 1
    re = jnp.where(odd, p[1][0], p[0][0])
    im = jnp.where(odd, p[1][1], p[0][1])
    return re, jnp.where(row < 4, -im, im)


def tile_mul(c, coef):
    return c * coef[0] + pltpu.roll(c, 4, 0) * coef[1]


def gather_carry(ends_ref, me, dmax, coef, coef8):
    chains = []
    for chain in range(8):
        acc = jnp.zeros((8, 128), F32)
        for i in range(7, -1, -1):
            d = chain * 8 + i
            e = ends_ref[jnp.maximum(me - 1 - d, 0), 0].astype(F32)
            e = jnp.where(d <= dmax, e, 0.0)
            acc = e if i == 7 else tile_mul(acc, coef) + e
        chains.append(acc)
    out = chains[7]
    for chain in range(6, -1, -1):
        out = tile_mul(out, coef8) + chains[chain]
    return out


def segment_tiles(lengths_ref, me):
    second = (rows_iota() & 2) == 2
    base = me * TOK
    ahead, bits = [], []
    for micro in range(MICRO):
        first, mask, at = jnp.int32(0), jnp.int32(0), jnp.int32(0)
        for slot in range(16):
            first = jnp.where(at <= base, jnp.maximum(first, at), first)
            unit = lax.shift_left(jnp.int32(1), jnp.minimum(at // (8 * TOK), 15))
            mask = jnp.where(at < N * TOK, mask | unit, mask)
            at = at + lengths_ref[micro, slot]
        ahead.append((base - first) // TOK - 1)
        bits.append(mask)
    pick = lambda two: jnp.where(second, two[1], two[0]).astype(F32)
    return pick(ahead), [pick([1 - (lax.shift_right_logical(b, g + 1) & 1) for b in bits]) for g in range(15)]


def groups_of(value, micro_groups=MICRO * GROUPS):
    return value.reshape(micro_groups, 8, 128)


def split_channels(value):
    out = []
    for half in range(HALVES):
        c = 256 * half
        out.append((groups_of(value[:, c : c + 128]), groups_of(value[:, c + 128 : c + 256])))
    return out


def join_channels(halves):
    cols = []
    for re, im in halves:
        cols.append(re.reshape(MICRO * TOK, 128))
        cols.append(im.reshape(MICRO * TOK, 128))
    return jnp.concatenate(cols, axis=1)


def permute(value_bf, matrix):
    return jnp.concatenate([dot(value_bf[:, :256], matrix), dot(value_bf[:, 256:], matrix)], axis=1)


def layer_norm(x):
    mean = jnp.mean(x, axis=1, keepdims=True)
    centered = x - mean
    var = jnp.mean(centered * centered, axis=1, keepdims=True)
    rstd = lax.rsqrt(var + 1e-05)
    return centered * rstd, rstd


def chain_from(x, micro, step8, init, reverse):
    before = {}
    v = init
    order = range(GROUPS - 1, -1, -1) if reverse else range(GROUPS)
    for g in order:
        before[g] = v
        xr, xi = x[0][micro * GROUPS + g], x[1][micro * GROUPS + g]
        if v is None:
            v = (xr, xi)
        else:
            m = cmul(v, step8)
            v = (xr + m[0], xi + m[1])
    return before, v


def edge_bcast(pair, edge):
    return tuple(jnp.broadcast_to(p[edge : edge + 1, :], (8, 128)) for p in pair)


class Ports:
    def __init__(self, ins, outs, refs):
        n_in, n_out = len(ins), len(outs)
        scratch = list(refs[n_in + n_out :])
        out_refs = {name: ref for (name, _, _, _), ref in zip(outs, refs[n_in:])}
        self.refs, self.pending, self.leaving, self.out_copies = {}, {}, [], {}
        sems = scratch.pop() if scratch else None
        i = 0
        for (name, _, mode), ref in zip(ins, refs):
            self.refs[name] = ref
            if mode == "any":
                self.sem = sems.at[i]
                i += 1
            if mode in ("hbm", "smem", "load"):
                target = out_refs[name] if mode == "load" else scratch.pop(0)
                self.pending[name] = pltpu.make_async_copy(ref, target, sems.at[i])
                self.pending[name].start()
                self.refs[name] = target
                i += 1
        for name, _, _, mode in outs:
            if name not in self.refs:
                self.refs[name] = out_refs[name]
            if mode == "hbm":
                self.refs[name] = scratch.pop(0)
                self.out_copies[name] = pltpu.make_async_copy(self.refs[name], out_refs[name], sems.at[i])
                i += 1

    def ref(self, name):
        if name in self.pending:
            self.pending.pop(name).wait()
        return self.refs[name]

    def get(self, name):
        return self.ref(name)[...]

    def put(self, name, value):
        self.refs[name][...] = value
        if name in self.out_copies:
            self.out_copies[name].start()
            self.leaving.append(name)

    def finish(self):
        for name in list(self.pending):
            self.ref(name)
        for name in self.leaving:
            self.out_copies[name].wait()


def call(kernel, ins, outs, extra=(), flops=0, nbytes=0):
    outs = list(outs) + [(name, array.shape, array.dtype, "vmem") for name, array, mode in ins if mode == "load"]

    def run(*refs):
        n_extra = len(extra)
        ports = Ports(ins, outs, refs[: len(refs) - n_extra])
        kernel(ports, *refs[len(refs) - n_extra :])
        ports.finish()

    args, scratch, copies = [], [], 0
    for _, array, mode in ins:
        args.append(pltpu.with_memory_space_constraint(array, pltpu.VMEM if mode == "vmem" else pltpu.HBM))
        copies += mode != "vmem"
        if mode in ("hbm", "smem"):
            scratch.append((pltpu.VMEM if mode == "hbm" else pltpu.SMEM)(array.shape, array.dtype))
    for _, shape, kind, mode in outs:
        if mode == "hbm":
            scratch.append(pltpu.VMEM(shape, kind))
            copies += 1
    if copies:
        scratch.append(pltpu.SemaphoreType.DMA((copies,)))
    out = pl.pallas_call(
        run,
        out_shape=[pltpu.VMEM(s, d) if mode == "vmem" else jax.ShapeDtypeStruct(s, d) for _, s, d, mode in outs],
        in_specs=[pl.BlockSpec(memory_space=pltpu.VMEM if mode == "vmem" else pl.ANY) for _, _, mode in ins],
        out_specs=[pl.BlockSpec(memory_space=pltpu.VMEM if mode == "vmem" else pl.ANY) for _, _, _, mode in outs],
        scratch_shapes=scratch + list(extra),
        compiler_params=pltpu.CompilerParams(vmem_limit_bytes=VMEM_LIMIT),
        cost_estimate=pl.CostEstimate(flops=flops, bytes_accessed=nbytes, transcendentals=0),
    )(*args)
    return {name: array for (name, _, _, _), array in zip(outs, out)}


def chunk_rows(left, right):
    w = left.shape[1]
    a = left.reshape(CHIPS, 8, w)
    b = right.reshape(CHIPS, 8, w)
    low = rows_iota((CHIPS, 8, w)) < 4
    return jnp.where(low, a, pltpu.roll(b, 4, 1)), jnp.where(low, pltpu.roll(a, 4, 1), b)


PER_HALF = ["ahead_r", "ahead_i", "back_r", "back_i", "l1_r", "l1_i", "l2_r", "l2_i", "l4_r", "l4_i", "step_r", "step_i", "scale", "u", "r", "lam_r", "lam_i"]
TABLES = {}
for half in range(HALVES):
    for name in PER_HALF:
        TABLES[name, half] = len(TABLES)
for name in ["coef_r", "coef_i", "coef8_r", "coef8_i", "devices_ahead"]:
    TABLES[name] = len(TABLES)
for group in range(15):
    TABLES["joined", group] = len(TABLES)


def pair_of(tables, name, half):
    return tables[TABLES[name + "_r", half]], tables[TABLES[name + "_i", half]]


def coefs_of(tables, name, forward):
    ci = tables[TABLES[name + "_i"]]
    return tables[TABLES[name + "_r"]], (ci if forward else -ci)


def kernel_first(io):
    me = lax.axis_index("seq")
    tables = io.refs["tables"]
    x = io.get("x").astype(F32)
    xhat, rstd = layer_norm(x)
    normed = (xhat * io.get("gain") + io.get("bias")).astype(BF16)
    io.put("normed", normed)
    io.put("xhat", xhat)
    io.put("rstd", jnp.broadcast_to(rstd, (MICRO * TOK, 128)))
    u, r, lam, scale = params(io.get("log_rate"), io.get("angle"))
    pows = powers(lam, 10)
    proj = dot(normed, io.get("b")).astype(BF16)
    pairs = permute(proj, io.get("deal"))
    io.put("pairs", pairs.astype(BF16))
    halves = split_channels(pairs)
    parts, scanned = {}, []
    for half in range(HALVES):
        mine = [spread_rows(p, half) for p in pows[:4]]
        (scale8,) = spread_rows((scale,), half)
        levels, table = scan_tables(mine, False)
        re, im = halves[half]
        x8 = group_scan((re * scale8, im * scale8), levels, False)
        scanned.append(x8)
        for micro in range(MICRO):
            _, v = chain_from(x8, micro, mine[3], None, False)
            parts[(micro, half)] = (v[0][7:8, :], v[1][7:8, :])
        back_levels, back_table = scan_tables([conj(p) for p in mine], True)
        u8, r8 = spread_rows((u, r), half)
        values = list(table) + list(back_table) + [v for _, level in back_levels for v in level] + list(mine[3])
        values += [scale8, u8, r8] + list(mine[0])
        for name, value in zip(PER_HALF, values):
            tables[TABLES[name, half]] = value
    ends = io.refs["ends"]
    ends[:, 0] = jnp.broadcast_to(tile_rows(parts).astype(BF16)[None], (N, 8, 128))
    even, odd = chunk_rows(xhat[:TOK].T, xhat[TOK:].T)
    ends[:, 1] = jnp.stack([even, odd], axis=1).reshape(N, 8, 128).astype(BF16)
    io.put("local", join_channels(scanned))
    for name, at in (("coef", 7), ("coef8", 10)):
        tables[TABLES[name + "_r"]], tables[TABLES[name + "_i"]] = tile_lam([spread_rows(pows[at], half) for half in range(HALVES)])
    ahead, joined = segment_tiles(io.ref("lengths"), me)
    tables[TABLES["devices_ahead"]] = ahead
    for group in range(15):
        tables[TABLES["joined", group]] = joined[group]
    copy = pltpu.make_async_copy(io.ref("b_tiles").at[me // 2], io.refs["b_rows"], io.sem)
    copy.start()
    copy.wait()


def tile_row(tile, comp, micro, half):
    at = comp * 4 + micro * 2 + half
    return jnp.broadcast_to(tile[at : at + 1, :], (8, 128))


def total(v):
    return jnp.sum(jnp.sum(v, axis=0), axis=0, keepdims=True)


def column_sum(v):
    return jnp.sum(v, axis=0, keepdims=True)


def two_parts(rows):
    high = [v.astype(BF16).astype(F32) for v in rows]
    rest = [v - h for v, h in zip(rows, high)]
    pad = jnp.zeros((16 - 2 * len(rows), rows[0].shape[1]), F32)
    return jnp.concatenate(high + rest + [pad], axis=0).astype(BF16)


def place_smalls(fours, twos):
    out = jnp.zeros((N, 128), F32)
    for rows, each, base in ((fours, 4, 0), (twos, 2, 16)):
        width = rows[0].shape[1]
        block = two_parts(rows)
        at = lax.broadcasted_iota(jnp.int32, (N, width), 0)
        device = 2 * (at % CHIPS) + at // CHIPS
        feature = lax.broadcasted_iota(jnp.int32, (N, width), 1)
        for j in range(each):
            chosen = jnp.where(feature == each * device + j, 1.0, 0.0).astype(BF16)
            above = 32 * j + base
            spread = [block, jnp.zeros((112 - above, width), BF16)] if above < 112 else [block]
            if above:
                spread = [jnp.zeros((above, width), BF16)] + spread
            out = out + dot_nt(chosen, jnp.concatenate(spread, axis=0))
    return out


def chain_rule(rows, d_re, d_im, d_scale):
    u, r, lr, li, scale = rows
    return u * (r * r * d_scale / scale - (lr * d_re + li * d_im)), lr * d_im - li * d_re


def kernel_middle(io):
    me = lax.axis_index("seq")
    core = me % 2
    tables = io.refs["tables"]
    coef, coef8 = coefs_of(tables, "coef", True), coefs_of(tables, "coef8", True)
    carry = gather_carry(io.refs["ends"], me, tables[TABLES["devices_ahead"]], coef, coef8)
    local = split_channels(io.get("local"))
    row = rows_iota((MICRO * GROUPS, 8, 128))
    states, priors, heads = [], [], {}
    for half in range(HALVES):
        table, step8 = pair_of(tables, "ahead", half), pair_of(tables, "step", half)
        x8 = local[half]
        before_r, before_i = [], []
        for micro in range(MICRO):
            init = (tile_row(carry, 0, micro, half), tile_row(carry, 1, micro, half))
            before, _ = chain_from(x8, micro, step8, init, False)
            for g in range(GROUPS):
                edge = edge_bcast(before[g], 7)
                before_r.append(edge[0])
                before_i.append(edge[1])
        br, bi = jnp.stack(before_r), jnp.stack(before_i)
        hr = x8[0] + (table[0] * br - table[1] * bi)
        hi = x8[1] + (table[0] * bi + table[1] * br)
        states.append((hr, hi))
        priors.append((jnp.where(row == 0, br, pltpu.roll(hr, 1, 1)), jnp.where(row == 0, bi, pltpu.roll(hi, 1, 1))))
    hidden = permute(join_channels(states).astype(BF16), io.get("deal_back")).astype(BF16)
    normed = io.get("normed")
    y = dot(hidden, io.get("c")) + io.get("skip") * normed.astype(F32)
    k0, k1 = 0.7978845608028654, 0.044715
    yy = y * y
    t = jnp.tanh(k0 * (y + k1 * (yy * y)))
    act = (0.5 * y * (1.0 + t)).astype(BF16)
    slope = 0.5 * (1.0 + t) + 0.5 * y * (1.0 - t * t) * (k0 * (1.0 + 3.0 * k1 * yy))
    gated = dot(act, io.get("glu"))
    value, gate = gated[:, :512], gated[:, 512:]
    sig = jax.nn.sigmoid(gate)
    go = io.get("go").astype(F32)
    io.put("out", (io.get("x").astype(F32) + value * sig).astype(BF16))
    gs = go * sig
    dgated = jnp.concatenate([gs, gs * value * (1.0 - sig)], axis=1).astype(BF16)
    dy = (dot_nt(dgated, io.get("glu")) * slope).astype(BF16)
    dhidden = dot_nt(dy, io.get("c")).astype(BF16)
    q = split_channels(permute(dhidden, io.get("deal")))
    pairs = split_channels(io.get("pairs").astype(F32))
    parts, projs, rates, angles = {}, [], [], []
    for half in range(HALVES):
        table, step8 = pair_of(tables, "back", half), conj(pair_of(tables, "step", half))
        scale = tables[TABLES["scale", half]]
        levels = [(s, pair_of(tables, "l%d" % s, half)) for s in (1, 2, 4)]
        x8 = group_scan(q[half], levels, True)
        after_r, after_i = [], []
        for micro in range(MICRO):
            zero = (jnp.zeros((8, 128), F32), jnp.zeros((8, 128), F32))
            after, v = chain_from(x8, micro, step8, zero, True)
            parts[(micro, half)] = (v[0][0:1, :], v[1][0:1, :])
            for g in range(GROUPS):
                edge = edge_bcast(after[g], 0)
                after_r.append(edge[0])
                after_i.append(edge[1])
        ar, ai = jnp.stack(after_r), jnp.stack(after_i)
        gr = x8[0] + (table[0] * ar - table[1] * ai)
        gi = x8[1] + (table[0] * ai + table[1] * ar)
        pr, pi = priors[half]
        d_re = total(gr * pr + gi * pi)
        d_im = total(gi * pr - gr * pi)
        d_scale = total(gr * pairs[half][0] + gi * pairs[half][1])
        rows = [tables[TABLES[name, half]][0:1, :] for name in ("u", "r", "lam_r", "lam_i", "scale")]
        rate, turn = chain_rule(rows, d_re, d_im, d_scale)
        rates.append(rate)
        angles.append(turn)
        projs.append((gr * scale, gi * scale))
        for micro in range(MICRO):
            _, v = chain_from(priors[half], micro, conj(step8), None, False)
            m = cmul(v, conj(table))
            heads[(micro, half)] = (column_sum(m[0]), column_sum(m[1]))
    dproj = permute(join_channels(projs).astype(BF16), io.get("deal_back")).astype(BF16)
    dyf = dy.astype(F32)
    dnormed = dot_nt(dproj, io.get("b")) + io.get("skip") * dyf
    io.put("dnormed", dnormed)
    fours = [column_sum(dnormed * io.get("xhat")), column_sum(dnormed), column_sum(dyf * normed.astype(F32))]
    join = lambda two: jnp.concatenate(two, axis=1)
    twos = [join(rates), join(angles)]
    for micro in range(MICRO):
        for comp in range(2):
            twos.append(join([heads[(micro, half)][comp] for half in range(HALVES)]))
    smalls = place_smalls(fours, twos)
    first = tile_rows(parts)
    keep, send = io.refs["keep"], io.refs["send"]
    low = rows_iota((CHIPS, 8, 128)) < 4
    chip = lax.broadcasted_iota(jnp.int32, (CHIPS, 8, 128), 0)
    for ref, flip in ((keep, 0), (send, 1)):
        small = jnp.where((core + flip) % 2 == 0, smalls[:CHIPS], smalls[CHIPS:])[:, None, :]
        ref[:, :, 1024:1152] = jnp.where(low, small, jnp.where(chip == 0, pltpu.roll(first, 4, 0), first)).astype(BF16)
    glu_grad = dot_tn(act, dgated)
    c_grad = dot_tn(hidden, dy)
    b_grad = dot_tn(normed, dproj)
    even, odd = chunk_rows(glu_grad, jnp.concatenate([c_grad, b_grad], axis=1))
    keep[:, :, 0:1024] = jnp.where(core == 0, even, odd).astype(BF16)
    send[:, :, 0:1024] = jnp.where(core == 0, odd, even).astype(BF16)


def kernel_pack(io):
    keep, got, out = io.refs["keep"], io.refs["got"], io.refs["packed"]
    out[:, :, 0:1024] = (keep[:, :, 0:1024].astype(F32) + got[:, :, 0:1024].astype(F32)).astype(BF16)
    low = rows_iota((CHIPS, 8, 128)) < 4
    own, other = keep[:, :, 1024:1152].astype(F32), got[:, :, 1024:1152].astype(F32)
    for at, tiles in ((1024, own), (1152, other)):
        tile = jnp.where(rows_iota() < 4, pltpu.roll(tiles[0], 4, 0), tiles[1])
        out[:, :, at : at + 128] = jnp.broadcast_to(tile.astype(BF16)[None], (CHIPS, 8, 128))
    out[:, :, 1280:1408] = jnp.where(low, own, pltpu.roll(other, 4, 1)).astype(BF16)


def all_carries(first, tables):
    coef, coef8 = coefs_of(tables, "coef", False), coefs_of(tables, "coef8", False)
    groups = first.reshape(16, 8, 8, 128)
    step = lambda c: c * coef[0] + pltpu.roll(c, 4, 1) * coef[1]
    inner = [None] * 8
    inner[7] = jnp.zeros((16, 8, 128), F32)
    for p in range(6, -1, -1):
        inner[p] = groups[:, p + 1] + step(inner[p + 1])
    whole = groups[:, 0] + step(inner[0])
    entering = [None] * 16
    entering[15] = jnp.zeros((8, 128), F32)
    for g in range(14, -1, -1):
        entering[g] = (whole[g + 1] + tile_mul(entering[g + 1], coef8)) * tables[TABLES["joined", g]]
    factor = jnp.stack(entering)
    out = []
    for p in range(7, -1, -1):
        out.append(inner[p] + factor)
        factor = step(factor)
    return jnp.stack(out[::-1], axis=1).reshape(N, 8, 128)


def kernel_last(io, carries):
    me = lax.axis_index("seq")
    core = me % 2
    tables = io.refs["tables"]
    parts = io.refs["parts"]
    own = parts[:, :, 1024:1152].astype(F32)
    other = parts[:, :, 1152:1280].astype(F32)
    first = jnp.stack([jnp.where(core == 0, own, other), jnp.where(core == 0, other, own)], axis=1).reshape(N, 8, 128)
    enter = all_carries(first, tables)
    carries[...] = enter
    mine = carries[me]
    reach = []
    for half in range(HALVES):
        step8 = conj(pair_of(tables, "step", half))
        tiles = [pair_of(tables, "back", half)]
        for _ in range(GROUPS - 1):
            tiles.append(cmul(tiles[-1], step8))
        reach.append(tuple(jnp.concatenate([t[comp] for t in tiles[::-1]], axis=0) for comp in range(2)))
    scale_row = jnp.concatenate([tables[TABLES["scale", half]][0:1, :] for half in (0, 0, 1, 1)], axis=1)
    rows = []
    for micro in range(MICRO):
        cols = []
        for half in range(HALVES):
            nr, ni = tile_row(mine, 0, micro, half)[0:1, :], tile_row(mine, 1, micro, half)[0:1, :]
            lr, li = reach[half]
            cols += [lr * nr - li * ni, lr * ni + li * nr]
        rows.append(jnp.concatenate(cols, axis=1))
    dproj = jnp.concatenate(rows, axis=0) * scale_row
    dproj = permute(dproj.astype(BF16), io.get("deal_back")).astype(BF16)
    dnormed = dot_nt(dproj, io.get("b")) + io.get("dnormed")
    xhat, rstd = io.get("xhat"), io.get("rstd")[:, 0:1]
    dx = dnormed * io.get("gain")
    m1 = jnp.mean(dx, axis=1, keepdims=True)
    m2 = jnp.mean(dx * xhat, axis=1, keepdims=True)
    io.put("in_grad", (io.get("go").astype(F32) + rstd * (dx - m1 - xhat * m2)).astype(BF16))
    summed = jnp.sum(parts[:, :, 0:1024].astype(F32), axis=0)
    io.put("glu_grad", summed[0:4, :])
    io.put("c_grad", summed[4:8, 0:512])
    ends = io.refs["ends"]
    reach_cols = jnp.concatenate([reach[0][0], reach[0][1], reach[1][0], reach[1][1]], axis=1)
    moved = dot(ends[:, 1].reshape(N * 8, 128), reach_cols.astype(BF16))
    low = rows_iota((N, 8, 128)) < 4
    spread = lambda comp, half: jnp.where(low, enter[:, comp * 4 + half : comp * 4 + half + 1, :], enter[:, comp * 4 + 2 + half : comp * 4 + 3 + half, :])
    cols = []
    for half in range(HALVES):
        c = 256 * half
        mr = moved[:, c : c + 128].reshape(N, 8, 128)
        mi = moved[:, c + 128 : c + 256].reshape(N, 8, 128)
        nr, ni = spread(0, half), spread(1, half)
        cols += [jnp.sum(mr * nr - mi * ni, axis=0), jnp.sum(mr * ni + mi * nr, axis=0)]
    rows8 = jnp.concatenate(cols, axis=1)
    rows8 = rows8 + pltpu.roll(rows8, 4, 0)
    enter_sum = jnp.sum(enter, axis=0)
    cols = []
    for half in range(HALVES):
        fold2 = lambda comp: enter_sum[comp * 4 + half : comp * 4 + half + 1, :] + enter_sum[comp * 4 + 2 + half : comp * 4 + 3 + half, :]
        nr, ni = fold2(0), fold2(1)
        lr, li = column_sum(reach[half][0]), column_sum(reach[half][1])
        cols += [lr * nr - li * ni, lr * ni + li * nr]
    sums_row = jnp.concatenate(cols, axis=1)
    low512 = rows_iota((8, 512)) < 4
    both = jnp.where(low512, rows8, sums_row) * scale_row
    back = io.get("deal_back").astype(F32)
    exact = functools.partial(jnp.dot, preferred_element_type=F32, precision=lax.Precision.HIGHEST)
    both = jnp.concatenate([exact(both[:, :256], back), exact(both[:, 256:], back)], axis=1)
    moved_x, moved_one = both, jnp.broadcast_to(both[4:5, :], (8, 512))
    feature = lax.broadcasted_iota(jnp.int32, (8, 512), 1)
    here = feature == 4 * me + rows_iota((8, 512)) % 4
    at_row = lambda name: jnp.sum(jnp.where(here, io.get(name), 0.0), axis=1, keepdims=True)
    gain_f, bias_f = at_row("gain"), at_row("bias")
    io.put("b_grad", summed[4:8, 512:1024] + (gain_f * moved_x + bias_f * moved_one)[0:4, :])
    b_rows = io.get("b_rows").astype(F32)
    b_rows = jnp.where(core == 0, b_rows, pltpu.roll(b_rows, 4, 0))
    gain_carry = jnp.sum(b_rows * moved_x, axis=1, keepdims=True)
    bias_carry = jnp.sum(b_rows * moved_one, axis=1, keepdims=True)
    hsel, lane0 = me // 64, (2 * me) % 128
    lane = lax.broadcasted_iota(jnp.int32, (128, 128), 0)
    col = lax.broadcasted_iota(jnp.int32, (128, 128), 1)
    pick = jnp.where(lane == lane0 + col // 32, 1.0, 0.0).astype(BF16)
    flat = enter.reshape(N * 8, 128)
    high = flat.astype(BF16)
    picked = dot(high, pick) + dot((flat - high.astype(F32)).astype(BF16), pick)
    picked = picked.reshape(CHIPS, 2, 8, 128)
    small = parts[:, :, 1280:1408].astype(F32)
    mine_n = jnp.where(core == 0, picked[:, 0], picked[:, 1])
    other_n = jnp.where(core == 0, picked[:, 1], picked[:, 0])
    products = jnp.sum(mine_n * small[:, 0:1, :] + other_n * small[:, 4:5, :], axis=0)
    sums = jnp.sum(small, axis=0)
    sums = sums[0:1, :] + sums[4:5, :]
    lane8 = lax.broadcasted_iota(jnp.int32, (8, 128), 1)
    w = lane8 % 32 - 16
    comp, micro = w & 1, (w % 6) // 2 - 1
    valid = (w >= 0) & (w < 12) & (micro >= 0) & (lane8 < 64)
    source = lambda c: valid & (rows_iota() == c * 4 + micro * 2 + hsel)
    same = column_sum(jnp.where(source(comp), products, 0.0))
    cross = column_sum(jnp.where(source(1 - comp), jnp.where(comp == 0, products, -products), 0.0))
    v, j = lane % 32, lane // 32
    w = v - 16
    spot = jnp.where(v < 6, 4 * (v % 3) + j, -1)
    spot = jnp.where((w >= 0) & (w < 12) & (j < 2), jnp.where(w % 6 < 2, 12 + 2 * (w % 6) + j, 16 + j), spot)
    gathered = exact(jnp.concatenate([sums, same, cross, jnp.zeros((5, 128), F32)], axis=0), jnp.where(spot == col, 1.0, 0.0))
    e = ends[:, 0].astype(F32)
    straight = jnp.sum(enter * e, axis=0)
    crossed = jnp.sum(enter * pltpu.roll(e, 4, 1), axis=0)
    folded = lambda t, at, half: t[at + half : at + half + 1, :] + t[at + 2 + half : at + 3 + half, :]
    stacked = []
    for half in range(HALVES):
        u, r, lr, li, scale = [tables[TABLES[name, half]][0:1, :] for name in ("u", "r", "lam_r", "lam_i", "scale")]
        z_re = folded(straight, 0, half) + folded(straight, 4, half)
        z_im = folded(crossed, 4, half) - folded(crossed, 0, half)
        d_scale = (lr * z_re + li * z_im) / scale
        stacked.append(jnp.concatenate([u, r, lr, li, scale, d_scale, jnp.zeros((2, 128), F32)], axis=0))
    local = exact(jnp.where(hsel == 0, stacked[0], stacked[1]), jnp.where(lane == lane0 + col % 2, 1.0, 0.0))
    rate, turn = chain_rule([local[i : i + 1, :] for i in range(5)], gathered[1:2, :], gathered[2:3, :], local[5:6, :])
    shift = lambda v, by: pltpu.roll(v, 128 - by, 1)
    diagonal = lane8 == rows_iota()
    to_lanes = lambda v: column_sum(jnp.where(diagonal, v, 0.0))
    sums = gathered[0:1, :]
    io.put("gain_grad", (sums + to_lanes(gain_carry))[:, 0:4])
    io.put("bias_grad", (shift(sums, 4) + to_lanes(bias_carry))[:, 0:4])
    io.put("skip_grad", shift(sums, 8)[:, 0:4])
    io.put("rate_grad", (shift(sums, 12) + shift(rate, 16))[:, 0:2])
    io.put("angle_grad", (shift(sums, 14) + shift(turn, 16))[:, 0:2])


def body(block_in, out_grad, lengths, ln_gain, ln_bias, b_proj, c_proj, glu_weight, skip_gain, log_rate, angle):
    rows = MICRO * TOK
    x = block_in.reshape(rows, 512)
    go = out_grad.reshape(rows, 512)
    gain, bias, skip = (v.reshape(1, 512) for v in (ln_gain, ln_bias, skip_gain))
    rate2, angle2 = log_rate.reshape(2, 128), angle.reshape(2, 128)
    spread = deal()
    deal_m = jnp.asarray(spread, BF16)
    back_m = jnp.asarray(spread.T.copy(), BF16)
    full = (rows, 512)
    k1 = call(
        kernel_first,
        [("x", x, "load"), ("b", b_proj, "load"), ("deal", deal_m, "load"), ("gain", gain, "load"), ("bias", bias, "load")]
        + [("log_rate", rate2, "hbm"), ("angle", angle2, "hbm"), ("lengths", lengths, "smem"), ("deal_back", back_m, "load")]
        + [("c", c_proj, "load"), ("skip", skip, "load"), ("glu", glu_weight, "load"), ("go", go, "load")]
        + [("b_tiles", b_proj.reshape(CHIPS, 8, 512), "any")],
        [("normed", full, BF16, "vmem"), ("xhat", full, F32, "vmem"), ("rstd", (rows, 128), F32, "vmem"), ("pairs", full, BF16, "vmem")]
        + [("local", full, F32, "vmem"), ("ends", (N, 2, 8, 128), BF16, "vmem"), ("tables", (len(TABLES), 8, 128), F32, "vmem")]
        + [("b_rows", (8, 512), BF16, "vmem")],
        flops=300_000_000, nbytes=3_000_000,
    )
    k1["ends"] = lax.all_to_all(k1["ends"], "seq", split_axis=0, concat_axis=0, tiled=True)
    use = lambda group, *names: [(name, group[name], "vmem") for name in names]
    held = (CHIPS, 8, 1152)
    k2 = call(
        kernel_middle,
        use(k1, "ends", "tables", "local", "normed", "xhat", "pairs", "deal", "deal_back", "c", "skip", "glu", "go", "x", "b"),
        [("out", full, BF16, "hbm"), ("dnormed", full, F32, "vmem"), ("keep", held, BF16, "vmem"), ("send", held, BF16, "vmem")],
        flops=1_600_000_000, nbytes=6_000_000,
    )
    got = lax.ppermute(k2["send"], "seq", [(i, i ^ 1) for i in range(N)])
    packed = call(
        kernel_pack, use(k2, "keep") + [("got", got, "vmem")], [("packed", (CHIPS, 8, 1408), BF16, "vmem")], flops=1_000_000, nbytes=2_400_000
    )["packed"]
    same_core = [[2 * t + core for t in range(CHIPS)] for core in range(2)]
    parts = lax.all_to_all(packed, "seq", split_axis=0, concat_axis=0, tiled=True, axis_index_groups=same_core)
    k3 = call(
        kernel_last,
        [("parts", parts, "vmem")] + use(k2, "dnormed") + use(k1, "ends", "tables", "deal_back", "b", "xhat", "rstd", "gain", "bias", "go", "b_rows"),
        [("in_grad", full, BF16, "hbm"), ("b_grad", (4, 512), F32, "hbm"), ("c_grad", (4, 512), F32, "hbm"), ("glu_grad", (4, 1024), F32, "hbm")]
        + [(name, (1, w), F32, "hbm") for name, w in (("gain_grad", 4), ("bias_grad", 4), ("skip_grad", 4), ("rate_grad", 2), ("angle_grad", 2))],
        extra=[pltpu.VMEM((N, 8, 128), F32)], flops=600_000_000, nbytes=5_000_000,
    )
    return (
        k2["out"].reshape(block_in.shape),
        k3["in_grad"].reshape(block_in.shape),
        k3["gain_grad"].reshape(4),
        k3["bias_grad"].reshape(4),
        k3["b_grad"],
        k3["c_grad"],
        k3["glu_grad"],
        k3["skip_grad"].reshape(4),
        k3["rate_grad"].reshape(2),
        k3["angle_grad"].reshape(2),
    )


def solution(mesh):
    tokens = P(None, "seq", None)
    in_specs = (tokens, tokens) + (P(),) * 9
    out_specs = (tokens, tokens, P("seq"), P("seq"), P("seq", None), P("seq", None), P("seq", None), P("seq"), P("seq"), P("seq"))
    return jax.shard_map(body, mesh=mesh, in_specs=in_specs, out_specs=out_specs, check_vma=False)
```

```python
import functools

import jax
import jax.numpy as jnp
import numpy as np
from jax import lax
from jax.experimental import pallas as pl
from jax.experimental.pallas import tpu as pltpu
from jax.sharding import PartitionSpec as P

F32 = jnp.float32
BF16 = jnp.bfloat16
VMEM_LIMIT = 40 * 1024 * 1024
TOK = 128
GROUPS = TOK // 8
MICRO = 2
HALVES = 2
N = 128
CHIPS = 64


def deal():
    out = np.zeros((256, 256), np.float32)
    for n in range(128):
        out[2 * n, n] = 1.0
        out[2 * n + 1, 128 + n] = 1.0
    return out


def dot(a, b):
    return jnp.dot(a, b, preferred_element_type=F32)


def dot_tn(a, b):
    return lax.dot_general(a, b, (((0,), (0,)), ((), ())), preferred_element_type=F32)


def dot_nt(a, b):
    return lax.dot_general(a, b, (((1,), (1,)), ((), ())), preferred_element_type=F32)


def cmul(a, b):
    return (a[0] * b[0] - a[1] * b[1], a[0] * b[1] + a[1] * b[0])


def conj(a):
    return (a[0], -a[1])


def rows_iota(shape=(8, 128)):
    return lax.broadcasted_iota(jnp.int32, shape, len(shape) - 2)


def rest(w):
    small = jnp.minimum(w, 0.5)
    poly = 1.0 - small * (1.0 / 11.0)
    for k in range(10, 1, -1):
        poly = 1.0 - small * (1.0 / k) * poly
    return jnp.where(w < 0.5, small * poly, 1.0 - jnp.exp(-w))


def params(log_rate, angle):
    u = jnp.exp(log_rate)
    r = jnp.where(u < 0.5, 1.0 - rest(u), jnp.exp(-u))
    lam = (r * jnp.cos(angle), r * jnp.sin(angle))
    return u, r, lam, jnp.sqrt(rest(2.0 * u))


def powers(lam, count):
    out = [lam]
    for _ in range(count):
        out.append(cmul(out[-1], out[-1]))
    return out


def spread_rows(pair, half):
    return tuple(jnp.broadcast_to(v[half : half + 1, :], (8, 128)) for v in pair)


def scan_tables(pows, reverse):
    row = rows_iota()
    pos = (7 - row) if reverse else row
    levels = []
    for s, p in ((1, pows[0]), (2, pows[1]), (4, pows[2])):
        keep = pos >= s
        levels.append((s, (jnp.where(keep, p[0], 0.0), jnp.where(keep, p[1], 0.0))))
    e = pos + 1
    table = (jnp.ones((8, 128), F32), jnp.zeros((8, 128), F32))
    for bit in range(4):
        on = (lax.shift_right_logical(e, bit) & 1) == 1
        table = cmul(table, (jnp.where(on, pows[bit][0], 1.0), jnp.where(on, pows[bit][1], 0.0)))
    return levels, table


def group_scan(x, levels, reverse):
    xr, xi = x
    for s, (mr, mi) in levels:
        shift = 8 - s if reverse else s
        rr = pltpu.roll(xr, shift, 1)
        ri = pltpu.roll(xi, shift, 1)
        xr, xi = xr + (mr * rr - mi * ri), xi + (mr * ri + mi * rr)
    return xr, xi


def tile_rows(parts):
    rows = []
    for comp in range(2):
        for micro in range(MICRO):
            for half in range(HALVES):
                rows.append(parts[(micro, half)][comp])
    return jnp.concatenate(rows, axis=0)


def tile_lam(p):
    row = rows_iota()
    odd = (row & 1) == 1
    re = jnp.where(odd, p[1][0], p[0][0])
    im = jnp.where(odd, p[1][1], p[0][1])
    return re, jnp.where(row < 4, -im, im)


def tile_mul(c, coef):
    return c * coef[0] + pltpu.roll(c, 4, 0) * coef[1]


def gather_carry(ends_ref, chip, dmax, coef, coef8):
    chains = []
    for chain in range(4):
        acc = None
        for i in range(7, -1, -1):
            d = chain * 8 + i
            at = jnp.maximum(chip - 1 - d, 0)
            e = ends_ref[at, 0].astype(F32) + ends_ref[at, 1].astype(F32)
            e = jnp.where(d <= dmax, e, 0.0)
            acc = e if acc is None else tile_mul(acc, coef) + e
        chains.append(acc)
    out = chains[3]
    for chain in range(2, -1, -1):
        out = tile_mul(out, coef8) + chains[chain]
    return out


def segment_tile(lengths_ref, chip):
    second = (rows_iota() & 2) == 2
    base = chip * 2 * TOK
    ahead = []
    for micro in range(MICRO):
        first, at = jnp.int32(0), jnp.int32(0)
        for slot in range(16):
            first = jnp.where(at <= base, jnp.maximum(first, at), first)
            at = at + lengths_ref[micro, slot]
        ahead.append((base - first) // (2 * TOK) - 1)
    return jnp.where(second, ahead[1], ahead[0]).astype(F32)


def groups_of(value, micro_groups=MICRO * GROUPS):
    return value.reshape(micro_groups, 8, 128)


def split_channels(value):
    out = []
    for half in range(HALVES):
        c = 256 * half
        out.append((groups_of(value[:, c : c + 128]), groups_of(value[:, c + 128 : c + 256])))
    return out


def join_channels(halves):
    cols = []
    for re, im in halves:
        cols.append(re.reshape(MICRO * TOK, 128))
        cols.append(im.reshape(MICRO * TOK, 128))
    return jnp.concatenate(cols, axis=1)


def permute(value_bf, matrix):
    return jnp.concatenate([dot(value_bf[:, :256], matrix), dot(value_bf[:, 256:], matrix)], axis=1)


def layer_norm(x):
    mean = jnp.mean(x, axis=1, keepdims=True)
    centered = x - mean
    var = jnp.mean(centered * centered, axis=1, keepdims=True)
    rstd = lax.rsqrt(var + 1e-05)
    return centered * rstd, rstd


def chain_from(x, micro, step8, init, reverse):
    before = {}
    v = init
    order = range(GROUPS - 1, -1, -1) if reverse else range(GROUPS)
    for g in order:
        before[g] = v
        xr, xi = x[0][micro * GROUPS + g], x[1][micro * GROUPS + g]
        if v is None:
            v = (xr, xi)
        else:
            m = cmul(v, step8)
            v = (xr + m[0], xi + m[1])
    return before, v


def edge_bcast(pair, edge):
    return tuple(jnp.broadcast_to(p[edge : edge + 1, :], (8, 128)) for p in pair)


HELD, LOAD, COPY, SCALARS, PLAIN = range(5)


class Bag:
    pass


class Ports:
    def __init__(self, ins, outs, refs):
        n_in, n_out = len(ins), len(outs)
        scratch = list(refs[n_in + n_out :])
        out_refs = {name: ref for (name, _, _, _), ref in zip(outs, refs[n_in:])}
        table, self.pending, self.leaving, self.out_copies = {}, {}, [], {}
        sems = scratch.pop() if scratch else None
        i = 0
        for (name, _, mode), ref in zip(ins, refs):
            table[name] = ref
            if mode == PLAIN:
                self.spare = sems.at[i]
                i += 1
            elif mode != HELD:
                target = out_refs[name] if mode == LOAD else scratch.pop(0)
                self.pending[name] = pltpu.make_async_copy(ref, target, sems.at[i])
                self.pending[name].start()
                table[name] = target
                i += 1
        for name, _, _, mode in outs:
            table.setdefault(name, out_refs[name])
            if mode == COPY:
                table[name] = scratch.pop(0)
                self.out_copies[name] = pltpu.make_async_copy(table[name], out_refs[name], sems.at[i])
                i += 1
        self.table = table
        self.refs = Bag()
        self.refs.__dict__.update(table)

    def __getattr__(self, name):
        if name in self.pending:
            self.pending.pop(name).wait()
        return self.table[name][...]

    def ready(self, **names):
        (name,) = names
        if name in self.pending:
            self.pending.pop(name).wait()
        return self.table[name]

    def settle(self, count):
        for name in list(self.pending)[:count]:
            self.pending.pop(name).wait()

    def put(self, **values):
        for name, value in values.items():
            self.table[name][...] = value
            if name in self.out_copies:
                self.out_copies[name].start()
                self.leaving.append(name)

    def finish(self):
        for copy in self.pending.values():
            copy.wait()
        for name in self.leaving:
            self.out_copies[name].wait()


def call(kernel, ins, outs, extra=(), flops=0, nbytes=0):
    ins = [(name, array, mode) for mode, group in ins for name, array in group.items()]
    outs = [(name, shape, kind, mode) for mode, group in outs for name, (shape, kind) in group.items()]
    outs += [(name, array.shape, array.dtype, HELD) for name, array, mode in ins if mode == LOAD]

    def run(*refs):
        n_extra = len(extra)
        ports = Ports(ins, outs, refs[: len(refs) - n_extra])
        kernel(ports, *refs[len(refs) - n_extra :])
        ports.finish()

    args, scratch, copies = [], [], 0
    for _, array, mode in ins:
        args.append(pltpu.with_memory_space_constraint(array, pltpu.VMEM if mode == HELD else pltpu.HBM))
        copies += mode != HELD
        if mode in (COPY, SCALARS):
            scratch.append((pltpu.VMEM if mode == COPY else pltpu.SMEM)(array.shape, array.dtype))
    for _, shape, kind, mode in outs:
        if mode == COPY:
            scratch.append(pltpu.VMEM(shape, kind))
            copies += 1
    if copies:
        scratch.append(pltpu.SemaphoreType.DMA((copies,)))
    spec = lambda mode: pl.BlockSpec(memory_space=pltpu.VMEM if mode == HELD else pl.ANY)
    out = pl.pallas_call(
        run,
        out_shape=[pltpu.VMEM(s, d) if mode == HELD else jax.ShapeDtypeStruct(s, d) for _, s, d, mode in outs],
        in_specs=[spec(mode) for _, _, mode in ins],
        out_specs=[spec(mode) for _, _, _, mode in outs],
        scratch_shapes=scratch + list(extra),
        compiler_params=pltpu.CompilerParams(vmem_limit_bytes=VMEM_LIMIT),
        cost_estimate=pl.CostEstimate(flops=flops, bytes_accessed=nbytes, transcendentals=0),
    )(*args)
    made = Bag()
    made.__dict__.update({name: array for (name, _, _, _), array in zip(outs, out)})
    return made


def chunk_rows(left, right):
    w = left.shape[1]
    a = left.reshape(CHIPS, 8, w)
    b = right.reshape(CHIPS, 8, w)
    low = rows_iota((CHIPS, 8, w)) < 4
    return jnp.where(low, a, pltpu.roll(b, 4, 1)), jnp.where(low, pltpu.roll(a, 4, 1), b)


AHEAD, BACK, LEVEL, STEP, LAM, SCALE, RATE_U, RADIUS, PER_HALF = 0, 2, 4, 10, 12, 14, 15, 16, 17
COEF, COEF2, COEF8, COEF16, CHIPS_AHEAD, TABLES = 34, 36, 38, 40, 42, 43


def pair_of(tables, at, half):
    return tables[half * PER_HALF + at], tables[half * PER_HALF + at + 1]


def rows_of(tables, half):
    return [tables[half * PER_HALF + at][0:1, :] for at in (RATE_U, RADIUS, LAM, LAM + 1, SCALE)]


def coefs_of(tables, at, forward):
    ci = tables[at + 1]
    return tables[at], (ci if forward else -ci)


def kernel_first(io):
    me = lax.axis_index("seq")
    copy = pltpu.make_async_copy(io.refs.b_tiles.at[me // 2], io.refs.b_rows, io.spare)
    copy.start()
    io.settle(8)
    tables = io.refs.tables
    x = io.x.astype(F32)
    xhat, rstd = layer_norm(x)
    normed = (xhat * io.gain + io.bias).astype(BF16)
    io.put(normed=normed)
    io.put(xhat=xhat)
    io.put(rstd=jnp.broadcast_to(rstd, (MICRO * TOK, 128)))
    u, r, lam, scale = params(io.log_rate, io.angle)
    pows = powers(lam, 11)
    proj = dot(normed, io.b).astype(BF16)
    pairs = permute(proj, io.deal)
    io.put(pairs=pairs.astype(BF16))
    halves = split_channels(pairs)
    parts, scanned = {}, []
    for half in range(HALVES):
        mine = [spread_rows(p, half) for p in pows[:4]]
        (scale8,) = spread_rows((scale,), half)
        levels, table = scan_tables(mine, False)
        re, im = halves[half]
        x8 = group_scan((re * scale8, im * scale8), levels, False)
        scanned.append(x8)
        for micro in range(MICRO):
            _, v = chain_from(x8, micro, mine[3], None, False)
            parts[(micro, half)] = (v[0][7:8, :], v[1][7:8, :])
        back_levels, back_table = scan_tables([conj(p) for p in mine], True)
        values = list(table) + list(back_table) + [v for _, level in back_levels for v in level] + list(mine[3]) + list(mine[0])
        for at, value in enumerate(values + [scale8] + list(spread_rows((u, r), half))):
            tables[half * PER_HALF + at] = value
    last = tile_rows(parts)
    io.put(last=last)
    even, odd = chunk_rows(xhat[:TOK].T, xhat[TOK:].T)
    io.put(columns=jnp.where(me % 2 == 0, even, odd).astype(BF16))
    send = io.refs.send
    send[0:CHIPS] = jnp.where(me % 2 == 0, odd, even).astype(BF16)
    for i, part in enumerate(in_parts(last, 2)):
        send[CHIPS + i] = part
    io.put(local=join_channels(scanned))
    for to, at in ((COEF, 7), (COEF2, 8), (COEF8, 10), (COEF16, 11)):
        tables[to], tables[to + 1] = tile_lam([spread_rows(pows[at], half) for half in range(HALVES)])
    tables[CHIPS_AHEAD] = segment_tile(io.ready(lengths=0), me // 2)
    copy.wait()


def kernel_join(io):
    core = lax.axis_index("seq") % 2
    own, got = io.last, io.refs.got
    other = got[CHIPS].astype(F32) + got[CHIPS + 1].astype(F32)
    first, second = jnp.where(core == 0, own, other), jnp.where(core == 0, other, own)
    whole = second + tile_mul(first, coefs_of(io.refs.tables, COEF, True))
    io.put(inside=jnp.where(core == 0, 0.0, other))
    ends = io.refs.ends
    for i, part in enumerate(in_parts(whole, 2)):
        ends[:, i] = jnp.broadcast_to(part[None], (CHIPS, 8, 128))
    ends[:, 2] = io.columns
    ends[:, 3] = got[0:CHIPS]


def tile_row(tile, comp, micro, half):
    at = comp * 4 + micro * 2 + half
    return jnp.broadcast_to(tile[at : at + 1, :], (8, 128))


def total(v):
    return jnp.sum(jnp.sum(v, axis=0), axis=0, keepdims=True)


def column_sum(v):
    return jnp.sum(v, axis=0, keepdims=True)


def in_parts(value, count):
    parts = []
    for _ in range(count):
        parts.append(value.astype(BF16))
        value = value - parts[-1].astype(F32)
    return parts


def choose(value, one_hot):
    out = dot(jnp.concatenate([p.astype(F32) for p in in_parts(value, 3)], axis=0).astype(BF16), one_hot)
    return out[0:8, :] + out[8:16, :] + out[16:24, :]


def one_hots(each, width):
    at = np.arange(N)
    device = 2 * (at % CHIPS) + at // CHIPS
    out = np.zeros((each, N, width), np.float32)
    for j in range(each):
        out[j, at, each * device + j] = 1.0
    return out


def place_smalls(fours, twos, chosen4, chosen2):
    out = jnp.zeros((N, 128), F32)
    for rows, chosen, each in ((fours, chosen4, 4), (twos, chosen2, 2)):
        width = rows[0].shape[1]
        high = [v.astype(BF16).astype(F32) for v in rows]
        block = high + [v - h for v, h in zip(rows, high)]
        block.append(jnp.zeros((-len(block) % 8, width), F32))
        block = jnp.concatenate(block, axis=0).astype(F32)
        for j in range(each):
            above = 64 * (j // 2) + 40 + 8 * (j % 2) if each == 4 else 64 * j
            spread = [jnp.zeros((above, width), F32)] if above else []
            spread += [block, jnp.zeros((128 - above - block.shape[0], width), F32)]
            out = out + dot_nt(chosen[j], jnp.concatenate(spread, axis=0).astype(BF16))
    return out


def chain_rule(rows, d_re, d_im, d_scale):
    u, r, lr, li, scale = rows
    return u * (r * r * d_scale / scale - (lr * d_re + li * d_im)), lr * d_im - li * d_re


def kernel_middle(io):
    me = lax.axis_index("seq")
    core = me % 2
    tables = io.refs.tables
    carry = gather_carry(io.refs.ends, me // 2, tables[CHIPS_AHEAD], coefs_of(tables, COEF2, True), coefs_of(tables, COEF16, True))
    carry = jnp.where(core == 0, carry, io.inside + tile_mul(carry, coefs_of(tables, COEF, True)))
    local = split_channels(io.local)
    row = rows_iota((MICRO * GROUPS, 8, 128))
    states, priors = [], []
    for half in range(HALVES):
        table, step8 = pair_of(tables, AHEAD, half), pair_of(tables, STEP, half)
        x8 = local[half]
        before_r, before_i = [], []
        for micro in range(MICRO):
            init = (tile_row(carry, 0, micro, half), tile_row(carry, 1, micro, half))
            before, _ = chain_from(x8, micro, step8, init, False)
            for g in range(GROUPS):
                edge = edge_bcast(before[g], 7)
                before_r.append(edge[0])
                before_i.append(edge[1])
        br, bi = jnp.stack(before_r), jnp.stack(before_i)
        hr = x8[0] + (table[0] * br - table[1] * bi)
        hi = x8[1] + (table[0] * bi + table[1] * br)
        states.append((hr, hi))
        priors.append((jnp.where(row == 0, br, pltpu.roll(hr, 1, 1)), jnp.where(row == 0, bi, pltpu.roll(hi, 1, 1))))
    hidden = permute(join_channels(states).astype(BF16), io.deal_back).astype(BF16)
    normed = io.normed
    y = dot(hidden, io.c) + io.skip * normed.astype(F32)
    k0, k1 = 0.7978845608028654, 0.044715
    yy = y * y
    t = jnp.tanh(k0 * (y + k1 * (yy * y)))
    act = (0.5 * y * (1.0 + t)).astype(BF16)
    slope = 0.5 * (1.0 + t) + 0.5 * y * (1.0 - t * t) * (k0 * (1.0 + 3.0 * k1 * yy))
    gated = dot(act, io.glu)
    value, gate = gated[:, :512], gated[:, 512:]
    sig = jax.nn.sigmoid(gate)
    go = io.go.astype(F32)
    io.put(out=(io.x.astype(F32) + value * sig).astype(BF16))
    gs = go * sig
    dgated = jnp.concatenate([gs, gs * value * (1.0 - sig)], axis=1).astype(BF16)
    dy = (dot_nt(dgated, io.glu) * slope).astype(BF16)
    dhidden = dot_nt(dy, io.c).astype(BF16)
    q = split_channels(permute(dhidden, io.deal))
    parts, scanned = {}, []
    for half in range(HALVES):
        step8 = conj(pair_of(tables, STEP, half))
        levels = [(1 << n, pair_of(tables, LEVEL + 2 * n, half)) for n in range(3)]
        x8 = group_scan(q[half], levels, True)
        scanned.append(x8)
        for micro in range(MICRO):
            _, v = chain_from(x8, micro, step8, None, True)
            parts[(micro, half)] = (v[0][0:1, :], v[1][0:1, :])
    io.put(first=tile_rows(parts), carry=carry, act=act, dgated=dgated, hidden=hidden, dy=dy, back=join_channels(scanned), prior=join_channels(priors))


def by_core(ref_keep, ref_send, core, even, odd):
    ref_keep[...] = jnp.where(core == 0, even, odd).astype(BF16)
    ref_send[...] = jnp.where(core == 0, odd, even).astype(BF16)


def kernel_products(io):
    core = lax.axis_index("seq") % 2
    glu_grad = dot_tn(io.act, io.dgated)
    c_grad = dot_tn(io.hidden, io.dy)
    even, odd = chunk_rows(glu_grad[:, :768], jnp.concatenate([glu_grad[:, 768:], c_grad], axis=1))
    by_core(io.refs.keep, io.refs.send, core, even, odd)


def kernel_carried(io):
    core = lax.axis_index("seq") % 2
    tables = io.refs.tables
    own, other = io.first, io.other
    first, second = jnp.where(core == 0, own, other), jnp.where(core == 0, other, own)
    whole = first + tile_mul(second, coefs_of(tables, COEF, False))
    io.put(chip_first=whole.astype(BF16))
    inside = jnp.where(core == 0, other, 0.0)
    far_step = [(tables[COEF][half : half + 1, :], tables[COEF + 1][4 + half : 5 + half, :]) for half in range(HALVES)]
    back, priors, pairs = split_channels(io.back), split_channels(io.prior), split_channels(io.pairs.astype(F32))
    projs, rates, angles, heads, tails = [], [], [], {}, {}
    for half in range(HALVES):
        table, step8 = pair_of(tables, BACK, half), conj(pair_of(tables, STEP, half))
        from_start = conj(pair_of(tables, AHEAD, half))
        from_start = [jnp.where(rows_iota() == 0, edge, pltpu.roll(t, 1, 0)) for edge, t in zip((1.0, 0.0), from_start)]
        scale = tables[half * PER_HALF + SCALE]
        x8 = back[half]
        after_r, after_i = [], []
        for micro in range(MICRO):
            init = (tile_row(inside, 0, micro, half), tile_row(inside, 1, micro, half))
            after, _ = chain_from(x8, micro, step8, init, True)
            for g in range(GROUPS):
                edge = edge_bcast(after[g], 0)
                after_r.append(edge[0])
                after_i.append(edge[1])
        ar, ai = jnp.stack(after_r), jnp.stack(after_i)
        gr = x8[0] + (table[0] * ar - table[1] * ai)
        gi = x8[1] + (table[0] * ai + table[1] * ar)
        pr, pi = priors[half]
        d_re = total(gr * pr + gi * pi)
        d_im = total(gi * pr - gr * pi)
        d_scale = total(gr * pairs[half][0] + gi * pairs[half][1])
        for micro in range(MICRO):
            used = tuple(io.carry[4 * comp + 2 * micro + half : 4 * comp + 2 * micro + half + 1, :] for comp in range(2))
            _, v = chain_from((gr, gi), micro, step8, None, True)
            m = cmul(v, from_start)
            tails[(micro, half)] = (column_sum(m[0]), column_sum(m[1]))
            m = cmul(tails[(micro, half)], conj(used))
            d_re, d_im = d_re - m[0], d_im - m[1]
            _, v = chain_from(priors[half], micro, conj(step8), None, False)
            m = cmul(v, conj(table))
            more = cmul(far_step[half], used)
            m = (column_sum(m[0]) - TOK * more[0], column_sum(m[1]) - TOK * more[1])
            far = cmul(m, far_step[half])
            heads[(micro, half)] = tuple(jnp.where(core == 0, f, n) for f, n in zip(far, m))
        rate, turn = chain_rule(rows_of(tables, half), d_re, d_im, d_scale)
        rates.append(rate)
        angles.append(turn)
        projs.append((gr * scale, gi * scale))
    dproj = permute(join_channels(projs).astype(BF16), io.deal_back).astype(BF16)
    dyf, normed = io.dy.astype(F32), io.normed
    dnormed = dot_nt(dproj, io.b) + io.skip * dyf
    io.put(dnormed=dnormed)
    fours = [column_sum(dnormed * io.xhat), column_sum(dnormed), column_sum(dyf * normed.astype(F32))]
    join = lambda two: jnp.concatenate(two, axis=1)
    twos = [join(rates), join(angles)]
    of_tile = lambda tile, at: join([tile[at : at + 1, :], tile[at + 1 : at + 2, :]])
    last = io.last
    for micro in range(MICRO):
        for sums in (tails, heads):
            twos += [join([sums[(micro, half)][comp] for half in range(HALVES)]) for comp in range(2)]
        twos += [of_tile(tile, 4 * comp + 2 * micro) for tile in (last, whole) for comp in range(2)]
    smalls = place_smalls(fours, twos, io.chosen4, io.chosen2)
    b_grad = dot_tn(normed, dproj)
    even, odd = chunk_rows(b_grad[:, :256], b_grad[:, 256:])
    tiles = [jnp.broadcast_to(v[:, None, :], (CHIPS, 8, 128)) for v in (smalls[:CHIPS], smalls[CHIPS:])]
    by_core(io.refs.keep, io.refs.send, core, jnp.concatenate([even, tiles[0]], axis=2), jnp.concatenate([odd, tiles[1]], axis=2))


def kernel_pack(io):
    out = io.refs.packed
    out[:, :, 0:768] = (io.keep.astype(F32) + io.got.astype(F32)).astype(BF16)
    keep, got = io.keep_b.astype(F32), io.got_b.astype(F32)
    out[:, :, 768:1024] = (keep[:, :, 0:256] + got[:, :, 0:256]).astype(BF16)
    out[:, :, 1024:1152] = jnp.broadcast_to(io.chip_first[None], (CHIPS, 8, 128))
    low = rows_iota((CHIPS, 8, 128)) < 4
    out[:, :, 1152:1280] = jnp.where(low, keep[:, :, 256:384], got[:, :, 256:384]).astype(BF16)


def segment_joins(lengths_ref):
    second = (rows_iota() & 2) == 2
    bits = []
    for micro in range(MICRO):
        mask, at = jnp.int32(0), jnp.int32(0)
        for slot in range(16):
            unit = lax.shift_left(jnp.int32(1), jnp.minimum(at // (8 * TOK), 15))
            mask = jnp.where(at < N * TOK, mask | unit, mask)
            at = at + lengths_ref[micro, slot]
        bits.append(mask)
    pick = lambda two: jnp.where(second, two[1], two[0]).astype(F32)
    return [pick([1 - (lax.shift_right_logical(b, g + 1) & 1) for b in bits]) for g in range(15)], bits


def kernel_ahead(io):
    me = lax.axis_index("seq")
    tables = io.refs.tables
    near, far = [], []
    for half in range(HALVES):
        step8 = conj(pair_of(tables, STEP, half))
        tiles = [pair_of(tables, BACK, half)]
        for _ in range(2 * GROUPS - 1):
            tiles.append(cmul(tiles[-1], step8))
        tiles = tiles[::-1]
        for comp in range(2):
            far.append(jnp.concatenate([t[comp] for t in tiles[:GROUPS]], axis=0))
            near.append(jnp.concatenate([t[comp] for t in tiles[GROUPS:]], axis=0))
    near, far = jnp.concatenate(near, axis=1), jnp.concatenate(far, axis=1)
    sums = jnp.concatenate([column_sum(near) + column_sum(far), jnp.zeros((7, 512), F32)], axis=0)
    io.put(reach=near, reach_sum=sums, reach_low=jnp.concatenate([far, near], axis=0).astype(BF16))
    ends = io.refs.ends
    own, other = (ends[:, i].reshape(CHIPS * 8, 128) for i in (2, 3))
    first = me % 2 == 0
    io.put(columns=jnp.concatenate([jnp.where(first, own, other), jnp.where(first, other, own)], axis=1))
    lane = lax.broadcasted_iota(jnp.int32, (128, 128), 0)
    col = lax.broadcasted_iota(jnp.int32, (128, 128), 1)
    w = lane % 64
    hot = lambda where: jnp.where(where, 1.0, 0.0).astype(BF16)
    spot = jnp.where((w >= 40) & (w < 56) & (w % 8 < 6), 4 * (w % 8 % 3) + 2 * (lane // 64) + (w - 40) // 8, -1)
    spot = jnp.where(w < 36, jnp.where(w % 18 < 2, 12 + 2 * (w % 18) + lane // 64, -1), spot)
    channel = (lane // 64) == col % 2
    wanted = lambda k: hot(channel & (w < 36) & (w % 18 == 2 + 8 * ((col // 2) % 2) + k))
    io.put(pick=jnp.concatenate([hot(spot == col)] + [wanted(k) for k in range(8)], axis=1))
    half_rows = [jnp.concatenate(rows_of(tables, half) + [jnp.zeros((3, 128), F32)], axis=0) for half in range(HALVES)]
    mine = choose(jnp.where(me // 64 == 0, half_rows[0], half_rows[1]), hot(lane == (2 * me) % 128 + col % 2))
    io.put(channels=mine)
    pows = powers((mine[2:3, :], mine[3:4, :]), 10)
    io.put(channel_pows=jnp.concatenate([v for at in (7, 8, 10) for v in pows[at]] + [jnp.zeros((2, 128), F32)], axis=0))
    feature = lax.broadcasted_iota(jnp.int32, (8, 512), 1)
    here = feature == 4 * me + rows_iota((8, 512)) % 4
    b_rows = io.b_rows.astype(F32)
    b_rows = jnp.where(me % 2 == 0, b_rows, pltpu.roll(b_rows, 4, 0))
    at_row = lambda v: jnp.broadcast_to(jnp.sum(jnp.where(here, v, 0.0), axis=1, keepdims=True), (8, 512))
    io.put(mine=jnp.concatenate([at_row(io.gain), at_row(io.bias), b_rows], axis=1))
    joins, bits = segment_joins(io.ready(lengths=0))
    for group, tile in enumerate(joins):
        io.refs.joined[group] = tile
    group = lax.broadcasted_iota(jnp.int32, (16, 128), 0)
    second = (lax.broadcasted_iota(jnp.int32, (16, 128), 1) // 2) % 2 == 1
    opens = lax.shift_right_logical(jnp.where(second, bits[1], bits[0]), group) & 1
    io.put(opens=opens.astype(F32))


def all_carries(first, tables, joined):
    coef2, coef8 = (coefs_of(tables, at, False) for at in (COEF2, COEF8))
    groups = first.reshape(16, 4, 8, 128)
    step = lambda c, by: c * by[0] + pltpu.roll(c, 4, 1) * by[1]
    inner = [None] * 4
    inner[3] = jnp.zeros((16, 8, 128), F32)
    for p in range(2, -1, -1):
        inner[p] = groups[:, p + 1] + step(inner[p + 1], coef2)
    whole = groups[:, 0] + step(inner[0], coef2)
    entering = [None] * 16
    entering[15] = jnp.zeros((8, 128), F32)
    for g in range(14, -1, -1):
        entering[g] = (whole[g + 1] + tile_mul(entering[g + 1], coef8)) * joined[g]
    factor = jnp.stack(entering)
    out = []
    for p in range(3, -1, -1):
        out.append(inner[p] + factor)
        factor = step(factor, coef2)
    return jnp.stack(out[::-1], axis=1).reshape(CHIPS, 8, 128)


def kernel_last(io, carries, split):
    me = lax.axis_index("seq")
    core = me % 2
    tables = io.refs.tables
    parts = io.refs.parts
    enter = all_carries(parts[:, :, 1024:1152].astype(F32), tables, io.refs.joined)
    carries[...] = enter
    mine = carries[me // 2]
    mine = jnp.where(core == 0, tile_mul(mine, coefs_of(tables, COEF, False)), mine)
    reach_cols = io.reach
    reach = [(reach_cols[:, c : c + 128], reach_cols[:, c + 128 : c + 256]) for c in (0, 256)]
    scale_row = jnp.concatenate([tables[half * PER_HALF + SCALE][0:1, :] for half in (0, 0, 1, 1)], axis=1)
    rows = []
    for micro in range(MICRO):
        cols = []
        for half in range(HALVES):
            nr, ni = tile_row(mine, 0, micro, half)[0:1, :], tile_row(mine, 1, micro, half)[0:1, :]
            lr, li = reach[half]
            cols += [lr * nr - li * ni, lr * ni + li * nr]
        rows.append(jnp.concatenate(cols, axis=1))
    dproj = jnp.concatenate(rows, axis=0) * scale_row
    dproj = permute(dproj.astype(BF16), io.deal_back).astype(BF16)
    dnormed = dot_nt(dproj, io.b) + io.dnormed
    xhat, rstd = io.xhat, io.rstd[:, 0:1]
    dx = dnormed * io.gain
    m1 = jnp.mean(dx, axis=1, keepdims=True)
    m2 = jnp.mean(dx * xhat, axis=1, keepdims=True)
    io.put(in_grad=(io.go.astype(F32) + rstd * (dx - m1 - xhat * m2)).astype(BF16))
    summed = jnp.sum(parts[:, :, 0:1024].astype(F32), axis=0)
    io.put(glu_grad=jnp.concatenate([summed[0:4, 0:768], summed[4:8, 0:256]], axis=1))
    io.put(c_grad=summed[4:8, 256:768])
    moved = dot(io.columns, io.reach_low)
    low = rows_iota((CHIPS, 8, 128)) < 4
    spread = lambda comp, half: jnp.where(low, enter[:, comp * 4 + half : comp * 4 + half + 1, :], enter[:, comp * 4 + 2 + half : comp * 4 + 3 + half, :])
    cols = []
    for half in range(HALVES):
        c = 256 * half
        mr = moved[:, c : c + 128].reshape(CHIPS, 8, 128)
        mi = moved[:, c + 128 : c + 256].reshape(CHIPS, 8, 128)
        nr, ni = spread(0, half), spread(1, half)
        cols += [jnp.sum(mr * nr - mi * ni, axis=0), jnp.sum(mr * ni + mi * nr, axis=0)]
    rows8 = jnp.concatenate(cols, axis=1)
    rows8 = rows8 + pltpu.roll(rows8, 4, 0)
    enter_sum = jnp.sum(enter, axis=0)
    reach_sum = io.reach_sum[0:1, :]
    cols = []
    for half in range(HALVES):
        c = 256 * half
        fold2 = lambda comp: enter_sum[comp * 4 + half : comp * 4 + half + 1, :] + enter_sum[comp * 4 + 2 + half : comp * 4 + 3 + half, :]
        nr, ni = fold2(0), fold2(1)
        lr, li = reach_sum[:, c : c + 128], reach_sum[:, c + 128 : c + 256]
        cols += [lr * nr - li * ni, lr * ni + li * nr]
    sums_row = jnp.concatenate(cols, axis=1)
    both = jnp.where(rows_iota((8, 512)) < 4, rows8, sums_row) * scale_row
    moved_x = jnp.concatenate([choose(both[:, :256], io.deal_back), choose(both[:, 256:], io.deal_back)], axis=1)
    moved_one = jnp.broadcast_to(moved_x[4:5, :], (8, 512))
    own = io.mine
    gain_f, bias_f, b_rows = own[:, 0:512], own[:, 512:1024], own[:, 1024:1536]
    b_sum = jnp.concatenate([summed[0:4, 768:1024], summed[4:8, 768:1024]], axis=1)
    io.put(b_grad=b_sum + (gain_f * moved_x + bias_f * moved_one)[0:4, :])
    gain_carry = jnp.sum(b_rows * moved_x, axis=1, keepdims=True)
    bias_carry = jnp.sum(b_rows * moved_one, axis=1, keepdims=True)
    small = parts[:, :, 1152:1280]
    own, other = small[:, 0, :].astype(F32), small[:, 4, :].astype(F32)
    sums = column_sum(own + other)
    gathered = choose(jnp.concatenate([sums, jnp.zeros((7, 128), F32)], axis=0), io.pick[:, 0:128])
    d_re, d_im, d_scale = owned_channels(own, other, core, io, split)
    rate, turn = chain_rule([io.channels[i : i + 1, :] for i in range(5)], d_re, d_im, d_scale)
    shift = lambda v, by: pltpu.roll(v, 128 - by, 1)
    diagonal = lax.broadcasted_iota(jnp.int32, (8, 128), 1) == rows_iota()
    to_lanes = lambda v: column_sum(jnp.where(diagonal, v, 0.0))
    sums = gathered[0:1, :]
    io.put(gain_grad=(sums + to_lanes(gain_carry))[:, 0:4])
    io.put(bias_grad=(shift(sums, 4) + to_lanes(bias_carry))[:, 0:4])
    io.put(skip_grad=shift(sums, 8)[:, 0:4])
    io.put(rate_grad=(shift(sums, 12) + rate)[:, 0:2])
    io.put(angle_grad=(shift(sums, 14) + turn)[:, 0:2])


def group_chain(coef, value, opens, reverse):
    row = lax.broadcasted_iota(jnp.int32, (16, 128), 0)
    pos = 15 - row if reverse else row
    moved = lambda v, by: pltpu.roll(v, 16 - by if reverse else by, 0)
    opens = jnp.where(row == 0, 1.0, opens)
    keep = jnp.where(pos == 0, 0.0, 1.0 - (moved(opens, 1) if reverse else opens))
    a = (keep * coef[0], keep * coef[1])
    b = tuple(keep * moved(v, 1) for v in value)
    for by in (1, 2, 4, 8):
        inside = pos >= by
        before = lambda v: jnp.where(inside, moved(v, by), 0.0)
        pb, pa = tuple(before(v) for v in b), tuple(before(v) for v in a)
        m = cmul(a, pb)
        b = (b[0] + m[0], b[1] + m[1])
        a = cmul(a, pa)
    return b


def owned_channels(own, other, core, io, split):
    first, second = jnp.where(core == 0, own, other), jnp.where(core == 0, other, own)
    values = []
    for rows in (first, second):
        values.append(dot(rows.astype(BF16), io.pick[:, 128:1152]))
    pows = [tuple(io.channel_pows[2 * i + comp : 2 * i + comp + 1, :] for comp in range(2)) for i in range(3)]
    step, step2, step8 = pows
    of = lambda q, k: (values[q][:, 128 * k : 128 * k + 128], values[q][:, 128 * k + 128 : 128 * k + 256])
    plus = lambda x, y: (x[0] + y[0], x[1] + y[1])
    last0, last1 = of(0, 4), of(1, 4)
    kept = [*plus(last1, cmul(last0, step)), *of(0, 6), *of(0, 0), *of(1, 0), *plus(of(0, 2), of(1, 2)), *last0]
    for i, v in enumerate(kept):
        split[i] = v
    at = lambda i, p: (split[i, pl.ds(p, 16, stride=4), :], split[i + 1, pl.ds(p, 16, stride=4), :])
    ends, firsts = [at(0, p) for p in range(4)], [at(2, p) for p in range(4)]
    zero = (jnp.zeros((16, 128), F32), jnp.zeros((16, 128), F32))
    states, grads = [zero], [zero]
    for p in range(1, 4):
        states.append(plus(cmul(states[-1], step2), ends[p - 1]))
        grads.append(plus(cmul(grads[-1], conj(step2)), firsts[4 - p]))
    grads = grads[::-1]
    into = group_chain(step8, plus(cmul(states[3], step2), ends[3]), io.opens, False)
    back = group_chain(conj(step8), plus(cmul(grads[0], conj(step2)), firsts[0]), io.opens, True)
    d_lam, d_scale = zero, zero
    for p in range(4):
        states[p] = plus(states[p], into)
        into = cmul(into, step2)
        grads[3 - p] = plus(grads[3 - p], back)
        back = cmul(back, conj(step2))
    for p in range(4):
        h0, n = states[p], grads[p]
        far = cmul(h0, step)
        h1 = plus(far, at(10, p))
        seen = plus(cmul(far, step), cmul(h1, step))
        seen = plus(at(8, p), (TOK * seen[0], TOK * seen[1]))
        for x, y in ((at(4, p), h0), (at(6, p), h1), (n, seen)):
            d_lam = plus(d_lam, cmul(x, conj(y)))
        d_scale = plus(d_scale, cmul(n, conj(ends[p])))
    both = lambda v: (lambda t: t + pltpu.roll(t, 126, 1))(column_sum(v))
    d_re, d_im, s_re, s_im = (both(v) for v in d_lam + d_scale)
    lr, li, scale = (io.channels[i : i + 1, :] for i in (2, 3, 4))
    return d_re, d_im, (lr * s_re + li * s_im) / scale


def body(block_in, out_grad, lengths, ln_gain, ln_bias, b_proj, c_proj, glu_weight, skip_gain, log_rate, angle):
    rows = MICRO * TOK
    x = block_in.reshape(rows, 512)
    go = out_grad.reshape(rows, 512)
    gain, bias, skip = (v.reshape(1, 512) for v in (ln_gain, ln_bias, skip_gain))
    rate2, angle2 = log_rate.reshape(2, 128), angle.reshape(2, 128)
    spread = deal()
    deal_m = jnp.asarray(spread, BF16)
    back_m = jnp.asarray(spread.T.copy(), BF16)
    chosen4, chosen2 = jnp.asarray(one_hots(4, 512), BF16), jnp.asarray(one_hots(2, 256), BF16)
    full = (rows, 512)
    k1 = call(
        kernel_first,
        [
            (LOAD, dict(x=x, b=b_proj, deal=deal_m, gain=gain, bias=bias)),
            (COPY, dict(log_rate=rate2, angle=angle2)),
            (SCALARS, dict(lengths=lengths)),
            (LOAD, dict(deal_back=back_m, c=c_proj, skip=skip, glu=glu_weight, go=go, chosen4=chosen4, chosen2=chosen2)),
            (PLAIN, dict(b_tiles=b_proj.reshape(CHIPS, 8, 512))),
        ],
        [
            (
                HELD,
                dict(
                    normed=(full, BF16), xhat=(full, F32), rstd=((rows, 128), F32), pairs=(full, BF16), local=(full, F32),
                    send=((CHIPS + 2, 8, 128), BF16), columns=((CHIPS, 8, 128), BF16), tables=((TABLES, 8, 128), F32), b_rows=((8, 512), BF16),
                    last=((8, 128), F32),
                ),
            )
        ],
        flops=300_000_000, nbytes=3_000_000,
    )
    swap = functools.partial(lax.ppermute, axis_name="seq", perm=[(i, i ^ 1) for i in range(N)])
    same_core = [[2 * t + core for t in range(CHIPS)] for core in range(2)]
    exchange = functools.partial(lax.all_to_all, axis_name="seq", split_axis=0, concat_axis=0, tiled=True, axis_index_groups=same_core)
    kj = call(
        kernel_join, [(HELD, dict(last=k1.last, got=swap(k1.send), columns=k1.columns, tables=k1.tables))],
        [(HELD, dict(inside=((8, 128), F32), ends=((CHIPS, 4, 8, 128), BF16)))], flops=1_000_000, nbytes=1_000_000,
    )
    ends = exchange(kj.ends)
    k2 = call(
        kernel_middle,
        [
            (HELD, dict(deal_back=k1.deal_back, c=k1.c, skip=k1.skip, glu=k1.glu, go=k1.go)),
            (HELD, dict(ends=ends, inside=kj.inside, tables=k1.tables, local=k1.local, normed=k1.normed, deal=k1.deal, x=k1.x)),
        ],
        [
            (COPY, dict(out=(full, BF16))),
            (
                HELD,
                dict(
                    first=((8, 128), F32), carry=((8, 128), F32), act=(full, BF16), dgated=((rows, 1024), BF16), hidden=(full, BF16), dy=(full, BF16),
                    back=(full, F32), prior=(full, F32),
                ),
            ),
        ],
        flops=1_000_000_000, nbytes=6_000_000,
    )
    other = swap(k2.first)
    wide, narrow = ((CHIPS, 8, 768), BF16), ((CHIPS, 8, 384), BF16)
    kp = call(
        kernel_products, [(HELD, dict(act=k2.act, dgated=k2.dgated, hidden=k2.hidden, dy=k2.dy))], [(HELD, dict(keep=wide, send=wide))],
        flops=2_000_000_000, nbytes=3_000_000,
    )
    got = swap(kp.send)
    kc = call(
        kernel_carried,
        [
            (HELD, dict(carry=k2.carry, last=k1.last)),
            (HELD, dict(first=k2.first, other=other, back=k2.back, prior=k2.prior, dy=k2.dy, tables=k1.tables, pairs=k1.pairs, b=k1.b)),
            (HELD, dict(deal_back=k1.deal_back, normed=k1.normed, xhat=k1.xhat, skip=k1.skip, chosen4=k1.chosen4, chosen2=k1.chosen2)),
        ],
        [(HELD, dict(chip_first=((8, 128), BF16), dnormed=(full, F32), keep=narrow, send=narrow))],
        flops=6_000_000_000, nbytes=3_000_000,
    )
    got_b = swap(kc.send)
    ka = call(
        kernel_ahead,
        [
            (SCALARS, dict(lengths=lengths)),
            (HELD, dict(tables=k1.tables, ends=ends, gain=k1.gain, bias=k1.bias, b_rows=k1.b_rows, dnormed=kc.dnormed)),
        ],
        [
            (
                HELD,
                dict(
                    reach=((TOK, 512), F32), reach_sum=((8, 512), F32), reach_low=((2 * TOK, 512), BF16), columns=((CHIPS * 8, 256), BF16),
                    channels=((8, 128), F32), channel_pows=((8, 128), F32), opens=((16, 128), F32), pick=((128, 1152), BF16), mine=((8, 1536), F32), joined=((15, 8, 128), F32),
                ),
            )
        ],
        flops=200_000_000, nbytes=3_000_000,
    )
    packed = call(
        kernel_pack, [(HELD, dict(keep=kp.keep, got=got, keep_b=kc.keep, got_b=got_b, chip_first=kc.chip_first, reach=ka.reach))],
        [(HELD, dict(packed=((CHIPS, 8, 1280), BF16)))], flops=1_000_000, nbytes=2_400_000,
    ).packed
    parts = exchange(packed)
    four, two = ((1, 4), F32), ((1, 2), F32)
    k3 = call(
        kernel_last,
        [
            (HELD, dict(parts=parts, dnormed=kc.dnormed, go=k1.go, deal_back=k1.deal_back, tables=k1.tables, b=k1.b, xhat=k1.xhat, rstd=k1.rstd)),
            (HELD, dict(gain=k1.gain, reach=ka.reach, reach_sum=ka.reach_sum, reach_low=ka.reach_low, columns=ka.columns)),
            (HELD, dict(channels=ka.channels, channel_pows=ka.channel_pows, opens=ka.opens, pick=ka.pick, mine=ka.mine, joined=ka.joined)),
        ],
        [
            (COPY, dict(in_grad=(full, BF16), b_grad=((4, 512), F32), c_grad=((4, 512), F32), glu_grad=((4, 1024), F32))),
            (COPY, dict(gain_grad=four, bias_grad=four, skip_grad=four, rate_grad=two, angle_grad=two)),
        ],
        extra=[pltpu.VMEM((CHIPS, 8, 128), F32), pltpu.VMEM((12, CHIPS, 128), F32)], flops=600_000_000, nbytes=5_000_000,
    )
    return (
        k2.out.reshape(block_in.shape),
        k3.in_grad.reshape(block_in.shape),
        k3.gain_grad.reshape(4),
        k3.bias_grad.reshape(4),
        k3.b_grad,
        k3.c_grad,
        k3.glu_grad,
        k3.skip_grad.reshape(4),
        k3.rate_grad.reshape(2),
        k3.angle_grad.reshape(2),
    )


def solution(mesh):
    tokens = P(None, "seq", None)
    in_specs = (tokens, tokens) + (P(),) * 9
    out_specs = (tokens, tokens, P("seq"), P("seq"), P("seq", None), P("seq", None), P("seq", None), P("seq"), P("seq"), P("seq"))
    return jax.shard_map(body, mesh=mesh, in_specs=in_specs, out_specs=out_specs, check_vma=False)
```

```python
import functools

import jax
import jax.numpy as jnp
import numpy as np
from jax import lax
from jax.experimental import pallas as pl
from jax.experimental.pallas import tpu as pltpu
from jax.sharding import PartitionSpec as P

F32 = jnp.float32
BF16 = jnp.bfloat16
VMEM_LIMIT = 40 * 1024 * 1024
TOK = 128
GROUPS = TOK // 8
MICRO = 2
HALVES = 2
N = 128
CHIPS = 64


def deal():
    out = np.zeros((256, 256), np.float32)
    for n in range(128):
        out[2 * n, n] = 1.0
        out[2 * n + 1, 128 + n] = 1.0
    return out


def dot(a, b):
    return jnp.dot(a, b, preferred_element_type=F32)


def dot_tn(a, b):
    return lax.dot_general(a, b, (((0,), (0,)), ((), ())), preferred_element_type=F32)


def dot_nt(a, b):
    return lax.dot_general(a, b, (((1,), (1,)), ((), ())), preferred_element_type=F32)


def cmul(a, b):
    return (a[0] * b[0] - a[1] * b[1], a[0] * b[1] + a[1] * b[0])


def conj(a):
    return (a[0], -a[1])


def rows_iota(shape=(8, 128)):
    return lax.broadcasted_iota(jnp.int32, shape, len(shape) - 2)


def rest(w):
    small = jnp.minimum(w, 0.5)
    poly = 1.0 - small * (1.0 / 11.0)
    for k in range(10, 1, -1):
        poly = 1.0 - small * (1.0 / k) * poly
    return jnp.where(w < 0.5, small * poly, 1.0 - jnp.exp(-w))


def params(log_rate, angle):
    u = jnp.exp(log_rate)
    r = jnp.where(u < 0.5, 1.0 - rest(u), jnp.exp(-u))
    lam = (r * jnp.cos(angle), r * jnp.sin(angle))
    return u, r, lam, jnp.sqrt(rest(2.0 * u))


def powers(lam, count):
    out = [lam]
    for _ in range(count):
        out.append(cmul(out[-1], out[-1]))
    return out


def spread_rows(pair, half):
    return tuple(jnp.broadcast_to(v[half : half + 1, :], (8, 128)) for v in pair)


def scan_tables(pows, reverse):
    row = rows_iota()
    pos = (7 - row) if reverse else row
    levels = []
    for s, p in ((1, pows[0]), (2, pows[1]), (4, pows[2])):
        keep = pos >= s
        levels.append((s, (jnp.where(keep, p[0], 0.0), jnp.where(keep, p[1], 0.0))))
    e = pos + 1
    table = (jnp.ones((8, 128), F32), jnp.zeros((8, 128), F32))
    for bit in range(4):
        on = (lax.shift_right_logical(e, bit) & 1) == 1
        table = cmul(table, (jnp.where(on, pows[bit][0], 1.0), jnp.where(on, pows[bit][1], 0.0)))
    return levels, table


def group_scan(x, levels, reverse):
    xr, xi = x
    for s, (mr, mi) in levels:
        shift = 8 - s if reverse else s
        rr = pltpu.roll(xr, shift, 1)
        ri = pltpu.roll(xi, shift, 1)
        xr, xi = xr + (mr * rr - mi * ri), xi + (mr * ri + mi * rr)
    return xr, xi


def tile_rows(parts):
    rows = []
    for comp in range(2):
        for micro in range(MICRO):
            for half in range(HALVES):
                rows.append(parts[(micro, half)][comp])
    return jnp.concatenate(rows, axis=0)


def tile_lam(p):
    row = rows_iota()
    odd = (row & 1) == 1
    re = jnp.where(odd, p[1][0], p[0][0])
    im = jnp.where(odd, p[1][1], p[0][1])
    return re, jnp.where(row < 4, -im, im)


def tile_mul(c, coef):
    return c * coef[0] + pltpu.roll(c, 4, 0) * coef[1]


def gather_carry(ends_ref, chip, dmax, coef, coef8):
    chains = []
    for chain in range(4):
        acc = None
        for i in range(7, -1, -1):
            d = chain * 8 + i
            at = jnp.maximum(chip - 1 - d, 0)
            e = ends_ref[at, 0].astype(F32) + ends_ref[at, 1].astype(F32)
            e = jnp.where(d <= dmax, e, 0.0)
            acc = e if acc is None else tile_mul(acc, coef) + e
        chains.append(acc)
    out = chains[3]
    for chain in range(2, -1, -1):
        out = tile_mul(out, coef8) + chains[chain]
    return out


def segment_tile(lengths_ref, chip):
    second = (rows_iota() & 2) == 2
    base = chip * 2 * TOK
    ahead = []
    for micro in range(MICRO):
        first, at = jnp.int32(0), jnp.int32(0)
        for slot in range(16):
            first = jnp.where(at <= base, jnp.maximum(first, at), first)
            at = at + lengths_ref[micro, slot]
        ahead.append((base - first) // (2 * TOK) - 1)
    return jnp.where(second, ahead[1], ahead[0]).astype(F32)


def groups_of(value, micro_groups=MICRO * GROUPS):
    return value.reshape(micro_groups, 8, 128)


def split_channels(value):
    out = []
    for half in range(HALVES):
        c = 256 * half
        out.append((groups_of(value[:, c : c + 128]), groups_of(value[:, c + 128 : c + 256])))
    return out


def join_channels(halves):
    cols = []
    for re, im in halves:
        cols.append(re.reshape(MICRO * TOK, 128))
        cols.append(im.reshape(MICRO * TOK, 128))
    return jnp.concatenate(cols, axis=1)


def permute(value_bf, matrix):
    return jnp.concatenate([dot(value_bf[:, :256], matrix), dot(value_bf[:, 256:], matrix)], axis=1)


def layer_norm(x):
    mean = jnp.mean(x, axis=1, keepdims=True)
    centered = x - mean
    var = jnp.mean(centered * centered, axis=1, keepdims=True)
    rstd = lax.rsqrt(var + 1e-05)
    return centered * rstd, rstd


def chain_from(x, micro, step8, init, reverse):
    before = {}
    v = init
    order = range(GROUPS - 1, -1, -1) if reverse else range(GROUPS)
    for g in order:
        before[g] = v
        xr, xi = x[0][micro * GROUPS + g], x[1][micro * GROUPS + g]
        if v is None:
            v = (xr, xi)
        else:
            m = cmul(v, step8)
            v = (xr + m[0], xi + m[1])
    return before, v


def edge_bcast(pair, edge):
    return tuple(jnp.broadcast_to(p[edge : edge + 1, :], (8, 128)) for p in pair)


HELD, LOAD, COPY, SCALARS, PLAIN = range(5)


class Bag:
    pass


class Ports:
    def __init__(self, ins, outs, refs):
        n_in, n_out = len(ins), len(outs)
        scratch = list(refs[n_in + n_out :])
        out_refs = {name: ref for (name, _, _, _), ref in zip(outs, refs[n_in:])}
        table, self.pending, self.leaving, self.out_copies = {}, {}, [], {}
        sems = scratch.pop() if scratch else None
        i = 0
        for (name, _, mode), ref in zip(ins, refs):
            table[name] = ref
            if mode == PLAIN:
                self.spare = sems.at[i]
                i += 1
            elif mode != HELD:
                target = out_refs[name] if mode == LOAD else scratch.pop(0)
                self.pending[name] = pltpu.make_async_copy(ref, target, sems.at[i])
                self.pending[name].start()
                table[name] = target
                i += 1
        for name, _, _, mode in outs:
            table.setdefault(name, out_refs[name])
            if mode == COPY:
                table[name] = scratch.pop(0)
                self.out_copies[name] = pltpu.make_async_copy(table[name], out_refs[name], sems.at[i])
                i += 1
        self.table = table
        self.refs = Bag()
        self.refs.__dict__.update(table)

    def __getattr__(self, name):
        if name in self.pending:
            self.pending.pop(name).wait()
        return self.table[name][...]

    def ready(self, **names):
        (name,) = names
        if name in self.pending:
            self.pending.pop(name).wait()
        return self.table[name]

    def settle(self, count):
        for name in list(self.pending)[:count]:
            self.pending.pop(name).wait()

    def put(self, **values):
        for name, value in values.items():
            self.table[name][...] = value
            if name in self.out_copies:
                self.out_copies[name].start()
                self.leaving.append(name)

    def finish(self):
        for copy in self.pending.values():
            copy.wait()
        for name in self.leaving:
            self.out_copies[name].wait()


def call(kernel, ins, outs, extra=(), flops=0, nbytes=0):
    ins = [(name, array, mode) for mode, group in ins for name, array in group.items()]
    outs = [(name, shape, kind, mode) for mode, group in outs for name, (shape, kind) in group.items()]
    outs += [(name, array.shape, array.dtype, HELD) for name, array, mode in ins if mode == LOAD]

    def run(*refs):
        n_extra = len(extra)
        ports = Ports(ins, outs, refs[: len(refs) - n_extra])
        kernel(ports, *refs[len(refs) - n_extra :])
        ports.finish()

    args, scratch, copies = [], [], 0
    for _, array, mode in ins:
        args.append(pltpu.with_memory_space_constraint(array, pltpu.VMEM if mode == HELD else pltpu.HBM))
        copies += mode != HELD
        if mode in (COPY, SCALARS):
            scratch.append((pltpu.VMEM if mode == COPY else pltpu.SMEM)(array.shape, array.dtype))
    for _, shape, kind, mode in outs:
        if mode == COPY:
            scratch.append(pltpu.VMEM(shape, kind))
            copies += 1
    if copies:
        scratch.append(pltpu.SemaphoreType.DMA((copies,)))
    spec = lambda mode: pl.BlockSpec(memory_space=pltpu.VMEM if mode == HELD else pl.ANY)
    out = pl.pallas_call(
        run,
        out_shape=[pltpu.VMEM(s, d) if mode == HELD else jax.ShapeDtypeStruct(s, d) for _, s, d, mode in outs],
        in_specs=[spec(mode) for _, _, mode in ins],
        out_specs=[spec(mode) for _, _, _, mode in outs],
        scratch_shapes=scratch + list(extra),
        compiler_params=pltpu.CompilerParams(vmem_limit_bytes=VMEM_LIMIT),
        cost_estimate=pl.CostEstimate(flops=flops, bytes_accessed=nbytes, transcendentals=0),
    )(*args)
    made = Bag()
    made.__dict__.update({name: array for (name, _, _, _), array in zip(outs, out)})
    return made


def chunk_rows(left, right):
    w = left.shape[1]
    a = left.reshape(CHIPS, 8, w)
    b = right.reshape(CHIPS, 8, w)
    low = rows_iota((CHIPS, 8, w)) < 4
    return jnp.where(low, a, pltpu.roll(b, 4, 1)), jnp.where(low, pltpu.roll(a, 4, 1), b)


AHEAD, BACK, LEVEL, STEP, LAM, SCALE, RATE_U, RADIUS, PER_HALF = 0, 2, 4, 10, 12, 14, 15, 16, 17
COEF, COEF2, COEF8, COEF16, TABLES = 34, 36, 38, 40, 42


def pair_of(tables, at, half):
    return tables[half * PER_HALF + at], tables[half * PER_HALF + at + 1]


def rows_of(tables, half):
    return [tables[half * PER_HALF + at][0:1, :] for at in (RATE_U, RADIUS, LAM, LAM + 1, SCALE)]


def coefs_of(tables, at, forward):
    ci = tables[at + 1]
    return tables[at], (ci if forward else -ci)


def kernel_first(io):
    me = lax.axis_index("seq")
    copy = pltpu.make_async_copy(io.refs.b_tiles.at[me // 2], io.refs.b_rows, io.spare)
    copy.start()
    io.settle(6)
    xhat, _ = layer_norm(io.x.astype(F32))
    normed = (xhat * io.gain + io.bias).astype(BF16)
    _, _, lam, scale = params(io.log_rate, io.angle)
    pows = powers(lam, 3)
    io.settle(2)
    io.put(normed=normed)
    proj = dot(normed, io.b).astype(BF16)
    pairs = permute(proj, io.deal)
    io.put(pairs=pairs.astype(BF16))
    halves = split_channels(pairs)
    parts, scanned = {}, []
    for half in range(HALVES):
        mine = [spread_rows(p, half) for p in pows]
        (scale8,) = spread_rows((scale,), half)
        levels, _ = scan_tables(mine, False)
        re, im = halves[half]
        x8 = group_scan((re * scale8, im * scale8), levels, False)
        scanned.append(x8)
        for micro in range(MICRO):
            _, v = chain_from(x8, micro, mine[3], None, False)
            parts[(micro, half)] = (v[0][7:8, :], v[1][7:8, :])
    last = tile_rows(parts)
    io.put(last=last)
    even, odd = chunk_rows(xhat[:TOK].T, xhat[TOK:].T)
    io.put(columns=jnp.where(me % 2 == 0, even, odd).astype(BF16))
    send = io.refs.send
    send[0:CHIPS] = jnp.where(me % 2 == 0, odd, even).astype(BF16)
    for i, part in enumerate(in_parts(last, 2)):
        send[CHIPS + i] = part
    io.put(local=join_channels(scanned), ahead=segment_tile(io.refs.lengths, me // 2))
    copy.wait()


def kernel_tables(io):
    tables = io.refs.tables
    u, r, lam, scale = params(io.log_rate, io.angle)
    pows = powers(lam, 11)
    for half in range(HALVES):
        mine = [spread_rows(p, half) for p in pows[:4]]
        _, table = scan_tables(mine, False)
        back_levels, back_table = scan_tables([conj(p) for p in mine], True)
        values = list(table) + list(back_table) + [v for _, level in back_levels for v in level] + list(mine[3]) + list(mine[0])
        for at, value in enumerate(values + list(spread_rows((scale, u, r), half))):
            tables[half * PER_HALF + at] = value
    for to, at in ((COEF, 7), (COEF2, 8), (COEF8, 10), (COEF16, 11)):
        tables[to], tables[to + 1] = tile_lam([spread_rows(pows[at], half) for half in range(HALVES)])
    xhat, rstd = layer_norm(io.x.astype(F32))
    io.put(xhat=xhat, rstd=jnp.broadcast_to(rstd, (MICRO * TOK, 128)), b_perm=permute(io.b, io.deal).astype(BF16))


def kernel_join(io):
    core = lax.axis_index("seq") % 2
    own, got = io.last, io.refs.got
    other = got[CHIPS].astype(F32) + got[CHIPS + 1].astype(F32)
    first, second = jnp.where(core == 0, own, other), jnp.where(core == 0, other, own)
    whole = second + tile_mul(first, coefs_of(io.refs.tables, COEF, True))
    io.put(inside=jnp.where(core == 0, 0.0, other))
    ends = io.refs.ends
    for i, part in enumerate(in_parts(whole, 2)):
        ends[:, i] = jnp.broadcast_to(part[None], (CHIPS, 8, 128))
    ends[:, 2] = io.columns
    ends[:, 3] = got[0:CHIPS]


def tile_row(tile, comp, micro, half):
    at = comp * 4 + micro * 2 + half
    return jnp.broadcast_to(tile[at : at + 1, :], (8, 128))


def total(v):
    return jnp.sum(jnp.sum(v, axis=0), axis=0, keepdims=True)


def column_sum(v):
    return jnp.sum(v, axis=0, keepdims=True)


def in_parts(value, count):
    parts = []
    for _ in range(count):
        parts.append(value.astype(BF16))
        value = value - parts[-1].astype(F32)
    return parts


def choose(value, one_hot):
    out = dot(jnp.concatenate([p.astype(F32) for p in in_parts(value, 3)], axis=0).astype(BF16), one_hot)
    return out[0:8, :] + out[8:16, :] + out[16:24, :]


def one_hots(each, width):
    at = np.arange(N)
    device = 2 * (at % CHIPS) + at // CHIPS
    out = np.zeros((each, N, width), np.float32)
    for j in range(each):
        out[j, at, each * device + j] = 1.0
    return out


def place_smalls(fours, twos, chosen4, chosen2):
    out = jnp.zeros((N, 128), F32)
    for rows, chosen, each in ((fours, chosen4, 4), (twos, chosen2, 2)):
        width = rows[0].shape[1]
        high = [v.astype(BF16).astype(F32) for v in rows]
        block = high + [v - h for v, h in zip(rows, high)]
        block.append(jnp.zeros((-len(block) % 8, width), F32))
        block = jnp.concatenate(block, axis=0).astype(F32)
        for j in range(each):
            above = 64 * (j // 2) + 40 + 8 * (j % 2) if each == 4 else 64 * j
            spread = [jnp.zeros((above, width), F32)] if above else []
            spread += [block, jnp.zeros((128 - above - block.shape[0], width), F32)]
            out = out + dot_nt(chosen[j], jnp.concatenate(spread, axis=0).astype(BF16))
    return out


def chain_rule(rows, d_re, d_im, d_scale):
    u, r, lr, li, scale = rows
    return u * (r * r * d_scale / scale - (lr * d_re + li * d_im)), lr * d_im - li * d_re


def kernel_middle(io):
    me = lax.axis_index("seq")
    core = me % 2
    tables = io.refs.tables
    carry = gather_carry(io.refs.ends, me // 2, io.ahead, coefs_of(tables, COEF2, True), coefs_of(tables, COEF16, True))
    carry = jnp.where(core == 0, carry, io.inside + tile_mul(carry, coefs_of(tables, COEF, True)))
    local = split_channels(io.local)
    row = rows_iota((MICRO * GROUPS, 8, 128))
    states, priors = [], []
    for half in range(HALVES):
        table, step8 = pair_of(tables, AHEAD, half), pair_of(tables, STEP, half)
        x8 = local[half]
        before_r, before_i = [], []
        for micro in range(MICRO):
            init = (tile_row(carry, 0, micro, half), tile_row(carry, 1, micro, half))
            before, _ = chain_from(x8, micro, step8, init, False)
            for g in range(GROUPS):
                edge = edge_bcast(before[g], 7)
                before_r.append(edge[0])
                before_i.append(edge[1])
        br, bi = jnp.stack(before_r), jnp.stack(before_i)
        hr = x8[0] + (table[0] * br - table[1] * bi)
        hi = x8[1] + (table[0] * bi + table[1] * br)
        states.append((hr, hi))
        priors.append((jnp.where(row == 0, br, pltpu.roll(hr, 1, 1)), jnp.where(row == 0, bi, pltpu.roll(hi, 1, 1))))
    hidden = permute(join_channels(states).astype(BF16), io.deal_back).astype(BF16)
    normed = io.normed
    y = dot(hidden, io.c) + io.skip * normed.astype(F32)
    k0, k1 = 0.7978845608028654, 0.044715
    yy = y * y
    t = jnp.tanh(k0 * (y + k1 * (yy * y)))
    act = (0.5 * y * (1.0 + t)).astype(BF16)
    slope = 0.5 * (1.0 + t) + 0.5 * y * (1.0 - t * t) * (k0 * (1.0 + 3.0 * k1 * yy))
    gated = dot(act, io.glu)
    value, gate = gated[:, :512], gated[:, 512:]
    sig = jax.nn.sigmoid(gate)
    go = io.go.astype(F32)
    io.put(out=(io.x.astype(F32) + value * sig).astype(BF16))
    gs = go * sig
    dgated = jnp.concatenate([gs, gs * value * (1.0 - sig)], axis=1).astype(BF16)
    dy = (dot_nt(dgated, io.glu) * slope).astype(BF16)
    dhidden = dot_nt(dy, io.c).astype(BF16)
    q = split_channels(permute(dhidden, io.deal))
    parts, scanned = {}, []
    for half in range(HALVES):
        step8 = conj(pair_of(tables, STEP, half))
        levels = [(1 << n, pair_of(tables, LEVEL + 2 * n, half)) for n in range(3)]
        x8 = group_scan(q[half], levels, True)
        scanned.append(x8)
        for micro in range(MICRO):
            _, v = chain_from(x8, micro, step8, None, True)
            parts[(micro, half)] = (v[0][0:1, :], v[1][0:1, :])
    io.put(first=tile_rows(parts), carry=carry, act=act, dgated=dgated, hidden=hidden, dy=dy, back=join_channels(scanned), prior=join_channels(priors))


def by_core(ref_keep, ref_send, core, even, odd):
    ref_keep[...] = jnp.where(core == 0, even, odd).astype(BF16)
    ref_send[...] = jnp.where(core == 0, odd, even).astype(BF16)


def kernel_products(io):
    core = lax.axis_index("seq") % 2
    glu_grad = dot_tn(io.act, io.dgated)
    c_grad = dot_tn(io.hidden, io.dy)
    even, odd = chunk_rows(glu_grad[:, :768], jnp.concatenate([glu_grad[:, 768:], c_grad], axis=1))
    by_core(io.refs.keep, io.refs.send, core, even, odd)


def kernel_carried(io):
    core = lax.axis_index("seq") % 2
    tables = io.refs.tables
    own, other = io.first, io.other
    first, second = jnp.where(core == 0, own, other), jnp.where(core == 0, other, own)
    whole = first + tile_mul(second, coefs_of(tables, COEF, False))
    io.put(chip_first=whole.astype(BF16))
    inside = jnp.where(core == 0, other, 0.0)
    far_step = [(tables[COEF][half : half + 1, :], tables[COEF + 1][4 + half : 5 + half, :]) for half in range(HALVES)]
    back, priors, pairs = split_channels(io.back), split_channels(io.prior), split_channels(io.pairs.astype(F32))
    projs, rates, angles, heads, tails = [], [], [], {}, {}
    for half in range(HALVES):
        table, step8 = pair_of(tables, BACK, half), conj(pair_of(tables, STEP, half))
        from_start = conj(pair_of(tables, AHEAD, half))
        from_start = [jnp.where(rows_iota() == 0, edge, pltpu.roll(t, 1, 0)) for edge, t in zip((1.0, 0.0), from_start)]
        scale = tables[half * PER_HALF + SCALE]
        x8 = back[half]
        after_r, after_i = [], []
        for micro in range(MICRO):
            init = (tile_row(inside, 0, micro, half), tile_row(inside, 1, micro, half))
            after, _ = chain_from(x8, micro, step8, init, True)
            for g in range(GROUPS):
                edge = edge_bcast(after[g], 0)
                after_r.append(edge[0])
                after_i.append(edge[1])
        ar, ai = jnp.stack(after_r), jnp.stack(after_i)
        gr = x8[0] + (table[0] * ar - table[1] * ai)
        gi = x8[1] + (table[0] * ai + table[1] * ar)
        pr, pi = priors[half]
        d_re = total(gr * pr + gi * pi)
        d_im = total(gi * pr - gr * pi)
        d_scale = total(gr * pairs[half][0] + gi * pairs[half][1])
        for micro in range(MICRO):
            used = tuple(io.carry[4 * comp + 2 * micro + half : 4 * comp + 2 * micro + half + 1, :] for comp in range(2))
            _, v = chain_from((gr, gi), micro, step8, None, True)
            m = cmul(v, from_start)
            tails[(micro, half)] = (column_sum(m[0]), column_sum(m[1]))
            m = cmul(tails[(micro, half)], conj(used))
            d_re, d_im = d_re - m[0], d_im - m[1]
            _, v = chain_from(priors[half], micro, conj(step8), None, False)
            m = cmul(v, conj(table))
            more = cmul(far_step[half], used)
            m = (column_sum(m[0]) - TOK * more[0], column_sum(m[1]) - TOK * more[1])
            far = cmul(m, far_step[half])
            heads[(micro, half)] = tuple(jnp.where(core == 0, f, n) for f, n in zip(far, m))
        rate, turn = chain_rule(rows_of(tables, half), d_re, d_im, d_scale)
        rates.append(rate)
        angles.append(turn)
        projs.append((gr * scale, gi * scale))
    dealt = join_channels(projs).astype(BF16)
    dproj = permute(dealt, io.deal_back).astype(BF16)
    dyf, normed = io.dy.astype(F32), io.normed
    dnormed = dot_nt(dealt, io.b_perm) + io.skip * dyf
    io.put(dnormed=dnormed)
    fours = [column_sum(dnormed * io.xhat), column_sum(dnormed), column_sum(dyf * normed.astype(F32))]
    join = lambda two: jnp.concatenate(two, axis=1)
    twos = [join(rates), join(angles)]
    of_tile = lambda tile, at: join([tile[at : at + 1, :], tile[at + 1 : at + 2, :]])
    last = io.last
    for micro in range(MICRO):
        for sums in (tails, heads):
            twos += [join([sums[(micro, half)][comp] for half in range(HALVES)]) for comp in range(2)]
        twos += [of_tile(tile, 4 * comp + 2 * micro) for tile in (last, whole) for comp in range(2)]
    smalls = place_smalls(fours, twos, io.chosen4, io.chosen2)
    b_grad = dot_tn(normed, dproj)
    even, odd = chunk_rows(b_grad[:, :256], b_grad[:, 256:])
    tiles = [jnp.broadcast_to(v[:, None, :], (CHIPS, 8, 128)) for v in (smalls[:CHIPS], smalls[CHIPS:])]
    by_core(io.refs.keep, io.refs.send, core, jnp.concatenate([even, tiles[0]], axis=2), jnp.concatenate([odd, tiles[1]], axis=2))


def kernel_pack(io):
    out = io.refs.packed
    out[:, :, 0:768] = (io.keep.astype(F32) + io.got.astype(F32)).astype(BF16)
    keep, got = io.keep_b.astype(F32), io.got_b.astype(F32)
    out[:, :, 768:1024] = (keep[:, :, 0:256] + got[:, :, 0:256]).astype(BF16)
    out[:, :, 1024:1152] = jnp.broadcast_to(io.chip_first[None], (CHIPS, 8, 128))
    low = rows_iota((CHIPS, 8, 128)) < 4
    out[:, :, 1152:1280] = jnp.where(low, keep[:, :, 256:384], got[:, :, 256:384]).astype(BF16)


def segment_joins(lengths_ref):
    second = (rows_iota() & 2) == 2
    bits = []
    for micro in range(MICRO):
        mask, at = jnp.int32(0), jnp.int32(0)
        for slot in range(16):
            unit = lax.shift_left(jnp.int32(1), jnp.minimum(at // (8 * TOK), 15))
            mask = jnp.where(at < N * TOK, mask | unit, mask)
            at = at + lengths_ref[micro, slot]
        bits.append(mask)
    pick = lambda two: jnp.where(second, two[1], two[0]).astype(F32)
    return [pick([1 - (lax.shift_right_logical(b, g + 1) & 1) for b in bits]) for g in range(15)], bits


def kernel_ahead(io):
    me = lax.axis_index("seq")
    tables = io.refs.tables
    near, far = [], []
    for half in range(HALVES):
        step8 = conj(pair_of(tables, STEP, half))
        tiles = [pair_of(tables, BACK, half)]
        for _ in range(2 * GROUPS - 1):
            tiles.append(cmul(tiles[-1], step8))
        tiles = tiles[::-1]
        for comp in range(2):
            far.append(jnp.concatenate([t[comp] for t in tiles[:GROUPS]], axis=0))
            near.append(jnp.concatenate([t[comp] for t in tiles[GROUPS:]], axis=0))
    near, far = jnp.concatenate(near, axis=1), jnp.concatenate(far, axis=1)
    sums = jnp.concatenate([column_sum(near) + column_sum(far), jnp.zeros((7, 512), F32)], axis=0)
    io.put(reach=near, reach_sum=sums, reach_low=jnp.concatenate([far, near], axis=0).astype(BF16))
    ends = io.refs.ends
    own, other = (ends[:, i].reshape(CHIPS * 8, 128) for i in (2, 3))
    first = me % 2 == 0
    io.put(columns=jnp.concatenate([jnp.where(first, own, other), jnp.where(first, other, own)], axis=1))
    lane = lax.broadcasted_iota(jnp.int32, (128, 128), 0)
    col = lax.broadcasted_iota(jnp.int32, (128, 128), 1)
    w = lane % 64
    hot = lambda where: jnp.where(where, 1.0, 0.0).astype(BF16)
    spot = jnp.where((w >= 40) & (w < 56) & (w % 8 < 6), 4 * (w % 8 % 3) + 2 * (lane // 64) + (w - 40) // 8, -1)
    spot = jnp.where(w < 36, jnp.where(w % 18 < 2, 12 + 2 * (w % 18) + lane // 64, -1), spot)
    channel = (lane // 64) == col % 2
    wanted = lambda k: hot(channel & (w < 36) & (w % 18 == 2 + 8 * ((col // 2) % 2) + k))
    io.put(pick=jnp.concatenate([hot(spot == col)] + [wanted(k) for k in range(8)], axis=1))
    half_rows = [jnp.concatenate(rows_of(tables, half) + [jnp.zeros((3, 128), F32)], axis=0) for half in range(HALVES)]
    mine = choose(jnp.where(me // 64 == 0, half_rows[0], half_rows[1]), hot(lane == (2 * me) % 128 + col % 2))
    io.put(channels=mine)
    pows = powers((mine[2:3, :], mine[3:4, :]), 10)
    io.put(channel_pows=jnp.concatenate([v for at in (7, 8, 10) for v in pows[at]] + [jnp.zeros((2, 128), F32)], axis=0))
    feature = lax.broadcasted_iota(jnp.int32, (8, 512), 1)
    here = feature == 4 * me + rows_iota((8, 512)) % 4
    b_rows = io.b_rows.astype(F32)
    b_rows = jnp.where(me % 2 == 0, b_rows, pltpu.roll(b_rows, 4, 0))
    at_row = lambda v: jnp.broadcast_to(jnp.sum(jnp.where(here, v, 0.0), axis=1, keepdims=True), (8, 512))
    io.put(mine=jnp.concatenate([at_row(io.gain), at_row(io.bias), b_rows], axis=1))
    joins, bits = segment_joins(io.ready(lengths=0))
    for group, tile in enumerate(joins):
        io.refs.joined[group] = tile
    group = lax.broadcasted_iota(jnp.int32, (16, 128), 0)
    second = (lax.broadcasted_iota(jnp.int32, (16, 128), 1) // 2) % 2 == 1
    opens = lax.shift_right_logical(jnp.where(second, bits[1], bits[0]), group) & 1
    io.put(opens=opens.astype(F32))


def all_carries(first, tables, joined):
    coef2, coef8 = (coefs_of(tables, at, False) for at in (COEF2, COEF8))
    groups = first.reshape(16, 4, 8, 128)
    step = lambda c, by: c * by[0] + pltpu.roll(c, 4, 1) * by[1]
    inner = [None] * 4
    inner[3] = jnp.zeros((16, 8, 128), F32)
    for p in range(2, -1, -1):
        inner[p] = groups[:, p + 1] + step(inner[p + 1], coef2)
    whole = groups[:, 0] + step(inner[0], coef2)
    entering = [None] * 16
    entering[15] = jnp.zeros((8, 128), F32)
    for g in range(14, -1, -1):
        entering[g] = (whole[g + 1] + tile_mul(entering[g + 1], coef8)) * joined[g]
    factor = jnp.stack(entering)
    out = []
    for p in range(3, -1, -1):
        out.append(inner[p] + factor)
        factor = step(factor, coef2)
    return jnp.stack(out[::-1], axis=1).reshape(CHIPS, 8, 128)


def kernel_last(io, carries, split):
    me = lax.axis_index("seq")
    core = me % 2
    tables = io.refs.tables
    parts = io.refs.parts
    enter = all_carries(parts[:, :, 1024:1152].astype(F32), tables, io.refs.joined)
    carries[...] = enter
    mine = carries[me // 2]
    mine = jnp.where(core == 0, tile_mul(mine, coefs_of(tables, COEF, False)), mine)
    reach_cols = io.reach
    reach = [(reach_cols[:, c : c + 128], reach_cols[:, c + 128 : c + 256]) for c in (0, 256)]
    scale_row = jnp.concatenate([tables[half * PER_HALF + SCALE][0:1, :] for half in (0, 0, 1, 1)], axis=1)
    rows = []
    for micro in range(MICRO):
        cols = []
        for half in range(HALVES):
            nr, ni = tile_row(mine, 0, micro, half)[0:1, :], tile_row(mine, 1, micro, half)[0:1, :]
            lr, li = reach[half]
            cols += [lr * nr - li * ni, lr * ni + li * nr]
        rows.append(jnp.concatenate(cols, axis=1))
    dproj = jnp.concatenate(rows, axis=0) * scale_row
    dnormed = dot_nt(dproj.astype(BF16), io.b_perm) + io.dnormed
    xhat, rstd = io.xhat, io.rstd[:, 0:1]
    dx = dnormed * io.gain
    m1 = jnp.mean(dx, axis=1, keepdims=True)
    m2 = jnp.mean(dx * xhat, axis=1, keepdims=True)
    io.put(in_grad=(io.go.astype(F32) + rstd * (dx - m1 - xhat * m2)).astype(BF16))
    summed = jnp.sum(parts[:, :, 0:1024].astype(F32), axis=0)
    io.put(glu_grad=jnp.concatenate([summed[0:4, 0:768], summed[4:8, 0:256]], axis=1))
    io.put(c_grad=summed[4:8, 256:768])
    moved = dot(io.columns, io.reach_low)
    low = rows_iota((CHIPS, 8, 128)) < 4
    spread = lambda comp, half: jnp.where(low, enter[:, comp * 4 + half : comp * 4 + half + 1, :], enter[:, comp * 4 + 2 + half : comp * 4 + 3 + half, :])
    cols = []
    for half in range(HALVES):
        c = 256 * half
        mr = moved[:, c : c + 128].reshape(CHIPS, 8, 128)
        mi = moved[:, c + 128 : c + 256].reshape(CHIPS, 8, 128)
        nr, ni = spread(0, half), spread(1, half)
        cols += [jnp.sum(mr * nr - mi * ni, axis=0), jnp.sum(mr * ni + mi * nr, axis=0)]
    rows8 = jnp.concatenate(cols, axis=1)
    rows8 = rows8 + pltpu.roll(rows8, 4, 0)
    enter_sum = jnp.sum(enter, axis=0)
    reach_sum = io.reach_sum[0:1, :]
    cols = []
    for half in range(HALVES):
        c = 256 * half
        fold2 = lambda comp: enter_sum[comp * 4 + half : comp * 4 + half + 1, :] + enter_sum[comp * 4 + 2 + half : comp * 4 + 3 + half, :]
        nr, ni = fold2(0), fold2(1)
        lr, li = reach_sum[:, c : c + 128], reach_sum[:, c + 128 : c + 256]
        cols += [lr * nr - li * ni, lr * ni + li * nr]
    sums_row = jnp.concatenate(cols, axis=1)
    both = jnp.where(rows_iota((8, 512)) < 4, rows8, sums_row) * scale_row
    moved_x = jnp.concatenate([choose(both[:, :256], io.deal_back), choose(both[:, 256:], io.deal_back)], axis=1)
    moved_one = jnp.broadcast_to(moved_x[4:5, :], (8, 512))
    own = io.mine
    gain_f, bias_f, b_rows = own[:, 0:512], own[:, 512:1024], own[:, 1024:1536]
    b_sum = jnp.concatenate([summed[0:4, 768:1024], summed[4:8, 768:1024]], axis=1)
    io.put(b_grad=b_sum + (gain_f * moved_x + bias_f * moved_one)[0:4, :])
    gain_carry = jnp.sum(b_rows * moved_x, axis=1, keepdims=True)
    bias_carry = jnp.sum(b_rows * moved_one, axis=1, keepdims=True)
    small = parts[:, :, 1152:1280]
    own, other = small[:, 0, :].astype(F32), small[:, 4, :].astype(F32)
    sums = column_sum(own + other)
    gathered = choose(jnp.concatenate([sums, jnp.zeros((7, 128), F32)], axis=0), io.pick[:, 0:128])
    d_re, d_im, d_scale = owned_channels(own, other, core, io, split)
    rate, turn = chain_rule([io.channels[i : i + 1, :] for i in range(5)], d_re, d_im, d_scale)
    shift = lambda v, by: pltpu.roll(v, 128 - by, 1)
    diagonal = lax.broadcasted_iota(jnp.int32, (8, 128), 1) == rows_iota()
    to_lanes = lambda v: column_sum(jnp.where(diagonal, v, 0.0))
    sums = gathered[0:1, :]
    io.put(gain_grad=(sums + to_lanes(gain_carry))[:, 0:4])
    io.put(bias_grad=(shift(sums, 4) + to_lanes(bias_carry))[:, 0:4])
    io.put(skip_grad=shift(sums, 8)[:, 0:4])
    io.put(rate_grad=(shift(sums, 12) + rate)[:, 0:2])
    io.put(angle_grad=(shift(sums, 14) + turn)[:, 0:2])


def group_chain(coef, value, opens, reverse):
    row = lax.broadcasted_iota(jnp.int32, (16, 128), 0)
    pos = 15 - row if reverse else row
    moved = lambda v, by: pltpu.roll(v, 16 - by if reverse else by, 0)
    opens = jnp.where(row == 0, 1.0, opens)
    keep = jnp.where(pos == 0, 0.0, 1.0 - (moved(opens, 1) if reverse else opens))
    a = (keep * coef[0], keep * coef[1])
    b = tuple(keep * moved(v, 1) for v in value)
    for by in (1, 2, 4, 8):
        inside = pos >= by
        before = lambda v: jnp.where(inside, moved(v, by), 0.0)
        pb, pa = tuple(before(v) for v in b), tuple(before(v) for v in a)
        m = cmul(a, pb)
        b = (b[0] + m[0], b[1] + m[1])
        a = cmul(a, pa)
    return b


def owned_channels(own, other, core, io, split):
    first, second = jnp.where(core == 0, own, other), jnp.where(core == 0, other, own)
    values = []
    for rows in (first, second):
        values.append(dot(rows.astype(BF16), io.pick[:, 128:1152]))
    pows = [tuple(io.channel_pows[2 * i + comp : 2 * i + comp + 1, :] for comp in range(2)) for i in range(3)]
    step, step2, step8 = pows
    of = lambda q, k: (values[q][:, 128 * k : 128 * k + 128], values[q][:, 128 * k + 128 : 128 * k + 256])
    plus = lambda x, y: (x[0] + y[0], x[1] + y[1])
    last0, last1 = of(0, 4), of(1, 4)
    kept = [*plus(last1, cmul(last0, step)), *of(0, 6), *of(0, 0), *of(1, 0), *plus(of(0, 2), of(1, 2)), *last0]
    for i, v in enumerate(kept):
        split[i] = v
    at = lambda i, p: (split[i, pl.ds(p, 16, stride=4), :], split[i + 1, pl.ds(p, 16, stride=4), :])
    ends, firsts = [at(0, p) for p in range(4)], [at(2, p) for p in range(4)]
    zero = (jnp.zeros((16, 128), F32), jnp.zeros((16, 128), F32))
    states, grads = [zero], [zero]
    for p in range(1, 4):
        states.append(plus(cmul(states[-1], step2), ends[p - 1]))
        grads.append(plus(cmul(grads[-1], conj(step2)), firsts[4 - p]))
    grads = grads[::-1]
    into = group_chain(step8, plus(cmul(states[3], step2), ends[3]), io.opens, False)
    back = group_chain(conj(step8), plus(cmul(grads[0], conj(step2)), firsts[0]), io.opens, True)
    d_lam, d_scale = zero, zero
    for p in range(4):
        states[p] = plus(states[p], into)
        into = cmul(into, step2)
        grads[3 - p] = plus(grads[3 - p], back)
        back = cmul(back, conj(step2))
    for p in range(4):
        h0, n = states[p], grads[p]
        far = cmul(h0, step)
        h1 = plus(far, at(10, p))
        seen = plus(cmul(far, step), cmul(h1, step))
        seen = plus(at(8, p), (TOK * seen[0], TOK * seen[1]))
        for x, y in ((at(4, p), h0), (at(6, p), h1), (n, seen)):
            d_lam = plus(d_lam, cmul(x, conj(y)))
        d_scale = plus(d_scale, cmul(n, conj(ends[p])))
    both = lambda v: (lambda t: t + pltpu.roll(t, 126, 1))(column_sum(v))
    d_re, d_im, s_re, s_im = (both(v) for v in d_lam + d_scale)
    lr, li, scale = (io.channels[i : i + 1, :] for i in (2, 3, 4))
    return d_re, d_im, (lr * s_re + li * s_im) / scale


def body(block_in, out_grad, lengths, ln_gain, ln_bias, b_proj, c_proj, glu_weight, skip_gain, log_rate, angle):
    rows = MICRO * TOK
    x = block_in.reshape(rows, 512)
    go = out_grad.reshape(rows, 512)
    gain, bias, skip = (v.reshape(1, 512) for v in (ln_gain, ln_bias, skip_gain))
    rate2, angle2 = log_rate.reshape(2, 128), angle.reshape(2, 128)
    spread = deal()
    deal_m = jnp.asarray(spread, BF16)
    back_m = jnp.asarray(spread.T.copy(), BF16)
    chosen4, chosen2 = jnp.asarray(one_hots(4, 512), BF16), jnp.asarray(one_hots(2, 256), BF16)
    full = (rows, 512)
    k1 = call(
        kernel_first,
        [
            (LOAD, dict(x=x, gain=gain, bias=bias, log_rate=rate2, angle=angle2)),
            (SCALARS, dict(lengths=lengths)),
            (LOAD, dict(b=b_proj, deal=deal_m)),
            (LOAD, dict(deal_back=back_m, c=c_proj, skip=skip, glu=glu_weight, go=go, chosen4=chosen4, chosen2=chosen2)),
            (PLAIN, dict(b_tiles=b_proj.reshape(CHIPS, 8, 512))),
        ],
        [
            (
                HELD,
                dict(
                    normed=(full, BF16), pairs=(full, BF16), local=(full, F32), send=((CHIPS + 2, 8, 128), BF16),
                    columns=((CHIPS, 8, 128), BF16), ahead=((8, 128), F32), b_rows=((8, 512), BF16), last=((8, 128), F32),
                ),
            )
        ],
        flops=300_000_000, nbytes=3_000_000,
    )
    swap = functools.partial(lax.ppermute, axis_name="seq", perm=[(i, i ^ 1) for i in range(N)])
    same_core = [[2 * t + core for t in range(CHIPS)] for core in range(2)]
    exchange = functools.partial(lax.all_to_all, axis_name="seq", split_axis=0, concat_axis=0, tiled=True, axis_index_groups=same_core)
    kt = call(
        kernel_tables,
        [(HELD, dict(x=k1.x, log_rate=k1.log_rate, angle=k1.angle, b=k1.b, deal=k1.deal))],
        [
            (HELD, dict(tables=((TABLES, 8, 128), F32), xhat=(full, F32), rstd=((rows, 128), F32), b_perm=((512, 512), BF16))),
        ],
        flops=600_000_000, nbytes=3_000_000,
    )
    kj = call(
        kernel_join, [(HELD, dict(last=k1.last, got=swap(k1.send), columns=k1.columns, tables=kt.tables))],
        [(HELD, dict(inside=((8, 128), F32), ends=((CHIPS, 4, 8, 128), BF16)))], flops=1_000_000, nbytes=1_000_000,
    )
    ends = exchange(kj.ends)
    k2 = call(
        kernel_middle,
        [
            (HELD, dict(deal_back=k1.deal_back, c=k1.c, skip=k1.skip, glu=k1.glu, go=k1.go, ahead=k1.ahead)),
            (HELD, dict(ends=ends, inside=kj.inside, tables=kt.tables, local=k1.local, normed=k1.normed, deal=k1.deal, x=k1.x)),
        ],
        [
            (COPY, dict(out=(full, BF16))),
            (
                HELD,
                dict(
                    first=((8, 128), F32), carry=((8, 128), F32), act=(full, BF16), dgated=((rows, 1024), BF16), hidden=(full, BF16), dy=(full, BF16),
                    back=(full, F32), prior=(full, F32),
                ),
            ),
        ],
        flops=1_000_000_000, nbytes=6_000_000,
    )
    other = swap(k2.first)
    wide, narrow = ((CHIPS, 8, 768), BF16), ((CHIPS, 8, 384), BF16)
    kp = call(
        kernel_products, [(HELD, dict(act=k2.act, dgated=k2.dgated, hidden=k2.hidden, dy=k2.dy, deal_back=k1.deal_back))], [(HELD, dict(keep=wide, send=wide))],
        flops=2_000_000_000, nbytes=3_000_000,
    )
    got = swap(kp.send)
    kc = call(
        kernel_carried,
        [
            (HELD, dict(carry=k2.carry, last=k1.last)),
            (HELD, dict(first=k2.first, other=other, back=k2.back, prior=k2.prior, dy=k2.dy, tables=kt.tables, pairs=k1.pairs, b_perm=kt.b_perm)),
            (HELD, dict(deal_back=k1.deal_back, normed=k1.normed, xhat=kt.xhat, skip=k1.skip, chosen4=k1.chosen4, chosen2=k1.chosen2)),
        ],
        [(HELD, dict(chip_first=((8, 128), BF16), dnormed=(full, F32), keep=narrow, send=narrow))],
        flops=6_000_000_000, nbytes=3_000_000,
    )
    got_b = swap(kc.send)
    ka = call(
        kernel_ahead,
        [
            (SCALARS, dict(lengths=lengths)),
            (HELD, dict(tables=kt.tables, ends=ends, gain=k1.gain, bias=k1.bias, b_rows=k1.b_rows, dnormed=kc.dnormed)),
        ],
        [
            (
                HELD,
                dict(
                    reach=((TOK, 512), F32), reach_sum=((8, 512), F32), reach_low=((2 * TOK, 512), BF16), columns=((CHIPS * 8, 256), BF16),
                    channels=((8, 128), F32), channel_pows=((8, 128), F32), opens=((16, 128), F32), pick=((128, 1152), BF16), mine=((8, 1536), F32), joined=((15, 8, 128), F32),
                ),
            )
        ],
        flops=200_000_000, nbytes=3_000_000,
    )
    packed = call(
        kernel_pack, [(HELD, dict(keep=kp.keep, got=got, keep_b=kc.keep, got_b=got_b, chip_first=kc.chip_first, reach=ka.reach))],
        [(HELD, dict(packed=((CHIPS, 8, 1280), BF16)))], flops=1_000_000, nbytes=2_400_000,
    ).packed
    parts = exchange(packed)
    four, two = ((1, 4), F32), ((1, 2), F32)
    k3 = call(
        kernel_last,
        [
            (HELD, dict(parts=parts, dnormed=kc.dnormed, go=k1.go, deal_back=k1.deal_back, tables=kt.tables, b_perm=kt.b_perm, xhat=kt.xhat, rstd=kt.rstd)),
            (HELD, dict(gain=k1.gain, reach=ka.reach, reach_sum=ka.reach_sum, reach_low=ka.reach_low, columns=ka.columns)),
            (HELD, dict(channels=ka.channels, channel_pows=ka.channel_pows, opens=ka.opens, pick=ka.pick, mine=ka.mine, joined=ka.joined)),
        ],
        [
            (COPY, dict(in_grad=(full, BF16), b_grad=((4, 512), F32), c_grad=((4, 512), F32), glu_grad=((4, 1024), F32))),
            (COPY, dict(gain_grad=four, bias_grad=four, skip_grad=four, rate_grad=two, angle_grad=two)),
        ],
        extra=[pltpu.VMEM((CHIPS, 8, 128), F32), pltpu.VMEM((12, CHIPS, 128), F32)], flops=600_000_000, nbytes=5_000_000,
    )
    return (
        k2.out.reshape(block_in.shape),
        k3.in_grad.reshape(block_in.shape),
        k3.gain_grad.reshape(4),
        k3.bias_grad.reshape(4),
        k3.b_grad,
        k3.c_grad,
        k3.glu_grad,
        k3.skip_grad.reshape(4),
        k3.rate_grad.reshape(2),
        k3.angle_grad.reshape(2),
    )


def solution(mesh):
    tokens = P(None, "seq", None)
    in_specs = (tokens, tokens) + (P(),) * 9
    out_specs = (tokens, tokens, P("seq"), P("seq"), P("seq", None), P("seq", None), P("seq", None), P("seq"), P("seq"), P("seq"))
    return jax.shard_map(body, mesh=mesh, in_specs=in_specs, out_specs=out_specs, check_vma=False)
```

```python
import functools

import jax
import jax.numpy as jnp
import numpy as np
from jax import lax
from jax.experimental import pallas as pl
from jax.experimental.pallas import tpu as pltpu
from jax.sharding import PartitionSpec as P

F32 = jnp.float32
BF16 = jnp.bfloat16
VMEM_LIMIT = 40 * 1024 * 1024
TOK = 128
GROUPS = TOK // 8
MICRO = 2
HALVES = 2
N = 128
CHIPS = 64


def deal():
    out = np.zeros((256, 256), np.float32)
    for n in range(128):
        out[2 * n, n] = 1.0
        out[2 * n + 1, 128 + n] = 1.0
    return out


def dot(a, b):
    return jnp.dot(a, b, preferred_element_type=F32)


def dot_tn(a, b):
    return lax.dot_general(a, b, (((0,), (0,)), ((), ())), preferred_element_type=F32)


def dot_nt(a, b):
    return lax.dot_general(a, b, (((1,), (1,)), ((), ())), preferred_element_type=F32)


def cmul(a, b):
    return (a[0] * b[0] - a[1] * b[1], a[0] * b[1] + a[1] * b[0])


def conj(a):
    return (a[0], -a[1])


def rows_iota(shape=(8, 128)):
    return lax.broadcasted_iota(jnp.int32, shape, len(shape) - 2)


def rest(w):
    small = jnp.minimum(w, 0.5)
    poly = 1.0 - small * (1.0 / 11.0)
    for k in range(10, 1, -1):
        poly = 1.0 - small * (1.0 / k) * poly
    return jnp.where(w < 0.5, small * poly, 1.0 - jnp.exp(-w))


def params(log_rate, angle):
    u = jnp.exp(log_rate)
    r = jnp.where(u < 0.5, 1.0 - rest(u), jnp.exp(-u))
    lam = (r * jnp.cos(angle), r * jnp.sin(angle))
    return u, r, lam, jnp.sqrt(rest(2.0 * u))


def powers(lam, count):
    out = [lam]
    for _ in range(count):
        out.append(cmul(out[-1], out[-1]))
    return out


def spread_rows(pair, half):
    return tuple(jnp.broadcast_to(v[half : half + 1, :], (8, 128)) for v in pair)


def scan_tables(pows, reverse):
    row = rows_iota()
    pos = (7 - row) if reverse else row
    levels = []
    for s, p in ((1, pows[0]), (2, pows[1]), (4, pows[2])):
        keep = pos >= s
        levels.append((s, (jnp.where(keep, p[0], 0.0), jnp.where(keep, p[1], 0.0))))
    e = pos + 1
    table = (jnp.ones((8, 128), F32), jnp.zeros((8, 128), F32))
    for bit in range(4):
        on = (lax.shift_right_logical(e, bit) & 1) == 1
        table = cmul(table, (jnp.where(on, pows[bit][0], 1.0), jnp.where(on, pows[bit][1], 0.0)))
    return levels, table


def group_scan(x, levels, reverse):
    xr, xi = x
    for s, (mr, mi) in levels:
        shift = 8 - s if reverse else s
        rr = pltpu.roll(xr, shift, 1)
        ri = pltpu.roll(xi, shift, 1)
        xr, xi = xr + (mr * rr - mi * ri), xi + (mr * ri + mi * rr)
    return xr, xi


def tile_rows(parts):
    rows = []
    for comp in range(2):
        for micro in range(MICRO):
            for half in range(HALVES):
                rows.append(parts[(micro, half)][comp])
    return jnp.concatenate(rows, axis=0)


def tile_lam(p):
    row = rows_iota()
    odd = (row & 1) == 1
    re = jnp.where(odd, p[1][0], p[0][0])
    im = jnp.where(odd, p[1][1], p[0][1])
    return re, jnp.where(row < 4, -im, im)


def tile_mul(c, coef):
    return c * coef[0] + pltpu.roll(c, 4, 0) * coef[1]


def gather_carry(ends_ref, chip, dmax, coef, coef8):
    chains = []
    for chain in range(4):
        acc = None
        for i in range(7, -1, -1):
            d = chain * 8 + i
            at = jnp.maximum(chip - 1 - d, 0)
            e = ends_ref[at, 0].astype(F32) + ends_ref[at, 1].astype(F32)
            e = jnp.where(d <= dmax, e, 0.0)
            acc = e if acc is None else tile_mul(acc, coef) + e
        chains.append(acc)
    out = chains[3]
    for chain in range(2, -1, -1):
        out = tile_mul(out, coef8) + chains[chain]
    return out


def segment_tile(lengths_ref, chip):
    second = (rows_iota() & 2) == 2
    base = chip * 2 * TOK
    ahead = []
    for micro in range(MICRO):
        first, at = jnp.int32(0), jnp.int32(0)
        for slot in range(16):
            first = jnp.where(at <= base, jnp.maximum(first, at), first)
            at = at + lengths_ref[micro, slot]
        ahead.append((base - first) // (2 * TOK) - 1)
    return jnp.where(second, ahead[1], ahead[0]).astype(F32)


def groups_of(value, micro_groups=MICRO * GROUPS):
    return value.reshape(micro_groups, 8, 128)


def split_channels(value):
    out = []
    for half in range(HALVES):
        c = 256 * half
        out.append((groups_of(value[:, c : c + 128]), groups_of(value[:, c + 128 : c + 256])))
    return out


def join_channels(halves):
    cols = []
    for re, im in halves:
        cols.append(re.reshape(MICRO * TOK, 128))
        cols.append(im.reshape(MICRO * TOK, 128))
    return jnp.concatenate(cols, axis=1)


def permute(value_bf, matrix):
    return jnp.concatenate([dot(value_bf[:, :256], matrix), dot(value_bf[:, 256:], matrix)], axis=1)


def layer_norm(x):
    mean = jnp.mean(x, axis=1, keepdims=True)
    centered = x - mean
    var = jnp.mean(centered * centered, axis=1, keepdims=True)
    rstd = lax.rsqrt(var + 1e-05)
    return centered * rstd, rstd


def chain_from(x, micro, step8, init, reverse):
    before = {}
    v = init
    order = range(GROUPS - 1, -1, -1) if reverse else range(GROUPS)
    for g in order:
        before[g] = v
        xr, xi = x[0][micro * GROUPS + g], x[1][micro * GROUPS + g]
        if v is None:
            v = (xr, xi)
        else:
            m = cmul(v, step8)
            v = (xr + m[0], xi + m[1])
    return before, v


def edge_bcast(pair, edge):
    return tuple(jnp.broadcast_to(p[edge : edge + 1, :], (8, 128)) for p in pair)


HELD, LOAD, COPY, SCALARS, PLAIN = range(5)


class Bag:
    pass


class Ports:
    def __init__(self, ins, outs, refs):
        n_in, n_out = len(ins), len(outs)
        scratch = list(refs[n_in + n_out :])
        out_refs = {name: ref for (name, _, _, _), ref in zip(outs, refs[n_in:])}
        table, self.pending, self.leaving, self.out_copies = {}, {}, [], {}
        sems = scratch.pop() if scratch else None
        i = 0
        for (name, _, mode), ref in zip(ins, refs):
            table[name] = ref
            if mode == PLAIN:
                self.spare = sems.at[i]
                i += 1
            elif mode != HELD:
                target = out_refs[name] if mode == LOAD else scratch.pop(0)
                self.pending[name] = pltpu.make_async_copy(ref, target, sems.at[i])
                self.pending[name].start()
                table[name] = target
                i += 1
        for name, _, _, mode in outs:
            table.setdefault(name, out_refs[name])
            if mode == COPY:
                table[name] = scratch.pop(0)
                self.out_copies[name] = pltpu.make_async_copy(table[name], out_refs[name], sems.at[i])
                i += 1
        self.table = table
        self.refs = Bag()
        self.refs.__dict__.update(table)

    def __getattr__(self, name):
        if name in self.pending:
            self.pending.pop(name).wait()
        return self.table[name][...]

    def ready(self, **names):
        (name,) = names
        if name in self.pending:
            self.pending.pop(name).wait()
        return self.table[name]

    def settle(self, count):
        for name in list(self.pending)[:count]:
            self.pending.pop(name).wait()

    def put(self, **values):
        for name, value in values.items():
            self.table[name][...] = value
            if name in self.out_copies:
                self.out_copies[name].start()
                self.leaving.append(name)

    def finish(self):
        for copy in self.pending.values():
            copy.wait()
        for name in self.leaving:
            self.out_copies[name].wait()


def call(kernel, ins, outs, extra=(), alias=None, flops=0, nbytes=0):
    ins = [(name, array, mode) for mode, group in ins for name, array in group.items()]
    outs = [(name, shape, kind, mode) for mode, group in outs for name, (shape, kind) in group.items()]
    outs += [(name, array.shape, array.dtype, HELD) for name, array, mode in ins if mode == LOAD]

    def run(*refs):
        n_extra = len(extra)
        ports = Ports(ins, outs, refs[: len(refs) - n_extra])
        kernel(ports, *refs[len(refs) - n_extra :])
        ports.finish()

    args, scratch, copies = [], [], 0
    for _, array, mode in ins:
        args.append(pltpu.with_memory_space_constraint(array, pltpu.VMEM if mode == HELD else pltpu.HBM))
        copies += mode != HELD
        if mode in (COPY, SCALARS):
            scratch.append((pltpu.VMEM if mode == COPY else pltpu.SMEM)(array.shape, array.dtype))
    for _, shape, kind, mode in outs:
        if mode == COPY:
            scratch.append(pltpu.VMEM(shape, kind))
            copies += 1
    if copies:
        scratch.append(pltpu.SemaphoreType.DMA((copies,)))
    spec = lambda mode: pl.BlockSpec(memory_space=pltpu.VMEM if mode == HELD else pl.ANY)
    out = pl.pallas_call(
        run,
        out_shape=[pltpu.VMEM(s, d) if mode == HELD else jax.ShapeDtypeStruct(s, d) for _, s, d, mode in outs],
        in_specs=[spec(mode) for _, _, mode in ins],
        out_specs=[spec(mode) for _, _, _, mode in outs],
        scratch_shapes=scratch + list(extra),
        input_output_aliases=alias or {},
        compiler_params=pltpu.CompilerParams(vmem_limit_bytes=VMEM_LIMIT),
        cost_estimate=pl.CostEstimate(flops=flops, bytes_accessed=nbytes, transcendentals=0),
    )(*args)
    made = Bag()
    made.__dict__.update({name: array for (name, _, _, _), array in zip(outs, out)})
    return made


def chunk_rows(left, right):
    w = left.shape[1]
    a = left.reshape(CHIPS, 8, w)
    b = right.reshape(CHIPS, 8, w)
    low = rows_iota((CHIPS, 8, w)) < 4
    return jnp.where(low, a, pltpu.roll(b, 4, 1)), jnp.where(low, pltpu.roll(a, 4, 1), b)


AHEAD, BACK, LEVEL, STEP, LAM, SCALE, RATE_U, RADIUS, PER_HALF = 0, 2, 4, 10, 12, 14, 15, 16, 17
COEF, COEF2, COEF8, COEF16, CHIPS_AHEAD, TABLES = 34, 36, 38, 40, 42, 43


def pair_of(tables, at, half):
    return tables[half * PER_HALF + at], tables[half * PER_HALF + at + 1]


def rows_of(tables, half):
    return [tables[half * PER_HALF + at][0:1, :] for at in (RATE_U, RADIUS, LAM, LAM + 1, SCALE)]


def coefs_of(tables, at, forward):
    ci = tables[at + 1]
    return tables[at], (ci if forward else -ci)


def kernel_first(io):
    me = lax.axis_index("seq")
    copy = pltpu.make_async_copy(io.refs.b_tiles.at[me // 2], io.refs.b_rows, io.spare)
    copy.start()
    io.settle(8)
    tables = io.refs.tables
    x = io.x.astype(F32)
    xhat, rstd = layer_norm(x)
    normed = (xhat * io.gain + io.bias).astype(BF16)
    io.put(normed=normed)
    io.put(xhat=xhat)
    io.put(rstd=jnp.broadcast_to(rstd, (MICRO * TOK, 128)))
    u, r, lam, scale = params(io.log_rate, io.angle)
    pows = powers(lam, 11)
    proj = dot(normed, io.b).astype(BF16)
    pairs = permute(proj, io.deal)
    io.put(pairs=pairs.astype(BF16))
    halves = split_channels(pairs)
    parts, scanned = {}, []
    for half in range(HALVES):
        mine = [spread_rows(p, half) for p in pows[:4]]
        (scale8,) = spread_rows((scale,), half)
        levels, table = scan_tables(mine, False)
        re, im = halves[half]
        x8 = group_scan((re * scale8, im * scale8), levels, False)
        scanned.append(x8)
        for micro in range(MICRO):
            _, v = chain_from(x8, micro, mine[3], None, False)
            parts[(micro, half)] = (v[0][7:8, :], v[1][7:8, :])
        back_levels, back_table = scan_tables([conj(p) for p in mine], True)
        values = list(table) + list(back_table) + [v for _, level in back_levels for v in level] + list(mine[3]) + list(mine[0])
        for at, value in enumerate(values + [scale8] + list(spread_rows((u, r), half))):
            tables[half * PER_HALF + at] = value
    last = tile_rows(parts)
    io.put(last=last)
    even, odd = chunk_rows(xhat[:TOK].T, xhat[TOK:].T)
    io.put(columns=jnp.where(me % 2 == 0, even, odd).astype(BF16))
    send = io.refs.send
    send[0:CHIPS] = jnp.where(me % 2 == 0, odd, even).astype(BF16)
    for i, part in enumerate(in_parts(last, 2)):
        send[CHIPS + i] = part
    io.put(local=join_channels(scanned))
    for to, at in ((COEF, 7), (COEF2, 8), (COEF8, 10), (COEF16, 11)):
        tables[to], tables[to + 1] = tile_lam([spread_rows(pows[at], half) for half in range(HALVES)])
    tables[CHIPS_AHEAD] = segment_tile(io.ready(lengths=0), me // 2)
    copy.wait()


def kernel_join(io):
    core = lax.axis_index("seq") % 2
    own, got = io.last, io.refs.got
    other = got[CHIPS].astype(F32) + got[CHIPS + 1].astype(F32)
    first, second = jnp.where(core == 0, own, other), jnp.where(core == 0, other, own)
    whole = second + tile_mul(first, coefs_of(io.refs.tables, COEF, True))
    io.put(inside=jnp.where(core == 0, 0.0, other))
    ends = io.refs.ends
    for i, part in enumerate(in_parts(whole, 2)):
        ends[:, i] = jnp.broadcast_to(part[None], (CHIPS, 8, 128))
    ends[:, 2] = io.columns
    ends[:, 3] = got[0:CHIPS]


def tile_row(tile, comp, micro, half):
    at = comp * 4 + micro * 2 + half
    return jnp.broadcast_to(tile[at : at + 1, :], (8, 128))


def total(v):
    return jnp.sum(jnp.sum(v, axis=0), axis=0, keepdims=True)


def column_sum(v):
    return jnp.sum(v, axis=0, keepdims=True)


def in_parts(value, count):
    parts = []
    for _ in range(count):
        parts.append(value.astype(BF16))
        value = value - parts[-1].astype(F32)
    return parts


def choose(value, one_hot):
    out = dot(jnp.concatenate([p.astype(F32) for p in in_parts(value, 3)], axis=0).astype(BF16), one_hot)
    return out[0:8, :] + out[8:16, :] + out[16:24, :]


def one_hots(each, width):
    at = np.arange(N)
    device = 2 * (at % CHIPS) + at // CHIPS
    out = np.zeros((each, N, width), np.float32)
    for j in range(each):
        out[j, at, each * device + j] = 1.0
    return out


def place_smalls(fours, twos, chosen4, chosen2):
    out = jnp.zeros((N, 128), F32)
    for rows, chosen, each in ((fours, chosen4, 4), (twos, chosen2, 2)):
        width = rows[0].shape[1]
        high = [v.astype(BF16).astype(F32) for v in rows]
        block = high + [v - h for v, h in zip(rows, high)]
        block.append(jnp.zeros((-len(block) % 8, width), F32))
        block = jnp.concatenate(block, axis=0).astype(F32)
        for j in range(each):
            above = 64 * (j // 2) + 40 + 8 * (j % 2) if each == 4 else 64 * j
            spread = [jnp.zeros((above, width), F32)] if above else []
            spread += [block, jnp.zeros((128 - above - block.shape[0], width), F32)]
            out = out + dot_nt(chosen[j], jnp.concatenate(spread, axis=0).astype(BF16))
    return out


def chain_rule(rows, d_re, d_im, d_scale):
    u, r, lr, li, scale = rows
    return u * (r * r * d_scale / scale - (lr * d_re + li * d_im)), lr * d_im - li * d_re


def kernel_middle(io):
    me = lax.axis_index("seq")
    core = me % 2
    tables = io.refs.tables
    carry = gather_carry(io.refs.ends, me // 2, tables[CHIPS_AHEAD], coefs_of(tables, COEF2, True), coefs_of(tables, COEF16, True))
    carry = jnp.where(core == 0, carry, io.inside + tile_mul(carry, coefs_of(tables, COEF, True)))
    local = split_channels(io.local)
    row = rows_iota((MICRO * GROUPS, 8, 128))
    states, priors = [], []
    for half in range(HALVES):
        table, step8 = pair_of(tables, AHEAD, half), pair_of(tables, STEP, half)
        x8 = local[half]
        before_r, before_i = [], []
        for micro in range(MICRO):
            init = (tile_row(carry, 0, micro, half), tile_row(carry, 1, micro, half))
            before, _ = chain_from(x8, micro, step8, init, False)
            for g in range(GROUPS):
                edge = edge_bcast(before[g], 7)
                before_r.append(edge[0])
                before_i.append(edge[1])
        br, bi = jnp.stack(before_r), jnp.stack(before_i)
        hr = x8[0] + (table[0] * br - table[1] * bi)
        hi = x8[1] + (table[0] * bi + table[1] * br)
        states.append((hr, hi))
        priors.append((jnp.where(row == 0, br, pltpu.roll(hr, 1, 1)), jnp.where(row == 0, bi, pltpu.roll(hi, 1, 1))))
    hidden = permute(join_channels(states).astype(BF16), io.deal_back).astype(BF16)
    normed = io.normed
    y = dot(hidden, io.c) + io.skip * normed.astype(F32)
    k0, k1 = 0.7978845608028654, 0.044715
    yy = y * y
    t = jnp.tanh(k0 * (y + k1 * (yy * y)))
    act = (0.5 * y * (1.0 + t)).astype(BF16)
    slope = 0.5 * (1.0 + t) + 0.5 * y * (1.0 - t * t) * (k0 * (1.0 + 3.0 * k1 * yy))
    gated = dot(act, io.glu)
    value, gate = gated[:, :512], gated[:, 512:]
    sig = jax.nn.sigmoid(gate)
    go = io.go.astype(F32)
    io.put(out=(io.x.astype(F32) + value * sig).astype(BF16))
    gs = go * sig
    dgated = jnp.concatenate([gs, gs * value * (1.0 - sig)], axis=1).astype(BF16)
    dy = (dot_nt(dgated, io.glu) * slope).astype(BF16)
    dhidden = dot_nt(dy, io.c).astype(BF16)
    q = split_channels(permute(dhidden, io.deal))
    parts, scanned = {}, []
    for half in range(HALVES):
        step8 = conj(pair_of(tables, STEP, half))
        levels = [(1 << n, pair_of(tables, LEVEL + 2 * n, half)) for n in range(3)]
        x8 = group_scan(q[half], levels, True)
        scanned.append(x8)
        for micro in range(MICRO):
            _, v = chain_from(x8, micro, step8, None, True)
            parts[(micro, half)] = (v[0][0:1, :], v[1][0:1, :])
    io.put(first=tile_rows(parts), carry=carry, act=act, dgated=dgated, hidden=hidden, dy=dy, back=join_channels(scanned), prior=join_channels(priors))


def by_core(ref_keep, ref_send, core, even, odd):
    ref_keep[...] = jnp.where(core == 0, even, odd).astype(BF16)
    ref_send[...] = jnp.where(core == 0, odd, even).astype(BF16)


def kernel_products(io):
    core = lax.axis_index("seq") % 2
    glu_grad = dot_tn(io.act, io.dgated)
    c_grad = dot_tn(io.hidden, io.dy)
    even, odd = chunk_rows(glu_grad[:, :768], jnp.concatenate([glu_grad[:, 768:], c_grad], axis=1))
    by_core(io.refs.keep, io.refs.send, core, even, odd)


def kernel_carried(io):
    core = lax.axis_index("seq") % 2
    tables = io.refs.tables
    own, other = io.first, io.other
    first, second = jnp.where(core == 0, own, other), jnp.where(core == 0, other, own)
    whole = first + tile_mul(second, coefs_of(tables, COEF, False))
    io.put(chip_first=whole.astype(BF16))
    inside = jnp.where(core == 0, other, 0.0)
    far_step = [(tables[COEF][half : half + 1, :], tables[COEF + 1][4 + half : 5 + half, :]) for half in range(HALVES)]
    back, priors, pairs = split_channels(io.back), split_channels(io.prior), split_channels(io.pairs.astype(F32))
    projs, rates, angles, heads, tails = [], [], [], {}, {}
    for half in range(HALVES):
        table, step8 = pair_of(tables, BACK, half), conj(pair_of(tables, STEP, half))
        from_start = conj(pair_of(tables, AHEAD, half))
        from_start = [jnp.where(rows_iota() == 0, edge, pltpu.roll(t, 1, 0)) for edge, t in zip((1.0, 0.0), from_start)]
        scale = tables[half * PER_HALF + SCALE]
        x8 = back[half]
        after_r, after_i = [], []
        for micro in range(MICRO):
            init = (tile_row(inside, 0, micro, half), tile_row(inside, 1, micro, half))
            after, _ = chain_from(x8, micro, step8, init, True)
            for g in range(GROUPS):
                edge = edge_bcast(after[g], 0)
                after_r.append(edge[0])
                after_i.append(edge[1])
        ar, ai = jnp.stack(after_r), jnp.stack(after_i)
        gr = x8[0] + (table[0] * ar - table[1] * ai)
        gi = x8[1] + (table[0] * ai + table[1] * ar)
        pr, pi = priors[half]
        d_re = total(gr * pr + gi * pi)
        d_im = total(gi * pr - gr * pi)
        d_scale = total(gr * pairs[half][0] + gi * pairs[half][1])
        for micro in range(MICRO):
            used = tuple(io.carry[4 * comp + 2 * micro + half : 4 * comp + 2 * micro + half + 1, :] for comp in range(2))
            _, v = chain_from((gr, gi), micro, step8, None, True)
            m = cmul(v, from_start)
            tails[(micro, half)] = (column_sum(m[0]), column_sum(m[1]))
            m = cmul(tails[(micro, half)], conj(used))
            d_re, d_im = d_re - m[0], d_im - m[1]
            _, v = chain_from(priors[half], micro, conj(step8), None, False)
            m = cmul(v, conj(table))
            more = cmul(far_step[half], used)
            m = (column_sum(m[0]) - TOK * more[0], column_sum(m[1]) - TOK * more[1])
            far = cmul(m, far_step[half])
            heads[(micro, half)] = tuple(jnp.where(core == 0, f, n) for f, n in zip(far, m))
        rate, turn = chain_rule(rows_of(tables, half), d_re, d_im, d_scale)
        rates.append(rate)
        angles.append(turn)
        projs.append((gr * scale, gi * scale))
    dproj = permute(join_channels(projs).astype(BF16), io.deal_back).astype(BF16)
    dyf, normed = io.dy.astype(F32), io.normed
    dnormed = dot_nt(dproj, io.b) + io.skip * dyf
    io.put(dnormed=dnormed)
    fours = [column_sum(dnormed * io.xhat), column_sum(dnormed), column_sum(dyf * normed.astype(F32))]
    join = lambda two: jnp.concatenate(two, axis=1)
    twos = [join(rates), join(angles)]
    of_tile = lambda tile, at: join([tile[at : at + 1, :], tile[at + 1 : at + 2, :]])
    last = io.last
    for micro in range(MICRO):
        for sums in (tails, heads):
            twos += [join([sums[(micro, half)][comp] for half in range(HALVES)]) for comp in range(2)]
        twos += [of_tile(tile, 4 * comp + 2 * micro) for tile in (last, whole) for comp in range(2)]
    smalls = place_smalls(fours, twos, io.chosen4, io.chosen2)
    b_grad = dot_tn(normed, dproj)
    even, odd = chunk_rows(b_grad[:, :256], b_grad[:, 256:])
    tiles = [jnp.broadcast_to(v[:, None, :], (CHIPS, 8, 128)) for v in (smalls[:CHIPS], smalls[CHIPS:])]
    by_core(io.refs.keep, io.refs.send, core, jnp.concatenate([even, tiles[0]], axis=2), jnp.concatenate([odd, tiles[1]], axis=2))


def kernel_pack_wide(io):
    io.refs.wide[:, :, 0:768] = (io.keep.astype(F32) + io.got.astype(F32)).astype(BF16)


def kernel_pack(io):
    out = io.refs.packed
    keep, got = io.keep_b.astype(F32), io.got_b.astype(F32)
    out[:, :, 768:1024] = (keep[:, :, 0:256] + got[:, :, 0:256]).astype(BF16)
    out[:, :, 1024:1152] = jnp.broadcast_to(io.chip_first[None], (CHIPS, 8, 128))
    low = rows_iota((CHIPS, 8, 128)) < 4
    out[:, :, 1152:1280] = jnp.where(low, keep[:, :, 256:384], got[:, :, 256:384]).astype(BF16)


def segment_joins(lengths_ref):
    second = (rows_iota() & 2) == 2
    bits = []
    for micro in range(MICRO):
        mask, at = jnp.int32(0), jnp.int32(0)
        for slot in range(16):
            unit = lax.shift_left(jnp.int32(1), jnp.minimum(at // (8 * TOK), 15))
            mask = jnp.where(at < N * TOK, mask | unit, mask)
            at = at + lengths_ref[micro, slot]
        bits.append(mask)
    pick = lambda two: jnp.where(second, two[1], two[0]).astype(F32)
    return [pick([1 - (lax.shift_right_logical(b, g + 1) & 1) for b in bits]) for g in range(15)], bits


def kernel_ahead(io):
    me = lax.axis_index("seq")
    tables = io.refs.tables
    near, far = [], []
    for half in range(HALVES):
        step8 = conj(pair_of(tables, STEP, half))
        tiles = [pair_of(tables, BACK, half)]
        for _ in range(2 * GROUPS - 1):
            tiles.append(cmul(tiles[-1], step8))
        tiles = tiles[::-1]
        for comp in range(2):
            far.append(jnp.concatenate([t[comp] for t in tiles[:GROUPS]], axis=0))
            near.append(jnp.concatenate([t[comp] for t in tiles[GROUPS:]], axis=0))
    near, far = jnp.concatenate(near, axis=1), jnp.concatenate(far, axis=1)
    sums = jnp.concatenate([column_sum(near) + column_sum(far), jnp.zeros((7, 512), F32)], axis=0)
    io.put(reach=near, reach_sum=sums, reach_low=jnp.concatenate([far, near], axis=0).astype(BF16))
    ends = io.refs.ends
    own, other = (ends[:, i].reshape(CHIPS * 8, 128) for i in (2, 3))
    first = me % 2 == 0
    io.put(columns=jnp.concatenate([jnp.where(first, own, other), jnp.where(first, other, own)], axis=1))
    lane = lax.broadcasted_iota(jnp.int32, (128, 128), 0)
    col = lax.broadcasted_iota(jnp.int32, (128, 128), 1)
    w = lane % 64
    hot = lambda where: jnp.where(where, 1.0, 0.0).astype(BF16)
    spot = jnp.where((w >= 40) & (w < 56) & (w % 8 < 6), 4 * (w % 8 % 3) + 2 * (lane // 64) + (w - 40) // 8, -1)
    spot = jnp.where(w < 36, jnp.where(w % 18 < 2, 12 + 2 * (w % 18) + lane // 64, -1), spot)
    channel = (lane // 64) == col % 2
    wanted = lambda k: hot(channel & (w < 36) & (w % 18 == 2 + 8 * ((col // 2) % 2) + k))
    io.put(pick=jnp.concatenate([hot(spot == col)] + [wanted(k) for k in range(8)], axis=1))
    half_rows = [jnp.concatenate(rows_of(tables, half) + [jnp.zeros((3, 128), F32)], axis=0) for half in range(HALVES)]
    mine = choose(jnp.where(me // 64 == 0, half_rows[0], half_rows[1]), hot(lane == (2 * me) % 128 + col % 2))
    io.put(channels=mine)
    pows = powers((mine[2:3, :], mine[3:4, :]), 10)
    io.put(channel_pows=jnp.concatenate([v for at in (7, 8, 10) for v in pows[at]] + [jnp.zeros((2, 128), F32)], axis=0))
    feature = lax.broadcasted_iota(jnp.int32, (8, 512), 1)
    here = feature == 4 * me + rows_iota((8, 512)) % 4
    b_rows = io.b_rows.astype(F32)
    b_rows = jnp.where(me % 2 == 0, b_rows, pltpu.roll(b_rows, 4, 0))
    at_row = lambda v: jnp.broadcast_to(jnp.sum(jnp.where(here, v, 0.0), axis=1, keepdims=True), (8, 512))
    io.put(mine=jnp.concatenate([at_row(io.gain), at_row(io.bias), b_rows], axis=1))
    joins, bits = segment_joins(io.ready(lengths=0))
    for group, tile in enumerate(joins):
        io.refs.joined[group] = tile
    group = lax.broadcasted_iota(jnp.int32, (16, 128), 0)
    second = (lax.broadcasted_iota(jnp.int32, (16, 128), 1) // 2) % 2 == 1
    opens = lax.shift_right_logical(jnp.where(second, bits[1], bits[0]), group) & 1
    io.put(opens=opens.astype(F32))


def all_carries(first, tables, joined):
    coef2, coef8 = (coefs_of(tables, at, False) for at in (COEF2, COEF8))
    groups = first.reshape(16, 4, 8, 128)
    step = lambda c, by: c * by[0] + pltpu.roll(c, 4, 1) * by[1]
    inner = [None] * 4
    inner[3] = jnp.zeros((16, 8, 128), F32)
    for p in range(2, -1, -1):
        inner[p] = groups[:, p + 1] + step(inner[p + 1], coef2)
    whole = groups[:, 0] + step(inner[0], coef2)
    entering = [None] * 16
    entering[15] = jnp.zeros((8, 128), F32)
    for g in range(14, -1, -1):
        entering[g] = (whole[g + 1] + tile_mul(entering[g + 1], coef8)) * joined[g]
    factor = jnp.stack(entering)
    out = []
    for p in range(3, -1, -1):
        out.append(inner[p] + factor)
        factor = step(factor, coef2)
    return jnp.stack(out[::-1], axis=1).reshape(CHIPS, 8, 128)


def kernel_last(io, carries, split):
    me = lax.axis_index("seq")
    core = me % 2
    tables = io.refs.tables
    parts = io.refs.parts
    enter = all_carries(parts[:, :, 1024:1152].astype(F32), tables, io.refs.joined)
    carries[...] = enter
    mine = carries[me // 2]
    mine = jnp.where(core == 0, tile_mul(mine, coefs_of(tables, COEF, False)), mine)
    reach_cols = io.reach
    reach = [(reach_cols[:, c : c + 128], reach_cols[:, c + 128 : c + 256]) for c in (0, 256)]
    scale_row = jnp.concatenate([tables[half * PER_HALF + SCALE][0:1, :] for half in (0, 0, 1, 1)], axis=1)
    rows = []
    for micro in range(MICRO):
        cols = []
        for half in range(HALVES):
            nr, ni = tile_row(mine, 0, micro, half)[0:1, :], tile_row(mine, 1, micro, half)[0:1, :]
            lr, li = reach[half]
            cols += [lr * nr - li * ni, lr * ni + li * nr]
        rows.append(jnp.concatenate(cols, axis=1))
    dproj = jnp.concatenate(rows, axis=0) * scale_row
    dproj = permute(dproj.astype(BF16), io.deal_back).astype(BF16)
    dnormed = dot_nt(dproj, io.b) + io.dnormed
    xhat, rstd = io.xhat, io.rstd[:, 0:1]
    dx = dnormed * io.gain
    m1 = jnp.mean(dx, axis=1, keepdims=True)
    m2 = jnp.mean(dx * xhat, axis=1, keepdims=True)
    io.put(in_grad=(io.go.astype(F32) + rstd * (dx - m1 - xhat * m2)).astype(BF16))
    summed = jnp.sum(parts[:, :, 0:1024].astype(F32), axis=0)
    io.put(glu_grad=jnp.concatenate([summed[0:4, 0:768], summed[4:8, 0:256]], axis=1))
    io.put(c_grad=summed[4:8, 256:768])
    moved = dot(io.columns, io.reach_low)
    low = rows_iota((CHIPS, 8, 128)) < 4
    spread = lambda comp, half: jnp.where(low, enter[:, comp * 4 + half : comp * 4 + half + 1, :], enter[:, comp * 4 + 2 + half : comp * 4 + 3 + half, :])
    cols = []
    for half in range(HALVES):
        c = 256 * half
        mr = moved[:, c : c + 128].reshape(CHIPS, 8, 128)
        mi = moved[:, c + 128 : c + 256].reshape(CHIPS, 8, 128)
        nr, ni = spread(0, half), spread(1, half)
        cols += [jnp.sum(mr * nr - mi * ni, axis=0), jnp.sum(mr * ni + mi * nr, axis=0)]
    rows8 = jnp.concatenate(cols, axis=1)
    rows8 = rows8 + pltpu.roll(rows8, 4, 0)
    enter_sum = jnp.sum(enter, axis=0)
    reach_sum = io.reach_sum[0:1, :]
    cols = []
    for half in range(HALVES):
        c = 256 * half
        fold2 = lambda comp: enter_sum[comp * 4 + half : comp * 4 + half + 1, :] + enter_sum[comp * 4 + 2 + half : comp * 4 + 3 + half, :]
        nr, ni = fold2(0), fold2(1)
        lr, li = reach_sum[:, c : c + 128], reach_sum[:, c + 128 : c + 256]
        cols += [lr * nr - li * ni, lr * ni + li * nr]
    sums_row = jnp.concatenate(cols, axis=1)
    both = jnp.where(rows_iota((8, 512)) < 4, rows8, sums_row) * scale_row
    moved_x = jnp.concatenate([choose(both[:, :256], io.deal_back), choose(both[:, 256:], io.deal_back)], axis=1)
    moved_one = jnp.broadcast_to(moved_x[4:5, :], (8, 512))
    own = io.mine
    gain_f, bias_f, b_rows = own[:, 0:512], own[:, 512:1024], own[:, 1024:1536]
    b_sum = jnp.concatenate([summed[0:4, 768:1024], summed[4:8, 768:1024]], axis=1)
    io.put(b_grad=b_sum + (gain_f * moved_x + bias_f * moved_one)[0:4, :])
    gain_carry = jnp.sum(b_rows * moved_x, axis=1, keepdims=True)
    bias_carry = jnp.sum(b_rows * moved_one, axis=1, keepdims=True)
    small = parts[:, :, 1152:1280]
    own, other = small[:, 0, :].astype(F32), small[:, 4, :].astype(F32)
    sums = column_sum(own + other)
    gathered = choose(jnp.concatenate([sums, jnp.zeros((7, 128), F32)], axis=0), io.pick[:, 0:128])
    d_re, d_im, d_scale = owned_channels(own, other, core, io, split)
    rate, turn = chain_rule([io.channels[i : i + 1, :] for i in range(5)], d_re, d_im, d_scale)
    shift = lambda v, by: pltpu.roll(v, 128 - by, 1)
    diagonal = lax.broadcasted_iota(jnp.int32, (8, 128), 1) == rows_iota()
    to_lanes = lambda v: column_sum(jnp.where(diagonal, v, 0.0))
    sums = gathered[0:1, :]
    io.put(gain_grad=(sums + to_lanes(gain_carry))[:, 0:4])
    io.put(bias_grad=(shift(sums, 4) + to_lanes(bias_carry))[:, 0:4])
    io.put(skip_grad=shift(sums, 8)[:, 0:4])
    io.put(rate_grad=(shift(sums, 12) + rate)[:, 0:2])
    io.put(angle_grad=(shift(sums, 14) + turn)[:, 0:2])


def group_chain(coef, value, opens, reverse):
    row = lax.broadcasted_iota(jnp.int32, (16, 128), 0)
    pos = 15 - row if reverse else row
    moved = lambda v, by: pltpu.roll(v, 16 - by if reverse else by, 0)
    opens = jnp.where(row == 0, 1.0, opens)
    keep = jnp.where(pos == 0, 0.0, 1.0 - (moved(opens, 1) if reverse else opens))
    a = (keep * coef[0], keep * coef[1])
    b = tuple(keep * moved(v, 1) for v in value)
    for by in (1, 2, 4, 8):
        inside = pos >= by
        before = lambda v: jnp.where(inside, moved(v, by), 0.0)
        pb, pa = tuple(before(v) for v in b), tuple(before(v) for v in a)
        m = cmul(a, pb)
        b = (b[0] + m[0], b[1] + m[1])
        a = cmul(a, pa)
    return b


def owned_channels(own, other, core, io, split):
    first, second = jnp.where(core == 0, own, other), jnp.where(core == 0, other, own)
    values = []
    for rows in (first, second):
        values.append(dot(rows.astype(BF16), io.pick[:, 128:1152]))
    pows = [tuple(io.channel_pows[2 * i + comp : 2 * i + comp + 1, :] for comp in range(2)) for i in range(3)]
    step, step2, step8 = pows
    of = lambda q, k: (values[q][:, 128 * k : 128 * k + 128], values[q][:, 128 * k + 128 : 128 * k + 256])
    plus = lambda x, y: (x[0] + y[0], x[1] + y[1])
    last0, last1 = of(0, 4), of(1, 4)
    kept = [*plus(last1, cmul(last0, step)), *of(0, 6), *of(0, 0), *of(1, 0), *plus(of(0, 2), of(1, 2)), *last0]
    for i, v in enumerate(kept):
        split[i] = v
    at = lambda i, p: (split[i, pl.ds(p, 16, stride=4), :], split[i + 1, pl.ds(p, 16, stride=4), :])
    ends, firsts = [at(0, p) for p in range(4)], [at(2, p) for p in range(4)]
    zero = (jnp.zeros((16, 128), F32), jnp.zeros((16, 128), F32))
    states, grads = [zero], [zero]
    for p in range(1, 4):
        states.append(plus(cmul(states[-1], step2), ends[p - 1]))
        grads.append(plus(cmul(grads[-1], conj(step2)), firsts[4 - p]))
    grads = grads[::-1]
    into = group_chain(step8, plus(cmul(states[3], step2), ends[3]), io.opens, False)
    back = group_chain(conj(step8), plus(cmul(grads[0], conj(step2)), firsts[0]), io.opens, True)
    d_lam, d_scale = zero, zero
    for p in range(4):
        states[p] = plus(states[p], into)
        into = cmul(into, step2)
        grads[3 - p] = plus(grads[3 - p], back)
        back = cmul(back, conj(step2))
    for p in range(4):
        h0, n = states[p], grads[p]
        far = cmul(h0, step)
        h1 = plus(far, at(10, p))
        seen = plus(cmul(far, step), cmul(h1, step))
        seen = plus(at(8, p), (TOK * seen[0], TOK * seen[1]))
        for x, y in ((at(4, p), h0), (at(6, p), h1), (n, seen)):
            d_lam = plus(d_lam, cmul(x, conj(y)))
        d_scale = plus(d_scale, cmul(n, conj(ends[p])))
    both = lambda v: (lambda t: t + pltpu.roll(t, 126, 1))(column_sum(v))
    d_re, d_im, s_re, s_im = (both(v) for v in d_lam + d_scale)
    lr, li, scale = (io.channels[i : i + 1, :] for i in (2, 3, 4))
    return d_re, d_im, (lr * s_re + li * s_im) / scale


def body(block_in, out_grad, lengths, ln_gain, ln_bias, b_proj, c_proj, glu_weight, skip_gain, log_rate, angle):
    rows = MICRO * TOK
    x = block_in.reshape(rows, 512)
    go = out_grad.reshape(rows, 512)
    gain, bias, skip = (v.reshape(1, 512) for v in (ln_gain, ln_bias, skip_gain))
    rate2, angle2 = log_rate.reshape(2, 128), angle.reshape(2, 128)
    spread = deal()
    deal_m = jnp.asarray(spread, BF16)
    back_m = jnp.asarray(spread.T.copy(), BF16)
    chosen4, chosen2 = jnp.asarray(one_hots(4, 512), BF16), jnp.asarray(one_hots(2, 256), BF16)
    full = (rows, 512)
    k1 = call(
        kernel_first,
        [
            (LOAD, dict(x=x, b=b_proj, deal=deal_m, gain=gain, bias=bias)),
            (COPY, dict(log_rate=rate2, angle=angle2)),
            (SCALARS, dict(lengths=lengths)),
            (LOAD, dict(deal_back=back_m, c=c_proj, skip=skip, glu=glu_weight, go=go, chosen4=chosen4, chosen2=chosen2)),
            (PLAIN, dict(b_tiles=b_proj.reshape(CHIPS, 8, 512))),
        ],
        [
            (
                HELD,
                dict(
                    normed=(full, BF16), xhat=(full, F32), rstd=((rows, 128), F32), pairs=(full, BF16), local=(full, F32),
                    send=((CHIPS + 2, 8, 128), BF16), columns=((CHIPS, 8, 128), BF16), tables=((TABLES, 8, 128), F32), b_rows=((8, 512), BF16),
                    last=((8, 128), F32),
                ),
            )
        ],
        flops=300_000_000, nbytes=3_000_000,
    )
    swap = functools.partial(lax.ppermute, axis_name="seq", perm=[(i, i ^ 1) for i in range(N)])
    same_core = [[2 * t + core for t in range(CHIPS)] for core in range(2)]
    exchange = functools.partial(lax.all_to_all, axis_name="seq", split_axis=0, concat_axis=0, tiled=True, axis_index_groups=same_core)
    kj = call(
        kernel_join, [(HELD, dict(last=k1.last, got=swap(k1.send), columns=k1.columns, tables=k1.tables))],
        [(HELD, dict(inside=((8, 128), F32), ends=((CHIPS, 4, 8, 128), BF16)))], flops=1_000_000, nbytes=1_000_000,
    )
    ends = exchange(kj.ends)
    k2 = call(
        kernel_middle,
        [
            (HELD, dict(deal_back=k1.deal_back, c=k1.c, skip=k1.skip, glu=k1.glu, go=k1.go)),
            (HELD, dict(ends=ends, inside=kj.inside, tables=k1.tables, local=k1.local, normed=k1.normed, deal=k1.deal, x=k1.x)),
        ],
        [
            (COPY, dict(out=(full, BF16))),
            (
                HELD,
                dict(
                    first=((8, 128), F32), carry=((8, 128), F32), act=(full, BF16), dgated=((rows, 1024), BF16), hidden=(full, BF16), dy=(full, BF16),
                    back=(full, F32), prior=(full, F32),
                ),
            ),
        ],
        flops=1_000_000_000, nbytes=6_000_000,
    )
    other = swap(k2.first)
    wide, narrow = ((CHIPS, 8, 768), BF16), ((CHIPS, 8, 384), BF16)
    kp = call(
        kernel_products, [(HELD, dict(act=k2.act, dgated=k2.dgated, hidden=k2.hidden, dy=k2.dy))], [(HELD, dict(keep=wide, send=wide))],
        flops=2_000_000_000, nbytes=3_000_000,
    )
    got = swap(kp.send)
    kc = call(
        kernel_carried,
        [
            (HELD, dict(carry=k2.carry, last=k1.last)),
            (HELD, dict(first=k2.first, other=other, back=k2.back, prior=k2.prior, dy=k2.dy, tables=k1.tables, pairs=k1.pairs, b=k1.b)),
            (HELD, dict(deal_back=k1.deal_back, normed=k1.normed, xhat=k1.xhat, skip=k1.skip, chosen4=k1.chosen4, chosen2=k1.chosen2)),
        ],
        [(HELD, dict(chip_first=((8, 128), BF16), dnormed=(full, F32), keep=narrow, send=narrow))],
        flops=6_000_000_000, nbytes=3_000_000,
    )
    got_b = swap(kc.send)
    ka = call(
        kernel_ahead,
        [
            (SCALARS, dict(lengths=lengths)),
            (HELD, dict(tables=k1.tables, ends=ends, gain=k1.gain, bias=k1.bias, b_rows=k1.b_rows, dnormed=kc.dnormed)),
        ],
        [
            (
                HELD,
                dict(
                    reach=((TOK, 512), F32), reach_sum=((8, 512), F32), reach_low=((2 * TOK, 512), BF16), columns=((CHIPS * 8, 256), BF16),
                    channels=((8, 128), F32), channel_pows=((8, 128), F32), opens=((16, 128), F32), pick=((128, 1152), BF16), mine=((8, 1536), F32), joined=((15, 8, 128), F32),
                ),
            )
        ],
        flops=200_000_000, nbytes=3_000_000,
    )
    chunks = ((CHIPS, 8, 1280), BF16)
    wide_part = call(
        kernel_pack_wide, [(HELD, dict(keep=kp.keep, got=got, reach=ka.reach))], [(HELD, dict(wide=chunks))], flops=1_000_000, nbytes=2_400_000
    ).wide
    packed = call(
        kernel_pack, [(HELD, dict(wide=wide_part, keep_b=kc.keep, got_b=got_b, chip_first=kc.chip_first))],
        [(HELD, dict(packed=chunks))], alias={0: 0}, flops=1_000_000, nbytes=1_200_000,
    ).packed
    parts = exchange(packed)
    four, two = ((1, 4), F32), ((1, 2), F32)
    k3 = call(
        kernel_last,
        [
            (HELD, dict(parts=parts, dnormed=kc.dnormed, go=k1.go, deal_back=k1.deal_back, tables=k1.tables, b=k1.b, xhat=k1.xhat, rstd=k1.rstd)),
            (HELD, dict(gain=k1.gain, reach=ka.reach, reach_sum=ka.reach_sum, reach_low=ka.reach_low, columns=ka.columns)),
            (HELD, dict(channels=ka.channels, channel_pows=ka.channel_pows, opens=ka.opens, pick=ka.pick, mine=ka.mine, joined=ka.joined)),
        ],
        [
            (COPY, dict(in_grad=(full, BF16), b_grad=((4, 512), F32), c_grad=((4, 512), F32), glu_grad=((4, 1024), F32))),
            (COPY, dict(gain_grad=four, bias_grad=four, skip_grad=four, rate_grad=two, angle_grad=two)),
        ],
        extra=[pltpu.VMEM((CHIPS, 8, 128), F32), pltpu.VMEM((12, CHIPS, 128), F32)], flops=600_000_000, nbytes=5_000_000,
    )
    return (
        k2.out.reshape(block_in.shape),
        k3.in_grad.reshape(block_in.shape),
        k3.gain_grad.reshape(4),
        k3.bias_grad.reshape(4),
        k3.b_grad,
        k3.c_grad,
        k3.glu_grad,
        k3.skip_grad.reshape(4),
        k3.rate_grad.reshape(2),
        k3.angle_grad.reshape(2),
    )


def solution(mesh):
    tokens = P(None, "seq", None)
    in_specs = (tokens, tokens) + (P(),) * 9
    out_specs = (tokens, tokens, P("seq"), P("seq"), P("seq", None), P("seq", None), P("seq", None), P("seq"), P("seq"), P("seq"))
    return jax.shard_map(body, mesh=mesh, in_specs=in_specs, out_specs=out_specs, check_vma=False)
```
